256 devices in a mesh: section: 16 (over y, z_hi), dp: 16 (over z_lo, x, core).
Axes of the slice: x: 4, y: 4, z: 8 (z_hi: 4, z_lo: 2; z = z_hi * 2 + z_lo), core: 2. Of those that a mesh axis runs over, the one named last changes fastest.
Arguments:
- inputs_down: bfloat16 [48, 24, 5120], P('dp'), may hold values from -6 to 6
- inputs_up: bfloat16 [48, 24, 5120], P('dp'), may hold values from -6 to 6
- w_in: bfloat16 [16, 2, 5120, 256], P('section'), as said below
- w_out: bfloat16 [16, 2, 5120, 256], P('section'), as said below
Outputs:
- grad_w_out: float32 [16, 5120, 256], P('section', 'dp')
The draws below stay inside these ranges and needn't reach their ends.
Inputs may be any that keep to these rules, and one draw needn't show every extreme that they name: w_in[s, 1] equals w_in[15 - s, 0] for every s: both directions use the same layers. w_out[s, 1] equals w_out[15 - s, 0] for every s: both directions use the same layers.
All inputs are finite; a program needn't handle non-finite values.
Results may differ from the reference program's by a relative error of at most 0.015.
Values may be sent and summed in bfloat16 or wider, within the bound.
No kernel may reach another device: no remote copies, remote signals or barrier semaphores. Data moves between devices by JAX's collectives and lax.ppermute only.
A program may use at most 128 MiB of HBM per device.

```python
import jax
import jax.numpy as jnp
from jax import lax

D = 5120
R = 256
TOK_MB = 24
LAYERS = 16
BATCH = 48
N_DP = 16


def mirrored(key, factor):
    base = jax.random.normal(key, (LAYERS, D, R), jnp.float32) * factor
    return jnp.stack([base, base[::-1]], axis=1)


def draw_w_in(key, part):
    key = jax.random.fold_in(key, 11)
    return mirrored(key, D ** (-0.5)).astype(jnp.bfloat16)


def draw_w_out(key, part):
    key = jax.random.fold_in(key, 23)
    return mirrored(key, 0.5 * R ** (-0.5)).astype(jnp.bfloat16)


def shard_levels(own_key, shape, cuts, low, top_value):
    def one(position, blocks):
        heights = jax.random.uniform(jax.random.fold_in(jax.random.fold_in(own_key, 6), position), (blocks,), jnp.float32, low / len(cuts), top_value / len(cuts))
        return jnp.repeat(jnp.exp(heights), shape[position] // blocks).reshape((-1,) + (1,) * (len(shape) - position - 1))

    gain = one(*cuts[0])
    for cut in cuts[1:]:
        gain = gain * one(*cut)
    return gain


def gaussian(stream_key, dims, width, most, cuts=(), held_as=jnp.bfloat16):
    array = jax.random.normal(stream_key, dims, jnp.float32) * width
    if len(cuts) > 0:
        array = shard_levels(stream_key, dims, cuts, -0.22, 0.18) * array
    return jnp.clip(array, min=-most, max=most).astype(held_as)


def setup_inputs(seed: int = 0) -> dict:
    key_list = jax.random.split(jax.random.key(seed), 5)
    return {
        "inputs_down": gaussian(key_list[0], (BATCH, TOK_MB, D), 1.0, 6.0, ((0, 16),)),
        "inputs_up": gaussian(key_list[1], (BATCH, TOK_MB, D), 1.0, 6.0, ((0, 16),)),
        "w_in": draw_w_in(jax.random.fold_in(key_list[4], 71), 0),
        "w_out": draw_w_out(jax.random.fold_in(key_list[4], 71), 0),
    }


epsilon = 1e-06
cot_weight = 0.0625

def forward_layer(hidden, w_one, w_two):
    widened = hidden.astype(jnp.float32)
    inv_rms = lax.rsqrt(lax.optimization_barrier(jnp.mean(widened * widened, axis=-1, keepdims=True)) + epsilon)
    normed = (widened * inv_rms).astype(jnp.bfloat16)
    pre_act = jnp.dot(normed, w_one, preferred_element_type=jnp.float32)
    active = jax.nn.silu(pre_act).astype(jnp.bfloat16)
    branch = lax.dot_general(active, w_two, (((1,), (1,)), ((), ())), preferred_element_type=jnp.float32)
    return (widened + branch).astype(jnp.bfloat16)

def backward_rows(hidden, upstream, w_one, w_two):
    widened = hidden.astype(jnp.float32)
    inv_rms = lax.rsqrt(lax.optimization_barrier(jnp.mean(widened * widened, axis=-1, keepdims=True)) + epsilon)
    unit_rows = widened * inv_rms
    normed = unit_rows.astype(jnp.bfloat16)
    pre_act = jnp.dot(normed, w_one, preferred_element_type=jnp.float32)
    active = jax.nn.silu(pre_act).astype(jnp.bfloat16)
    d_active = jnp.dot(upstream, w_two, preferred_element_type=jnp.float32)
    sigma = jax.nn.sigmoid(pre_act)
    d_pre = (d_active * sigma * (1.0 + pre_act * (1.0 - sigma))).astype(jnp.bfloat16)
    d_normed = lax.dot_general(d_pre, w_one, (((1,), (1,)), ((), ())), preferred_element_type=jnp.float32)
    d_hidden = inv_rms * (d_normed - unit_rows * lax.optimization_barrier(jnp.mean(d_normed * unit_rows, axis=-1, keepdims=True)))
    return ((upstream.astype(jnp.float32) + d_hidden).astype(jnp.bfloat16), active)

def reference(inputs_down, inputs_up, w_in, w_out):
    all_rows = jnp.concatenate([inputs_down.reshape(-1, D), inputs_up.reshape(-1, D)], axis=0)
    w_in_layers = w_in[:, 0]
    w_out_layers = w_out[:, 0]

    def forward_step(hidden, weights):
        return (forward_layer(hidden, weights[0], weights[1]), hidden)
    final_rows, stashed = lax.scan(forward_step, all_rows, (w_in_layers, w_out_layers))
    upstream = (final_rows.astype(jnp.float32) * cot_weight).astype(jnp.bfloat16)
    groups = 2 * N_DP

    def backward_step(upstream_now, packed):
        hidden, w_one, w_two = packed
        new_up, active = backward_rows(hidden, upstream_now, w_one, w_two)
        per_group = jnp.einsum('gnd,gnr->gdr', upstream_now.reshape(groups, -1, D).astype(jnp.float32), active.reshape(groups, -1, R).astype(jnp.float32))
        part_sums = lax.optimization_barrier(per_group.astype(jnp.bfloat16)).astype(jnp.float32)
        part_sums = part_sums.reshape(2, N_DP, D, R)
        replica = lax.optimization_barrier(lax.optimization_barrier(jnp.sum(part_sums, axis=1)).astype(jnp.bfloat16)).astype(jnp.float32)
        return (new_up, replica[0] + replica[1])
    unused_up, grads = lax.scan(backward_step, upstream, (stashed, w_in_layers, w_out_layers), reverse=True)
    return grads
```

```python
import jax
import jax.numpy as jnp
from jax import lax
from jax.experimental import pallas as pl
from jax.experimental.pallas import tpu as pltpu
from jax.sharding import Mesh, PartitionSpec as P

EPS = 1e-06
COT = 0.0625
D, R = 5120, 256
REAL, ROWS = 18, 24
SET = 4
CH = 4
CW = D // CH
DP = ("zl", "x", "core")
GRID_AXES = ("y", "zh", "zl", "x", "core")
ANY = pl.BlockSpec(memory_space=pl.ANY)
VM = pl.BlockSpec(memory_space=pltpu.VMEM)
SM = pl.BlockSpec(memory_space=pltpu.SMEM)


def weight_copy(w_ref, wbuf, sem, flags, layer, which):
    held = jnp.where(flags[1] == 1, SET - 1 - layer, layer)
    slot = lax.rem(layer, 2)
    return pltpu.make_async_copy(
        w_ref.at[held, :, which], wbuf.at[slot, which], sem.at[slot, which]
    )


def chunk(wbuf, slot, which, c):
    per = 16 // CH
    return wbuf[slot, which, c * per : (c + 1) * per].reshape(CW, R)


def columns(c):
    return slice(c * CW, (c + 1) * CW)


def inverse_rms(hbuf, layer):
    total = jnp.zeros((ROWS, 1), jnp.float32)
    for c in range(CH):
        v = hbuf[layer, :, columns(c)].astype(jnp.float32)
        total = total + jnp.sum(v * v, axis=-1, keepdims=True)
    return lax.rsqrt(total * (1.0 / D) + EPS)


def forward_kernel(*refs, aliased):
    flags, x_ref, w_ref = refs[:3]
    refs = refs[3 + (3 if aliased else 0) :]
    y_ref, h_out, pre_out, act_out = refs[:4]
    wbuf, hbuf, prebuf, actbuf, sem_w, sem_h, sem_p, sem_a = refs[4:]

    @pl.when(flags[0] == 1)
    def _():
        for which in range(2):
            weight_copy(w_ref, wbuf, sem_w, flags, 0, which).start()
        hbuf[0] = x_ref[...]

        def step(layer, carry):
            slot = lax.rem(layer, 2)

            @pl.when(layer + 1 < SET)
            def _():
                for which in range(2):
                    weight_copy(w_ref, wbuf, sem_w, flags, layer + 1, which).start()

            pltpu.make_async_copy(hbuf.at[layer], h_out.at[layer], sem_h.at[layer]).start()
            inv = inverse_rms(hbuf, layer)
            weight_copy(w_ref, wbuf, sem_w, flags, layer, 0).wait()
            pre = jnp.zeros((ROWS, R), jnp.float32)
            for c in range(CH):
                normed = (hbuf[layer, :, columns(c)].astype(jnp.float32) * inv).astype(jnp.bfloat16)
                pre = pre + jnp.dot(
                    normed, chunk(wbuf, slot, 0, c), preferred_element_type=jnp.float32
                )
            active = (pre / (1.0 + jnp.exp(-pre))).astype(jnp.bfloat16)
            prebuf[layer] = pre
            actbuf[layer] = active
            weight_copy(w_ref, wbuf, sem_w, flags, layer, 1).wait()
            for c in range(CH):
                branch = lax.dot_general(
                    active,
                    chunk(wbuf, slot, 1, c),
                    (((1,), (1,)), ((), ())),
                    preferred_element_type=jnp.float32,
                )
                before = hbuf[layer, :, columns(c)].astype(jnp.float32)
                hbuf[layer + 1, :, columns(c)] = (before + branch).astype(jnp.bfloat16)
            return carry

        lax.fori_loop(0, SET, step, 0)
        y_ref[...] = hbuf[SET]
        copies = [
            pltpu.make_async_copy(prebuf, pre_out, sem_p.at[0]),
            pltpu.make_async_copy(actbuf, act_out, sem_a.at[0]),
        ]
        for one in copies:
            one.start()
        for layer in range(SET):
            copies.append(
                pltpu.make_async_copy(hbuf.at[layer], h_out.at[layer], sem_h.at[layer])
            )
        for one in copies:
            one.wait()


def run_forward(flags, rows, weights, held=None):
    outs = (
        jax.ShapeDtypeStruct((ROWS, D), jnp.bfloat16),
        jax.ShapeDtypeStruct((SET, ROWS, D), jnp.bfloat16),
        jax.ShapeDtypeStruct((SET, ROWS, R), jnp.float32),
        jax.ShapeDtypeStruct((SET, ROWS, R), jnp.bfloat16),
    )
    aliased = held is not None
    return pl.pallas_call(
        lambda *refs: forward_kernel(*refs, aliased=aliased),
        out_shape=outs,
        in_specs=[SM, VM, ANY] + ([ANY] * 3 if aliased else []),
        out_specs=(VM, ANY, ANY, ANY),
        scratch_shapes=[
            pltpu.VMEM((2, 2, 16, D // 16, R), jnp.bfloat16),
            pltpu.VMEM((SET + 1, ROWS, D), jnp.bfloat16),
            pltpu.VMEM((SET, ROWS, R), jnp.float32),
            pltpu.VMEM((SET, ROWS, R), jnp.bfloat16),
            pltpu.SemaphoreType.DMA((2, 2)),
            pltpu.SemaphoreType.DMA((SET,)),
            pltpu.SemaphoreType.DMA((1,)),
            pltpu.SemaphoreType.DMA((1,)),
        ],
        input_output_aliases={3: 1, 4: 2, 5: 3} if aliased else {},
        compiler_params=pltpu.CompilerParams(vmem_limit_bytes=40 * 2**20),
        cost_estimate=pl.CostEstimate(
            flops=4 * SET * ROWS * D * R, bytes_accessed=SET * 4 * D * R, transcendentals=0
        ),
        name="forward_set",
    )(flags, rows, weights, *(held or ()))


def backward_kernel(*refs, aliased, from_final, last):
    flags, g_ref, w_ref, h_in, pre_in = refs[:5]
    refs = refs[5 + (1 if aliased else 0) :]
    y_ref, g_out = refs[:2]
    wbuf, hbuf, prebuf, gbuf, dnbuf, sem_w, sem_h, sem_p, sem_g = refs[2:]

    @pl.when(flags[0] == 1)
    def _():
        def wanted(step, which):
            held = jnp.where(flags[1] == 1, step, SET - 1 - step)
            slot = lax.rem(step, 2)
            return pltpu.make_async_copy(
                w_ref.at[held, :, which], wbuf.at[slot, which], sem_w.at[slot, which]
            )

        wanted(0, 1).start()
        wanted(0, 0).start()
        pre_copy = pltpu.make_async_copy(pre_in, prebuf, sem_p.at[0])
        pre_copy.start()
        for layer in range(SET - 1, -1, -1):
            pltpu.make_async_copy(h_in.at[layer], hbuf.at[layer], sem_h.at[layer]).start()
        if from_final:
            gbuf[0] = (g_ref[...].astype(jnp.float32) * COT).astype(jnp.bfloat16)
        else:
            gbuf[0] = g_ref[...]
        pre_copy.wait()
        steps = SET - 1 if last else SET

        def one_layer(step, carry):
            layer = SET - 1 - step
            slot = lax.rem(step, 2)

            @pl.when(step + 1 < steps)
            def _():
                wanted(step + 1, 1).start()
                wanted(step + 1, 0).start()

            pltpu.make_async_copy(gbuf.at[step], g_out.at[layer], sem_g.at[step]).start()
            pltpu.make_async_copy(h_in.at[layer], hbuf.at[layer], sem_h.at[layer]).wait()
            inv = inverse_rms(hbuf, layer)
            pre = prebuf[layer]
            sigma = 1.0 / (1.0 + jnp.exp(-pre))
            slope = sigma * (1.0 + pre * (1.0 - sigma))
            wanted(step, 1).wait()
            d_active = jnp.zeros((ROWS, R), jnp.float32)
            for c in range(CH):
                d_active = d_active + jnp.dot(
                    gbuf[step, :, columns(c)],
                    chunk(wbuf, slot, 1, c),
                    preferred_element_type=jnp.float32,
                )
            d_pre = (d_active * slope).astype(jnp.bfloat16)
            wanted(step, 0).wait()
            total = jnp.zeros((ROWS, 1), jnp.float32)
            for c in range(CH):
                d_normed = lax.dot_general(
                    d_pre,
                    chunk(wbuf, slot, 0, c),
                    (((1,), (1,)), ((), ())),
                    preferred_element_type=jnp.float32,
                )
                unit = hbuf[layer, :, columns(c)].astype(jnp.float32) * inv
                total = total + jnp.sum(d_normed * unit, axis=-1, keepdims=True)
                dnbuf[:, columns(c)] = d_normed
            mean = total * (1.0 / D)
            for c in range(CH):
                unit = hbuf[layer, :, columns(c)].astype(jnp.float32) * inv
                moved = inv * (dnbuf[:, columns(c)] - unit * mean)
                before = gbuf[step, :, columns(c)].astype(jnp.float32)
                gbuf[step + 1, :, columns(c)] = (before + moved).astype(jnp.bfloat16)
            return carry

        lax.fori_loop(0, steps, one_layer, 0)
        if last:
            pltpu.make_async_copy(gbuf.at[SET - 1], g_out.at[0], sem_g.at[SET - 1]).start()
            pltpu.make_async_copy(h_in.at[0], hbuf.at[0], sem_h.at[0]).wait()
        y_ref[...] = gbuf[steps]
        for step in range(SET):
            pltpu.make_async_copy(
                gbuf.at[step], g_out.at[SET - 1 - step], sem_g.at[step]
            ).wait()


def run_backward(flags, g_rows, weights, h_held, pre_held, held=None, from_final=False, last=False):
    outs = (
        jax.ShapeDtypeStruct((ROWS, D), jnp.bfloat16),
        jax.ShapeDtypeStruct((SET, ROWS, D), jnp.bfloat16),
    )
    aliased = held is not None
    return pl.pallas_call(
        lambda *refs: backward_kernel(*refs, aliased=aliased, from_final=from_final, last=last),
        out_shape=outs,
        in_specs=[SM, VM, ANY, ANY, ANY] + ([ANY] if aliased else []),
        out_specs=(VM, ANY),
        scratch_shapes=[
            pltpu.VMEM((2, 2, 16, D // 16, R), jnp.bfloat16),
            pltpu.VMEM((SET, ROWS, D), jnp.bfloat16),
            pltpu.VMEM((SET, ROWS, R), jnp.float32),
            pltpu.VMEM((SET + 1, ROWS, D), jnp.bfloat16),
            pltpu.VMEM((ROWS, D), jnp.float32),
            pltpu.SemaphoreType.DMA((2, 2)),
            pltpu.SemaphoreType.DMA((SET,)),
            pltpu.SemaphoreType.DMA((1,)),
            pltpu.SemaphoreType.DMA((SET,)),
        ],
        input_output_aliases={5: 1} if aliased else {},
        compiler_params=pltpu.CompilerParams(vmem_limit_bytes=40 * 2**20),
        cost_estimate=pl.CostEstimate(
            flops=4 * SET * ROWS * D * R, bytes_accessed=SET * 4 * D * R, transcendentals=0
        ),
        name="backward_set",
    )(flags, g_rows, weights, h_held, pre_held, *((held,) if aliased else ()))


def grad_kernel(g_ref, act_ref, out_ref, *, first):
    for layer in range(SET):
        g = g_ref[:, layer].reshape(16 * ROWS, D // 16)
        act = act_ref[:, first + layer].reshape(16 * ROWS, R)
        out_ref[layer] = lax.dot_general(
            g, act, (((0,), (0,)), ((), ())), preferred_element_type=jnp.float32
        ).astype(jnp.bfloat16)


def run_grad(g_all, act_all, first):
    return pl.pallas_call(
        lambda *refs: grad_kernel(*refs, first=first),
        out_shape=jax.ShapeDtypeStruct((SET, D // 16, R), jnp.bfloat16),
        in_specs=[VM, VM],
        out_specs=VM,
        compiler_params=pltpu.CompilerParams(vmem_limit_bytes=40 * 2**20),
        name="grad_set",
    )(g_all, act_all)


def hop(rows):
    return lax.ppermute(rows, "y", [(0, 1), (1, 0), (2, 3), (3, 2)])


def spread(g_set):
    cut = g_set.reshape(SET, ROWS, 16, D // 16).transpose(2, 0, 1, 3)
    return lax.all_to_all(cut, DP, 0, 0)


def shards(inputs_down, inputs_up, w_in, w_out):
    y, zh, dp = lax.axis_index("y"), lax.axis_index("zh"), lax.axis_index(DP)
    low_half = y < 2
    stage_p = (y == 0) | (y == 3)

    def own(layer_slot):
        parts = [
            lax.dynamic_slice(w, (0, layer_slot, dp * (D // 16), 0), (1, 1, D // 16, R))[0, 0]
            for w in (w_in, w_out)
        ]
        return jnp.stack(parts)

    def gathered(own_part):
        return lax.all_gather(own_part, ("zh",) + DP).reshape(SET, 16, 2, D // 16, R)

    first_slot = jnp.where(low_half, 0, 1)
    own_a, own_b = own(first_slot), own(1 - first_slot)
    w_a = gathered(own_a)
    own_b, w_a = lax.optimization_barrier((own_b, w_a))
    w_b = gathered(own_b)

    def flag(active, reverse):
        return jnp.stack([active.astype(jnp.int32), reverse.astype(jnp.int32)])

    p_a, p_b = flag(stage_p, ~low_half), flag(stage_p, low_half)
    q_a, q_b = flag(~stage_p, ~low_half), flag(~stage_p, low_half)

    mine = jnp.where(low_half, inputs_down, inputs_up).reshape(-1, D)
    mine = lax.dynamic_slice(mine, (zh * REAL, 0), (REAL, D))
    rows = jnp.pad(mine, ((0, ROWS - REAL), (0, 0)))

    rows, h_a, pre_a, act_a = run_forward(p_a, rows, w_a)
    rows = hop(rows)
    rows, h_a, pre_a, act_a = run_forward(q_a, rows, w_a, (h_a, pre_a, act_a))
    rows, h_b, pre_b, act_b = run_forward(q_b, rows, w_b)
    rows = hop(rows)
    rows, h_b, pre_b, act_b = run_forward(p_b, rows, w_b, (h_b, pre_b, act_b))
    act_all = lax.all_gather(jnp.concatenate([act_a, act_b], axis=0), DP)
    rows, g_b = run_backward(p_b, rows, w_b, h_b, pre_b, from_final=True)
    rows = hop(rows)
    rows, g_b = run_backward(q_b, rows, w_b, h_b, pre_b, held=g_b)
    rows, g_a = run_backward(q_a, rows, w_a, h_a, pre_a)
    rows = hop(rows)
    rows, g_a = run_backward(p_a, rows, w_a, h_a, pre_a, held=g_a, last=True)
    part_b = run_grad(spread(g_b), act_all, SET)
    sum_b = lax.psum_scatter(part_b, "zh", scatter_dimension=0, tiled=True)[0]
    part_a = run_grad(spread(g_a), act_all, 0)
    sum_a = lax.psum_scatter(part_a, "zh", scatter_dimension=0, tiled=True)[0]
    kept = jnp.where(low_half, sum_a, sum_b)
    other = jnp.where(low_half, sum_b, sum_a)
    received = lax.ppermute(other, "y", [(0, 3), (3, 0), (1, 2), (2, 1)])
    return (kept.astype(jnp.float32) + received.astype(jnp.float32))[None]


def solution(mesh):
    fine = Mesh(mesh.devices.reshape(4, 4, 2, 4, 2), GRID_AXES)
    section = ("y", "zh")
    placed = (
        P(DP, None, None),
        P(DP, None, None),
        P(section, None, None, None),
        P(section, None, None, None),
    )
    return jax.shard_map(
        shards, mesh=fine, in_specs=placed, out_specs=P(section, DP, None), check_vma=False
    )
```

```python
import jax
import jax.numpy as jnp
from jax import lax
from jax.experimental import pallas as pl
from jax.experimental.pallas import tpu as pltpu
from jax.sharding import Mesh, PartitionSpec as P

EPS = 1e-06
COT = 0.0625
D, R = 5120, 256
REAL, ROWS = 18, 24
SET = 4
CH = 4
PIECES = 1
CW = D // CH
DP = ("zl", "x", "core")
GRID_AXES = ("y", "zh", "zl", "x", "core")
ANY = pl.BlockSpec(memory_space=pl.ANY)
VM = pl.BlockSpec(memory_space=pltpu.VMEM)
SM = pl.BlockSpec(memory_space=pltpu.SMEM)


def weight_copy(w_ref, wbuf, sem, held, slot, which, c):
    per = 16 // PIECES
    piece = pl.ds(c * per, per)
    return pltpu.make_async_copy(
        w_ref.at[held, piece, which], wbuf.at[slot, which, piece], sem.at[slot, which, c]
    )


def chunk(wbuf, slot, which, c):
    per = 16 // CH
    return wbuf[slot, which, c * per : (c + 1) * per].reshape(CW, R)


def columns(c):
    return slice(c * CW, (c + 1) * CW)


def inverse_rms(hbuf, layer):
    total = jnp.zeros((ROWS, 1), jnp.float32)
    for c in range(CH):
        v = hbuf[layer, :, columns(c)].astype(jnp.float32)
        total = total + jnp.sum(v * v, axis=-1, keepdims=True)
    return lax.rsqrt(total * (1.0 / D) + EPS)


def forward_kernel(*refs, aliased):
    flags, x_ref, w_ref = refs[:3]
    refs = refs[3 + (3 if aliased else 0) :]
    y_ref, h_out, pre_out, act_out = refs[:4]
    wbuf, hbuf, prebuf, actbuf, sem_w, sem_h, sem_p, sem_a = refs[4:]

    @pl.when(flags[0] == 1)
    def _():
        def wanted(layer, which, c):
            held = jnp.where(flags[1] == 1, SET - 1 - layer, layer)
            return weight_copy(w_ref, wbuf, sem_w, held, layer % 2, which, c)

        for which in range(2):
            for c in range(PIECES):
                wanted(0, which, c).start()
        hbuf[0] = x_ref[...]

        def step(layer):
            slot = layer % 2

            def arrive(which, c):
                if c % (CH // PIECES) == 0:
                    c = c // (CH // PIECES)
                    wanted(layer, which, c).wait()
                    if layer + 1 < SET:
                        wanted(layer + 1, which, c).start()

            pltpu.make_async_copy(hbuf.at[layer], h_out.at[layer], sem_h.at[layer]).start()
            inv = inverse_rms(hbuf, layer)
            pre = jnp.zeros((ROWS, R), jnp.float32)
            for c in range(CH):
                normed = (hbuf[layer, :, columns(c)].astype(jnp.float32) * inv).astype(jnp.bfloat16)
                arrive(0, c)
                pre = pre + jnp.dot(
                    normed, chunk(wbuf, slot, 0, c), preferred_element_type=jnp.float32
                )
            active = (pre / (1.0 + jnp.exp(-pre))).astype(jnp.bfloat16)
            prebuf[layer] = pre
            actbuf[layer] = active
            for c in range(CH):
                arrive(1, c)
                branch = lax.dot_general(
                    active,
                    chunk(wbuf, slot, 1, c),
                    (((1,), (1,)), ((), ())),
                    preferred_element_type=jnp.float32,
                )
                before = hbuf[layer, :, columns(c)].astype(jnp.float32)
                hbuf[layer + 1, :, columns(c)] = (before + branch).astype(jnp.bfloat16)

        for layer in range(SET):
            step(layer)
        y_ref[...] = hbuf[SET]
        copies = [
            pltpu.make_async_copy(prebuf, pre_out, sem_p.at[0]),
            pltpu.make_async_copy(actbuf, act_out, sem_a.at[0]),
        ]
        for one in copies:
            one.start()
        for layer in range(SET):
            copies.append(
                pltpu.make_async_copy(hbuf.at[layer], h_out.at[layer], sem_h.at[layer])
            )
        for one in copies:
            one.wait()


def run_forward(flags, rows, weights, held=None):
    outs = (
        jax.ShapeDtypeStruct((ROWS, D), jnp.bfloat16),
        jax.ShapeDtypeStruct((SET, ROWS, D), jnp.bfloat16),
        jax.ShapeDtypeStruct((SET, ROWS, R), jnp.float32),
        jax.ShapeDtypeStruct((SET, ROWS, R), jnp.bfloat16),
    )
    aliased = held is not None
    return pl.pallas_call(
        lambda *refs: forward_kernel(*refs, aliased=aliased),
        out_shape=outs,
        in_specs=[SM, VM, ANY] + ([ANY] * 3 if aliased else []),
        out_specs=(VM, ANY, ANY, ANY),
        scratch_shapes=[
            pltpu.VMEM((2, 2, 16, D // 16, R), jnp.bfloat16),
            pltpu.VMEM((SET + 1, ROWS, D), jnp.bfloat16),
            pltpu.VMEM((SET, ROWS, R), jnp.float32),
            pltpu.VMEM((SET, ROWS, R), jnp.bfloat16),
            pltpu.SemaphoreType.DMA((2, 2, PIECES)),
            pltpu.SemaphoreType.DMA((SET,)),
            pltpu.SemaphoreType.DMA((1,)),
            pltpu.SemaphoreType.DMA((1,)),
        ],
        input_output_aliases={3: 1, 4: 2, 5: 3} if aliased else {},
        compiler_params=pltpu.CompilerParams(vmem_limit_bytes=40 * 2**20),
        cost_estimate=pl.CostEstimate(
            flops=SET * ROWS * D * R, bytes_accessed=SET * D * R, transcendentals=0
        ),
        name="forward_set",
    )(flags, rows, weights, *(held or ()))


def backward_kernel(*refs, aliased, from_final, last):
    flags, g_ref, w_ref, h_in, pre_in = refs[:5]
    refs = refs[5 + (1 if aliased else 0) :]
    y_ref, g_out = refs[:2]
    wbuf, hbuf, prebuf, gbuf, dnbuf, gcut, sem_w, sem_h, sem_p, sem_g = refs[2:]

    @pl.when(flags[0] == 1)
    def _():
        def wanted(step, which, c):
            held = jnp.where(flags[1] == 1, step, SET - 1 - step)
            return weight_copy(w_ref, wbuf, sem_w, held, step % 2, which, c)

        def g_copy(step):
            return pltpu.make_async_copy(
                gcut.at[:, step], g_out.at[:, SET - 1 - step], sem_g.at[step]
            )

        def g_send(step):
            for r in range(16):
                gcut[r, step] = gbuf[step, :, r * (D // 16) : (r + 1) * (D // 16)]
            g_copy(step).start()

        def h_copy(layer):
            return pltpu.make_async_copy(h_in.at[layer], hbuf.at[layer], sem_h.at[layer])

        pre_copy = pltpu.make_async_copy(pre_in, prebuf, sem_p.at[0])
        pre_copy.start()
        h_copy(SET - 1).start()
        for which in (1, 0):
            for c in range(PIECES):
                wanted(0, which, c).start()
        for layer in range(SET - 2, -1, -1):
            h_copy(layer).start()
        if from_final:
            gbuf[0] = (g_ref[...].astype(jnp.float32) * COT).astype(jnp.bfloat16)
        else:
            gbuf[0] = g_ref[...]
        pre_copy.wait()
        steps = SET - 1 if last else SET

        def one_layer(step):
            layer = SET - 1 - step
            slot = step % 2

            def arrive(which, c):
                if c % (CH // PIECES) == 0:
                    c = c // (CH // PIECES)
                    wanted(step, which, c).wait()
                    if step + 1 < steps:
                        wanted(step + 1, which, c).start()

            g_send(step)
            h_copy(layer).wait()
            inv = inverse_rms(hbuf, layer)
            pre = prebuf[layer]
            sigma = 1.0 / (1.0 + jnp.exp(-pre))
            slope = sigma * (1.0 + pre * (1.0 - sigma))
            d_active = jnp.zeros((ROWS, R), jnp.float32)
            for c in range(CH):
                arrive(1, c)
                d_active = d_active + jnp.dot(
                    gbuf[step, :, columns(c)],
                    chunk(wbuf, slot, 1, c),
                    preferred_element_type=jnp.float32,
                )
            d_pre = (d_active * slope).astype(jnp.bfloat16)
            total = jnp.zeros((ROWS, 1), jnp.float32)
            for c in range(CH):
                arrive(0, c)
                d_normed = lax.dot_general(
                    d_pre,
                    chunk(wbuf, slot, 0, c),
                    (((1,), (1,)), ((), ())),
                    preferred_element_type=jnp.float32,
                )
                unit = hbuf[layer, :, columns(c)].astype(jnp.float32) * inv
                total = total + jnp.sum(d_normed * unit, axis=-1, keepdims=True)
                dnbuf[:, columns(c)] = d_normed
            mean = total * (1.0 / D)
            for c in range(CH):
                unit = hbuf[layer, :, columns(c)].astype(jnp.float32) * inv
                moved = inv * (dnbuf[:, columns(c)] - unit * mean)
                before = gbuf[step, :, columns(c)].astype(jnp.float32)
                gbuf[step + 1, :, columns(c)] = (before + moved).astype(jnp.bfloat16)

        for step in range(steps):
            one_layer(step)
        if last:
            g_send(SET - 1)
            h_copy(0).wait()
        y_ref[...] = gbuf[steps]
        for step in range(SET):
            g_copy(step).wait()


def run_backward(flags, g_rows, weights, h_held, pre_held, held=None, from_final=False, last=False):
    outs = (
        jax.ShapeDtypeStruct((ROWS, D), jnp.bfloat16),
        jax.ShapeDtypeStruct((16, SET, ROWS, D // 16), jnp.bfloat16),
    )
    aliased = held is not None
    return pl.pallas_call(
        lambda *refs: backward_kernel(*refs, aliased=aliased, from_final=from_final, last=last),
        out_shape=outs,
        in_specs=[SM, VM, ANY, ANY, ANY] + ([ANY] if aliased else []),
        out_specs=(VM, ANY),
        scratch_shapes=[
            pltpu.VMEM((2, 2, 16, D // 16, R), jnp.bfloat16),
            pltpu.VMEM((SET, ROWS, D), jnp.bfloat16),
            pltpu.VMEM((SET, ROWS, R), jnp.float32),
            pltpu.VMEM((SET + 1, ROWS, D), jnp.bfloat16),
            pltpu.VMEM((ROWS, D), jnp.float32),
            pltpu.VMEM((16, SET, ROWS, D // 16), jnp.bfloat16),
            pltpu.SemaphoreType.DMA((2, 2, PIECES)),
            pltpu.SemaphoreType.DMA((SET,)),
            pltpu.SemaphoreType.DMA((1,)),
            pltpu.SemaphoreType.DMA((SET,)),
        ],
        input_output_aliases={5: 1} if aliased else {},
        compiler_params=pltpu.CompilerParams(vmem_limit_bytes=40 * 2**20),
        cost_estimate=pl.CostEstimate(
            flops=SET * ROWS * D * R, bytes_accessed=SET * D * R, transcendentals=0
        ),
        name="backward_set",
    )(flags, g_rows, weights, h_held, pre_held, *((held,) if aliased else ()))


def grad_kernel(place, g_ref, act_ref, *out_refs, first):
    for k in range(SET):
        layer = lax.rem(place[0] + k, SET)
        g = g_ref[:, layer].reshape(16 * ROWS, D // 16)
        act = act_ref[:, first + layer].reshape(16 * ROWS, R)
        out_refs[k][...] = lax.dot_general(
            g, act, (((0,), (0,)), ((), ())), preferred_element_type=jnp.float32
        ).astype(jnp.bfloat16)


def run_grad(place, g_all, act_all, first):
    return pl.pallas_call(
        lambda *refs: grad_kernel(*refs, first=first),
        out_shape=(jax.ShapeDtypeStruct((D // 16, R), jnp.bfloat16),) * SET,
        in_specs=[SM, VM, VM],
        out_specs=(VM,) * SET,
        compiler_params=pltpu.CompilerParams(vmem_limit_bytes=40 * 2**20),
        name="grad_set",
    )(place, g_all, act_all)


def summed_over_zh(place, g_all, act_all, first):
    parts = run_grad(place, g_all, act_all, first)
    total = parts[0].astype(jnp.float32)
    for k in range(1, SET):
        route = [(source, (source + k) % SET) for source in range(SET)]
        total = total + lax.ppermute(parts[k], "zh", route).astype(jnp.float32)
    return total.astype(jnp.bfloat16)


def hop(rows):
    return lax.ppermute(rows, "y", [(0, 1), (1, 0), (2, 3), (3, 2)])


def spread(g_set):
    return lax.all_to_all(g_set, DP, 0, 0)


def shards(inputs_down, inputs_up, w_in, w_out):
    y, zh, dp = lax.axis_index("y"), lax.axis_index("zh"), lax.axis_index(DP)
    low_half = y < 2
    stage_p = (y == 0) | (y == 3)

    def own(layer_slot):
        parts = [
            lax.dynamic_slice(w, (0, layer_slot, dp * (D // 16), 0), (1, 1, D // 16, R))[0, 0]
            for w in (w_in, w_out)
        ]
        return jnp.stack(parts)

    def gathered(own_part):
        return lax.all_gather(own_part, ("zh",) + DP).reshape(SET, 16, 2, D // 16, R)

    first_slot = jnp.where(low_half, 0, 1)
    own_a, own_b = own(first_slot), own(1 - first_slot)
    w_a = gathered(own_a)
    own_b, w_a = lax.optimization_barrier((own_b, w_a))
    w_b = gathered(own_b)

    def flag(active, reverse):
        return jnp.stack([active.astype(jnp.int32), reverse.astype(jnp.int32)])

    p_a, p_b = flag(stage_p, ~low_half), flag(stage_p, low_half)
    q_a, q_b = flag(~stage_p, ~low_half), flag(~stage_p, low_half)

    mine = jnp.where(low_half, inputs_down, inputs_up).reshape(-1, D)
    mine = lax.dynamic_slice(mine, (zh * REAL, 0), (REAL, D))
    rows = jnp.pad(mine, ((0, ROWS - REAL), (0, 0)))

    rows, h_a, pre_a, act_a = run_forward(p_a, rows, w_a)
    rows = hop(rows)
    rows, h_a, pre_a, act_a = run_forward(q_a, rows, w_a, (h_a, pre_a, act_a))
    rows, h_b, pre_b, act_b = run_forward(q_b, rows, w_b)
    rows = hop(rows)
    rows, h_b, pre_b, act_b = run_forward(p_b, rows, w_b, (h_b, pre_b, act_b))
    act_all = lax.all_gather(jnp.concatenate([act_a, act_b], axis=0), DP)
    rows, g_b = run_backward(p_b, rows, w_b, h_b, pre_b, from_final=True)
    rows = hop(rows)
    rows, g_b = run_backward(q_b, rows, w_b, h_b, pre_b, held=g_b)
    rows, g_a = run_backward(q_a, rows, w_a, h_a, pre_a)
    rows = hop(rows)
    rows, g_a = run_backward(p_a, rows, w_a, h_a, pre_a, held=g_a, last=True)
    place = zh.astype(jnp.int32)[None]
    far_b = spread(g_b)
    g_a, far_b = lax.optimization_barrier((g_a, far_b))
    far_a = spread(g_a)
    sum_b = summed_over_zh(place, far_b, act_all, SET)
    sum_a = summed_over_zh(place, far_a, act_all, 0)
    kept = jnp.where(low_half, sum_a, sum_b)
    other = jnp.where(low_half, sum_b, sum_a)
    received = lax.ppermute(other, "y", [(0, 3), (3, 0), (1, 2), (2, 1)])
    return (kept.astype(jnp.float32) + received.astype(jnp.float32))[None]


def solution(mesh):
    fine = Mesh(mesh.devices.reshape(4, 4, 2, 4, 2), GRID_AXES)
    section = ("y", "zh")
    placed = (
        P(DP, None, None),
        P(DP, None, None),
        P(section, None, None, None),
        P(section, None, None, None),
    )
    return jax.shard_map(
        shards, mesh=fine, in_specs=placed, out_specs=P(section, DP, None), check_vma=False
    )
```

```python
import jax
import jax.numpy as jnp
from jax import lax
from jax.experimental import pallas as pl
from jax.experimental.pallas import tpu as pltpu
from jax.sharding import Mesh, PartitionSpec as P

EPS = 1e-06
COT = 0.0625
D, R = 5120, 256
REAL, ROWS = 18, 24
SET = 4
CH = 4
CW = D // CH
DP = ("zl", "x", "core")
GRID_AXES = ("y", "zh", "zl", "x", "core")
ANY = pl.BlockSpec(memory_space=pl.ANY)
VM = pl.BlockSpec(memory_space=pltpu.VMEM)
SM = pl.BlockSpec(memory_space=pltpu.SMEM)


class Gathered:
    count = 1

    def __init__(self, refs, flags, wbuf, sem):
        self.w, self.flags, self.wbuf, self.sem = refs[0], flags, wbuf, sem

    def copy(self, layer, slot, which):
        held = jnp.where(self.flags[1] == 1, SET - 1 - layer, layer)
        return pltpu.make_async_copy(
            self.w.at[held, :, which], self.wbuf.at[slot, :, which], self.sem.at[slot, which]
        )

    def first(self, layer, order):
        for which in order:
            self.copy(layer, 0, which).start()

    def begin(self, layer, slot):
        pass

    def arrive(self, layer, slot, which, following):
        self.copy(layer, slot, which).wait()
        if following is not None:
            self.copy(following, 1 - slot, which).start()


class Scattered:
    count = 18

    def __init__(self, refs, flags, wbuf, sem):
        self.own, self.parts = refs[:2], refs[2:]
        self.flags, self.wbuf, self.sem = flags, wbuf, sem

    def fetch(self, layer, slot):
        flags = self.flags
        held = jnp.where(flags[1] == 1, SET - 1 - layer, layer)
        away = lax.rem(held + SET - flags[3], SET)

        @pl.when(away == 0)
        def _():
            for which in range(2):
                pltpu.make_async_copy(
                    self.own[which].at[flags[2]], self.wbuf.at[slot, :, which], self.sem.at[slot, 0]
                ).start()

        @pl.when(away > 0)
        def _():
            for n in range(16):
                zl_off, x_off, core_off = n // 8, (n // 2) % 4, n % 2
                zl = lax.rem(flags[4] + zl_off, 2)
                x = lax.rem(flags[5] + x_off, 4)
                core = lax.rem(flags[6] + core_off, 2)
                pltpu.make_async_copy(
                    self.parts[n].at[away - 1],
                    self.wbuf.at[slot, zl * 8 + x * 2 + core],
                    self.sem.at[slot, 0],
                ).start()

    def first(self, layer, order):
        self.leading = order[0]
        self.fetch(layer, 0)

    def begin(self, following, slot):
        if following is not None:
            self.fetch(following, 1 - slot)

    def arrive(self, layer, slot, which, following):
        if which == self.leading:
            pltpu.make_async_copy(
                self.wbuf.at[1 - slot], self.wbuf.at[slot], self.sem.at[slot, 0]
            ).wait()


def chunk(wbuf, slot, which, c):
    per = 16 // CH
    return wbuf[slot, c * per : (c + 1) * per, which].reshape(CW, R)


def columns(c):
    return slice(c * CW, (c + 1) * CW)


def inverse_rms(hbuf, layer):
    total = jnp.zeros((ROWS, 1), jnp.float32)
    for c in range(CH):
        v = hbuf[layer, :, columns(c)].astype(jnp.float32)
        total = total + jnp.sum(v * v, axis=-1, keepdims=True)
    return lax.rsqrt(total * (1.0 / D) + EPS)


def forward_kernel(*refs, source, aliased):
    flags, x_ref = refs[:2]
    w_refs = refs[2 : 2 + source.count]
    refs = refs[2 + source.count + (3 if aliased else 0) :]
    y_ref, h_out, pre_out, act_out = refs[:4]
    wbuf, hbuf, prebuf, actbuf, sem_w, sem_h, sem_p, sem_a = refs[4:]

    @pl.when(flags[0] == 1)
    def _():
        weights = source(w_refs, flags, wbuf, sem_w)
        weights.first(0, (0, 1))
        hbuf[0] = x_ref[...]

        def step(layer):
            slot = layer % 2

            following = layer + 1 if layer + 1 < SET else None
            weights.begin(following, slot)
            pltpu.make_async_copy(hbuf.at[layer], h_out.at[layer], sem_h.at[layer]).start()
            inv = inverse_rms(hbuf, layer)
            pre = jnp.zeros((ROWS, R), jnp.float32)
            weights.arrive(layer, slot, 0, following)
            for c in range(CH):
                normed = (hbuf[layer, :, columns(c)].astype(jnp.float32) * inv).astype(jnp.bfloat16)
                pre = pre + jnp.dot(
                    normed, chunk(wbuf, slot, 0, c), preferred_element_type=jnp.float32
                )
            active = (pre / (1.0 + jnp.exp(-pre))).astype(jnp.bfloat16)
            prebuf[layer] = pre
            actbuf[layer] = active
            weights.arrive(layer, slot, 1, following)
            for c in range(CH):
                branch = lax.dot_general(
                    active,
                    chunk(wbuf, slot, 1, c),
                    (((1,), (1,)), ((), ())),
                    preferred_element_type=jnp.float32,
                )
                before = hbuf[layer, :, columns(c)].astype(jnp.float32)
                hbuf[layer + 1, :, columns(c)] = (before + branch).astype(jnp.bfloat16)

        for layer in range(SET):
            step(layer)
        y_ref[...] = hbuf[SET]
        copies = [
            pltpu.make_async_copy(prebuf, pre_out, sem_p.at[0]),
            pltpu.make_async_copy(actbuf, act_out, sem_a.at[0]),
        ]
        for one in copies:
            one.start()
        for layer in range(SET):
            copies.append(
                pltpu.make_async_copy(hbuf.at[layer], h_out.at[layer], sem_h.at[layer])
            )
        for one in copies:
            one.wait()


def run_forward(flags, rows, weights, held=None):
    source = Gathered if len(weights) == 1 else Scattered
    first = 2 + source.count
    outs = (
        jax.ShapeDtypeStruct((ROWS, D), jnp.bfloat16),
        jax.ShapeDtypeStruct((SET, ROWS, D), jnp.bfloat16),
        jax.ShapeDtypeStruct((SET, ROWS, R), jnp.float32),
        jax.ShapeDtypeStruct((SET, ROWS, R), jnp.bfloat16),
    )
    aliased = held is not None
    return pl.pallas_call(
        lambda *refs: forward_kernel(*refs, source=source, aliased=aliased),
        out_shape=outs,
        in_specs=[SM, VM] + [ANY] * (source.count + (3 if aliased else 0)),
        out_specs=(VM, ANY, ANY, ANY),
        scratch_shapes=[
            pltpu.VMEM((2, 16, 2, D // 16, R), jnp.bfloat16),
            pltpu.VMEM((SET + 1, ROWS, D), jnp.bfloat16),
            pltpu.VMEM((SET, ROWS, R), jnp.float32),
            pltpu.VMEM((SET, ROWS, R), jnp.bfloat16),
            pltpu.SemaphoreType.DMA((2, 2)),
            pltpu.SemaphoreType.DMA((SET,)),
            pltpu.SemaphoreType.DMA((1,)),
            pltpu.SemaphoreType.DMA((1,)),
        ],
        input_output_aliases={first: 1, first + 1: 2, first + 2: 3} if aliased else {},
        compiler_params=pltpu.CompilerParams(vmem_limit_bytes=52 * 2**20),
        cost_estimate=pl.CostEstimate(
            flops=SET * ROWS * D * R, bytes_accessed=SET * D * R, transcendentals=0
        ),
        name="forward_set",
    )(flags, rows, *weights, *(held or ()))


def backward_kernel(*refs, source, aliased, from_final, last):
    flags, g_ref, h_in, pre_in = refs[:4]
    w_refs = refs[4 : 4 + source.count]
    refs = refs[4 + source.count + (1 if aliased else 0) :]
    y_ref, g_out = refs[:2]
    wbuf, hbuf, prebuf, gbuf, dnbuf, gcut, sem_w, sem_h, sem_p, sem_g = refs[2:]

    @pl.when(flags[0] == 1)
    def _():
        weights = source(w_refs, flags, wbuf, sem_w)

        def g_copy(step):
            return pltpu.make_async_copy(
                gcut.at[:, step], g_out.at[:, SET - 1 - step], sem_g.at[step]
            )

        def g_send(step):
            for r in range(16):
                gcut[r, step] = gbuf[step, :, r * (D // 16) : (r + 1) * (D // 16)]
            g_copy(step).start()

        def h_copy(layer):
            return pltpu.make_async_copy(h_in.at[layer], hbuf.at[layer], sem_h.at[layer])

        pre_copy = pltpu.make_async_copy(pre_in, prebuf, sem_p.at[0])
        pre_copy.start()
        h_copy(SET - 1).start()
        weights.first(SET - 1, (1, 0))
        for layer in range(SET - 2, -1, -1):
            h_copy(layer).start()
        if from_final:
            gbuf[0] = (g_ref[...].astype(jnp.float32) * COT).astype(jnp.bfloat16)
        else:
            gbuf[0] = g_ref[...]
        pre_copy.wait()
        steps = SET - 1 if last else SET

        def one_layer(step):
            layer = SET - 1 - step
            slot = step % 2

            following = layer - 1 if step + 1 < steps else None
            weights.begin(following, slot)
            g_send(step)
            h_copy(layer).wait()
            inv = inverse_rms(hbuf, layer)
            pre = prebuf[layer]
            sigma = 1.0 / (1.0 + jnp.exp(-pre))
            slope = sigma * (1.0 + pre * (1.0 - sigma))
            d_active = jnp.zeros((ROWS, R), jnp.float32)
            weights.arrive(layer, slot, 1, following)
            for c in range(CH):
                d_active = d_active + jnp.dot(
                    gbuf[step, :, columns(c)],
                    chunk(wbuf, slot, 1, c),
                    preferred_element_type=jnp.float32,
                )
            d_pre = (d_active * slope).astype(jnp.bfloat16)
            total = jnp.zeros((ROWS, 1), jnp.float32)
            weights.arrive(layer, slot, 0, following)
            for c in range(CH):
                d_normed = lax.dot_general(
                    d_pre,
                    chunk(wbuf, slot, 0, c),
                    (((1,), (1,)), ((), ())),
                    preferred_element_type=jnp.float32,
                )
                unit = hbuf[layer, :, columns(c)].astype(jnp.float32) * inv
                total = total + jnp.sum(d_normed * unit, axis=-1, keepdims=True)
                dnbuf[:, columns(c)] = d_normed
            mean = total * (1.0 / D)
            for c in range(CH):
                unit = hbuf[layer, :, columns(c)].astype(jnp.float32) * inv
                moved = inv * (dnbuf[:, columns(c)] - unit * mean)
                before = gbuf[step, :, columns(c)].astype(jnp.float32)
                gbuf[step + 1, :, columns(c)] = (before + moved).astype(jnp.bfloat16)

        for step in range(steps):
            one_layer(step)
        if last:
            g_send(SET - 1)
            h_copy(0).wait()
        y_ref[...] = gbuf[steps]
        for step in range(SET):
            g_copy(step).wait()


def run_backward(flags, g_rows, weights, h_held, pre_held, held=None, from_final=False, last=False):
    source = Gathered if len(weights) == 1 else Scattered
    outs = (
        jax.ShapeDtypeStruct((ROWS, D), jnp.bfloat16),
        jax.ShapeDtypeStruct((16, SET, ROWS, D // 16), jnp.bfloat16),
    )
    aliased = held is not None
    return pl.pallas_call(
        lambda *refs: backward_kernel(
            *refs, source=source, aliased=aliased, from_final=from_final, last=last
        ),
        out_shape=outs,
        in_specs=[SM, VM, ANY, ANY] + [ANY] * (source.count + (1 if aliased else 0)),
        out_specs=(VM, ANY),
        scratch_shapes=[
            pltpu.VMEM((2, 16, 2, D // 16, R), jnp.bfloat16),
            pltpu.VMEM((SET, ROWS, D), jnp.bfloat16),
            pltpu.VMEM((SET, ROWS, R), jnp.float32),
            pltpu.VMEM((SET + 1, ROWS, D), jnp.bfloat16),
            pltpu.VMEM((ROWS, D), jnp.float32),
            pltpu.VMEM((16, SET, ROWS, D // 16), jnp.bfloat16),
            pltpu.SemaphoreType.DMA((2, 2)),
            pltpu.SemaphoreType.DMA((SET,)),
            pltpu.SemaphoreType.DMA((1,)),
            pltpu.SemaphoreType.DMA((SET,)),
        ],
        input_output_aliases={4 + source.count: 1} if aliased else {},
        compiler_params=pltpu.CompilerParams(vmem_limit_bytes=52 * 2**20),
        cost_estimate=pl.CostEstimate(
            flops=SET * ROWS * D * R, bytes_accessed=SET * D * R, transcendentals=0
        ),
        name="backward_set",
    )(flags, g_rows, h_held, pre_held, *weights, *((held,) if aliased else ()))


def grad_kernel(place, g_ref, act_ref, *out_refs, first):
    for k in range(SET):
        layer = lax.rem(place[0] + k, SET)
        g = g_ref[:, layer].reshape(16 * ROWS, D // 16)
        act = act_ref[:, first + layer].reshape(16 * ROWS, R)
        out_refs[k][...] = lax.dot_general(
            g, act, (((0,), (0,)), ((), ())), preferred_element_type=jnp.float32
        ).astype(jnp.bfloat16)


def run_grad(place, g_all, act_all, first):
    return pl.pallas_call(
        lambda *refs: grad_kernel(*refs, first=first),
        out_shape=(jax.ShapeDtypeStruct((D // 16, R), jnp.bfloat16),) * SET,
        in_specs=[SM, VM, VM],
        out_specs=(VM,) * SET,
        compiler_params=pltpu.CompilerParams(vmem_limit_bytes=52 * 2**20),
        name="grad_set",
    )(place, g_all, act_all)


def summed_over_zh(place, g_all, act_all, first):
    parts = run_grad(place, g_all, act_all, first)
    total = parts[0].astype(jnp.float32)
    for k in range(1, SET):
        route = [(source, (source + k) % SET) for source in range(SET)]
        total = total + lax.ppermute(parts[k], "zh", route).astype(jnp.float32)
    return total.astype(jnp.bfloat16)


def hop(rows):
    return lax.ppermute(rows, "y", [(0, 1), (1, 0), (2, 3), (3, 2)])


def spread(g_set):
    return lax.all_to_all(g_set, DP, 0, 0)


def from_ring(block, axis, away):
    count = lax.axis_size(axis)
    return lax.ppermute(block, axis, [((d + away) % count, d) for d in range(count)])


def passed_round(own_part):
    near = jnp.stack([from_ring(own_part, "zh", away) for away in (1, 2, 3)])
    far = from_ring(near, "zl", 1)
    near_up, near_down = from_ring(near, "x", 1), from_ring(near, "x", -1)
    near_across = from_ring(near_up, "x", 1)
    far_up, far_down = from_ring(far, "x", 1), from_ring(far, "x", -1)
    far_across = from_ring(far_down, "x", -1)
    parts = []
    for one in (near, near_up, near_across, near_down, far, far_up, far_across, far_down):
        parts += [one, from_ring(one, "core", 1)]
    return tuple(parts)


def shards(inputs_down, inputs_up, w_in, w_out):
    y, zh, dp = lax.axis_index("y"), lax.axis_index("zh"), lax.axis_index(DP)
    low_half = y < 2
    stage_p = (y == 0) | (y == 3)

    def own(layer_slot):
        parts = [
            lax.dynamic_slice(w, (0, layer_slot, dp * (D // 16), 0), (1, 1, D // 16, R))[0, 0]
            for w in (w_in, w_out)
        ]
        return jnp.stack(parts)

    def gathered(own_part):
        return lax.all_gather(own_part, ("zh",) + DP).reshape(SET, 16, 2, D // 16, R)

    first_slot = jnp.where(low_half, 0, 1)
    w_a = (gathered(own(first_slot)),)
    w_b = tuple(w[0].reshape(2, 16, D // 16, R) for w in (w_in, w_out)) + passed_round(
        own(1 - first_slot)
    )
    place_flags = jnp.stack([1 - first_slot, zh] + [lax.axis_index(name) for name in DP])

    def flag(active, reverse):
        both = jnp.stack([active.astype(jnp.int32), reverse.astype(jnp.int32)])
        return jnp.concatenate([both, place_flags.astype(jnp.int32)])

    p_a, p_b = flag(stage_p, ~low_half), flag(stage_p, low_half)
    q_a, q_b = flag(~stage_p, ~low_half), flag(~stage_p, low_half)

    mine = jnp.where(low_half, inputs_down, inputs_up).reshape(-1, D)
    mine = lax.dynamic_slice(mine, (zh * REAL, 0), (REAL, D))
    rows = jnp.pad(mine, ((0, ROWS - REAL), (0, 0)))

    rows, h_a, pre_a, act_a = run_forward(p_a, rows, w_a)
    rows = hop(rows)
    rows, h_a, pre_a, act_a = run_forward(q_a, rows, w_a, (h_a, pre_a, act_a))
    rows, h_b, pre_b, act_b = run_forward(q_b, rows, w_b)
    rows = hop(rows)
    rows, h_b, pre_b, act_b = run_forward(p_b, rows, w_b, (h_b, pre_b, act_b))
    act_all = lax.all_gather(jnp.concatenate([act_a, act_b], axis=0), DP)
    rows, g_b = run_backward(p_b, rows, w_b, h_b, pre_b, from_final=True)
    rows = hop(rows)
    rows, g_b = run_backward(q_b, rows, w_b, h_b, pre_b, held=g_b)
    rows, g_a = run_backward(q_a, rows, w_a, h_a, pre_a)
    rows = hop(rows)
    rows, g_a = run_backward(p_a, rows, w_a, h_a, pre_a, held=g_a, last=True)
    place = zh.astype(jnp.int32)[None]
    far_b = spread(g_b)
    g_a, far_b = lax.optimization_barrier((g_a, far_b))
    far_a = spread(g_a)
    sum_b = summed_over_zh(place, far_b, act_all, SET)
    sum_a = summed_over_zh(place, far_a, act_all, 0)
    kept = jnp.where(low_half, sum_a, sum_b)
    other = jnp.where(low_half, sum_b, sum_a)
    received = lax.ppermute(other, "y", [(0, 3), (3, 0), (1, 2), (2, 1)])
    return (kept.astype(jnp.float32) + received.astype(jnp.float32))[None]


def solution(mesh):
    fine = Mesh(mesh.devices.reshape(4, 4, 2, 4, 2), GRID_AXES)
    section = ("y", "zh")
    placed = (
        P(DP, None, None),
        P(DP, None, None),
        P(section, None, None, None),
        P(section, None, None, None),
    )
    return jax.shard_map(
        shards, mesh=fine, in_specs=placed, out_specs=P(section, DP, None), check_vma=False
    )
```

```python
import jax
import jax.numpy as jnp
from jax import lax
from jax.experimental import pallas as pl
from jax.experimental.pallas import tpu as pltpu
from jax.sharding import Mesh, PartitionSpec as P

EPS = 1e-06
COT = 0.0625
D, R = 5120, 256
REAL, ROWS = 18, 24
SET = 4
CH = 4
CW = D // CH
DP = ("zl", "x", "core")
GRID_AXES = ("y", "zh", "zl", "x", "core")
ANY = pl.BlockSpec(memory_space=pl.ANY)
VM = pl.BlockSpec(memory_space=pltpu.VMEM)
SM = pl.BlockSpec(memory_space=pltpu.SMEM)


class Gathered:
    count = 1

    def __init__(self, refs, flags, wbuf, sem):
        self.w, self.flags, self.wbuf, self.sem = refs[0], flags, wbuf, sem

    def copy(self, layer, slot, which):
        held = jnp.where(self.flags[1] == 1, SET - 1 - layer, layer)
        return pltpu.make_async_copy(
            self.w.at[held, :, which], self.wbuf.at[slot, :, which], self.sem.at[slot, which]
        )

    def first(self, layer, order):
        self.order = order
        self.begin(layer, 0)

    def begin(self, layer, slot):
        for which in self.order:
            self.copy(layer, slot, which).start()

    def arrive(self, layer, slot, which):
        self.copy(layer, slot, which).wait()


class Scattered:
    count = 18

    def __init__(self, refs, flags, wbuf, sem):
        self.own, self.parts = refs[:2], refs[2:]
        self.flags, self.wbuf, self.sem = flags, wbuf, sem

    def fetch(self, layer, slot):
        flags = self.flags
        held = jnp.where(flags[1] == 1, SET - 1 - layer, layer)
        away = lax.rem(held + SET - flags[3], SET)

        @pl.when(away == 0)
        def _():
            for which in range(2):
                pltpu.make_async_copy(
                    self.own[which].at[flags[2]], self.wbuf.at[slot, :, which], self.sem.at[slot, 0]
                ).start()

        @pl.when(away > 0)
        def _():
            for n in range(16):
                zl_off, x_off, core_off = n // 8, (n // 2) % 4, n % 2
                zl = lax.rem(flags[4] + zl_off, 2)
                x = lax.rem(flags[5] + x_off, 4)
                core = lax.rem(flags[6] + core_off, 2)
                pltpu.make_async_copy(
                    self.parts[n].at[away - 1],
                    self.wbuf.at[slot, zl * 8 + x * 2 + core],
                    self.sem.at[slot, 0],
                ).start()

    def first(self, layer, order):
        self.leading = order[0]
        self.fetch(layer, 0)

    def begin(self, layer, slot):
        self.fetch(layer, slot)

    def arrive(self, layer, slot, which):
        if which == self.leading:
            pltpu.make_async_copy(
                self.wbuf.at[1 - slot], self.wbuf.at[slot], self.sem.at[slot, 0]
            ).wait()


def chunk(wbuf, slot, which, c):
    per = 16 // CH
    return wbuf[slot, c * per : (c + 1) * per, which].reshape(CW, R)


def columns(c):
    return slice(c * CW, (c + 1) * CW)


def inverse_rms(hbuf, layer):
    total = jnp.zeros((ROWS, 1), jnp.float32)
    for c in range(CH):
        v = hbuf[layer, :, columns(c)].astype(jnp.float32)
        total = total + jnp.sum(v * v, axis=-1, keepdims=True)
    return lax.rsqrt(total * (1.0 / D) + EPS)


def forward_kernel(*refs, source, aliased):
    flags, x_ref = refs[:2]
    w_refs = refs[2 : 2 + source.count]
    refs = refs[2 + source.count + (3 if aliased else 0) :]
    y_ref, h_out, pre_out, act_out = refs[:4]
    wbuf, hbuf, prebuf, actbuf, sem_w, sem_h, sem_p, sem_a = refs[4:]

    @pl.when(flags[0] == 1)
    def _():
        weights = source(w_refs, flags, wbuf, sem_w)
        weights.first(0, (0, 1))
        hbuf[0] = x_ref[...]

        def step(layer, carry):
            slot = lax.rem(layer, 2)


            @pl.when(layer + 1 < SET)
            def _():
                weights.begin(layer + 1, 1 - slot)

            pltpu.make_async_copy(hbuf.at[layer], h_out.at[layer], sem_h.at[layer]).start()
            inv = inverse_rms(hbuf, layer)
            pre = jnp.zeros((ROWS, R), jnp.float32)
            weights.arrive(layer, slot, 0)
            for c in range(CH):
                normed = (hbuf[layer, :, columns(c)].astype(jnp.float32) * inv).astype(jnp.bfloat16)
                pre = pre + jnp.dot(
                    normed, chunk(wbuf, slot, 0, c), preferred_element_type=jnp.float32
                )
            active = (pre / (1.0 + jnp.exp(-pre))).astype(jnp.bfloat16)
            prebuf[layer] = pre
            actbuf[layer] = active
            weights.arrive(layer, slot, 1)
            for c in range(CH):
                branch = lax.dot_general(
                    active,
                    chunk(wbuf, slot, 1, c),
                    (((1,), (1,)), ((), ())),
                    preferred_element_type=jnp.float32,
                )
                before = hbuf[layer, :, columns(c)].astype(jnp.float32)
                hbuf[layer + 1, :, columns(c)] = (before + branch).astype(jnp.bfloat16)
            return carry

        lax.fori_loop(0, SET, step, 0)
        y_ref[...] = hbuf[SET]
        copies = [
            pltpu.make_async_copy(prebuf, pre_out, sem_p.at[0]),
            pltpu.make_async_copy(actbuf, act_out, sem_a.at[0]),
        ]
        for one in copies:
            one.start()
        for layer in range(SET):
            copies.append(
                pltpu.make_async_copy(hbuf.at[layer], h_out.at[layer], sem_h.at[layer])
            )
        for one in copies:
            one.wait()


def run_forward(flags, rows, weights, held=None):
    source = Gathered if len(weights) == 1 else Scattered
    first = 2 + source.count
    outs = (
        jax.ShapeDtypeStruct((ROWS, D), jnp.bfloat16),
        jax.ShapeDtypeStruct((SET, ROWS, D), jnp.bfloat16),
        jax.ShapeDtypeStruct((SET, ROWS, R), jnp.float32),
        jax.ShapeDtypeStruct((SET, ROWS, R), jnp.bfloat16),
    )
    aliased = held is not None
    return pl.pallas_call(
        lambda *refs: forward_kernel(*refs, source=source, aliased=aliased),
        out_shape=outs,
        in_specs=[SM, VM] + [ANY] * (source.count + (3 if aliased else 0)),
        out_specs=(VM, ANY, ANY, ANY),
        scratch_shapes=[
            pltpu.VMEM((2, 16, 2, D // 16, R), jnp.bfloat16),
            pltpu.VMEM((SET + 1, ROWS, D), jnp.bfloat16),
            pltpu.VMEM((SET, ROWS, R), jnp.float32),
            pltpu.VMEM((SET, ROWS, R), jnp.bfloat16),
            pltpu.SemaphoreType.DMA((2, 2)),
            pltpu.SemaphoreType.DMA((SET,)),
            pltpu.SemaphoreType.DMA((1,)),
            pltpu.SemaphoreType.DMA((1,)),
        ],
        input_output_aliases={first: 1, first + 1: 2, first + 2: 3} if aliased else {},
        compiler_params=pltpu.CompilerParams(vmem_limit_bytes=52 * 2**20),
        cost_estimate=pl.CostEstimate(
            flops=SET * ROWS * D * R, bytes_accessed=SET * D * R, transcendentals=0
        ),
        name="forward_set",
    )(flags, rows, *weights, *(held or ()))


def backward_kernel(*refs, source, aliased, from_final, last):
    flags, g_ref, h_in, pre_in = refs[:4]
    w_refs = refs[4 : 4 + source.count]
    refs = refs[4 + source.count + (1 if aliased else 0) :]
    y_ref, g_out = refs[:2]
    wbuf, hbuf, prebuf, gbuf, dnbuf, gcut, sem_w, sem_h, sem_p, sem_g = refs[2:]

    @pl.when(flags[0] == 1)
    def _():
        weights = source(w_refs, flags, wbuf, sem_w)

        def g_copy(step):
            return pltpu.make_async_copy(
                gcut.at[:, step], g_out.at[:, SET - 1 - step], sem_g.at[step]
            )

        def g_send(step):
            for r in range(16):
                gcut[r, step] = gbuf[step, :, r * (D // 16) : (r + 1) * (D // 16)]
            g_copy(step).start()

        def h_copy(layer):
            return pltpu.make_async_copy(h_in.at[layer], hbuf.at[layer], sem_h.at[layer])

        pre_copy = pltpu.make_async_copy(pre_in, prebuf, sem_p.at[0])
        pre_copy.start()
        h_copy(SET - 1).start()
        weights.first(SET - 1, (1, 0))
        for layer in range(SET - 2, -1, -1):
            h_copy(layer).start()
        if from_final:
            gbuf[0] = (g_ref[...].astype(jnp.float32) * COT).astype(jnp.bfloat16)
        else:
            gbuf[0] = g_ref[...]
        pre_copy.wait()
        steps = SET - 1 if last else SET

        def one_layer(step, carry):
            layer = SET - 1 - step
            slot = lax.rem(step, 2)


            @pl.when(step + 1 < steps)
            def _():
                weights.begin(layer - 1, 1 - slot)

            g_send(step)
            h_copy(layer).wait()
            inv = inverse_rms(hbuf, layer)
            pre = prebuf[layer]
            sigma = 1.0 / (1.0 + jnp.exp(-pre))
            slope = sigma * (1.0 + pre * (1.0 - sigma))
            d_active = jnp.zeros((ROWS, R), jnp.float32)
            weights.arrive(layer, slot, 1)
            for c in range(CH):
                d_active = d_active + jnp.dot(
                    gbuf[step, :, columns(c)],
                    chunk(wbuf, slot, 1, c),
                    preferred_element_type=jnp.float32,
                )
            d_pre = (d_active * slope).astype(jnp.bfloat16)
            total = jnp.zeros((ROWS, 1), jnp.float32)
            weights.arrive(layer, slot, 0)
            for c in range(CH):
                d_normed = lax.dot_general(
                    d_pre,
                    chunk(wbuf, slot, 0, c),
                    (((1,), (1,)), ((), ())),
                    preferred_element_type=jnp.float32,
                )
                unit = hbuf[layer, :, columns(c)].astype(jnp.float32) * inv
                total = total + jnp.sum(d_normed * unit, axis=-1, keepdims=True)
                dnbuf[:, columns(c)] = d_normed
            mean = total * (1.0 / D)
            for c in range(CH):
                unit = hbuf[layer, :, columns(c)].astype(jnp.float32) * inv
                moved = inv * (dnbuf[:, columns(c)] - unit * mean)
                before = gbuf[step, :, columns(c)].astype(jnp.float32)
                gbuf[step + 1, :, columns(c)] = (before + moved).astype(jnp.bfloat16)
            return carry

        lax.fori_loop(0, steps, one_layer, 0)
        if last:
            g_send(SET - 1)
            h_copy(0).wait()
        y_ref[...] = gbuf[steps]
        for step in range(SET):
            g_copy(step).wait()


def run_backward(flags, g_rows, weights, h_held, pre_held, held=None, from_final=False, last=False):
    source = Gathered if len(weights) == 1 else Scattered
    outs = (
        jax.ShapeDtypeStruct((ROWS, D), jnp.bfloat16),
        jax.ShapeDtypeStruct((16, SET, ROWS, D // 16), jnp.bfloat16),
    )
    aliased = held is not None
    return pl.pallas_call(
        lambda *refs: backward_kernel(
            *refs, source=source, aliased=aliased, from_final=from_final, last=last
        ),
        out_shape=outs,
        in_specs=[SM, VM, ANY, ANY] + [ANY] * (source.count + (1 if aliased else 0)),
        out_specs=(VM, ANY),
        scratch_shapes=[
            pltpu.VMEM((2, 16, 2, D // 16, R), jnp.bfloat16),
            pltpu.VMEM((SET, ROWS, D), jnp.bfloat16),
            pltpu.VMEM((SET, ROWS, R), jnp.float32),
            pltpu.VMEM((SET + 1, ROWS, D), jnp.bfloat16),
            pltpu.VMEM((ROWS, D), jnp.float32),
            pltpu.VMEM((16, SET, ROWS, D // 16), jnp.bfloat16),
            pltpu.SemaphoreType.DMA((2, 2)),
            pltpu.SemaphoreType.DMA((SET,)),
            pltpu.SemaphoreType.DMA((1,)),
            pltpu.SemaphoreType.DMA((SET,)),
        ],
        input_output_aliases={4 + source.count: 1} if aliased else {},
        compiler_params=pltpu.CompilerParams(vmem_limit_bytes=52 * 2**20),
        cost_estimate=pl.CostEstimate(
            flops=SET * ROWS * D * R, bytes_accessed=SET * D * R, transcendentals=0
        ),
        name="backward_set",
    )(flags, g_rows, h_held, pre_held, *weights, *((held,) if aliased else ()))


def grad_kernel(place, g_ref, act_ref, *out_refs, first):
    for k in range(SET):
        layer = lax.rem(place[0] + k, SET)
        g = g_ref[:, layer].reshape(16 * ROWS, D // 16)
        act = act_ref[:, first + layer].reshape(16 * ROWS, R)
        out_refs[k][...] = lax.dot_general(
            g, act, (((0,), (0,)), ((), ())), preferred_element_type=jnp.float32
        ).astype(jnp.bfloat16)


def run_grad(place, g_all, act_all, first):
    return pl.pallas_call(
        lambda *refs: grad_kernel(*refs, first=first),
        out_shape=(jax.ShapeDtypeStruct((D // 16, R), jnp.bfloat16),) * SET,
        in_specs=[SM, VM, VM],
        out_specs=(VM,) * SET,
        compiler_params=pltpu.CompilerParams(vmem_limit_bytes=52 * 2**20),
        name="grad_set",
    )(place, g_all, act_all)


def summed_over_zh(place, g_all, act_all, first):
    parts = run_grad(place, g_all, act_all, first)
    total = parts[0].astype(jnp.float32)
    for k in range(1, SET):
        route = [(source, (source + k) % SET) for source in range(SET)]
        total = total + lax.ppermute(parts[k], "zh", route).astype(jnp.float32)
    return total.astype(jnp.bfloat16)


def hop(rows):
    return lax.ppermute(rows, "y", [(0, 1), (1, 0), (2, 3), (3, 2)])


def spread(g_set):
    return lax.all_to_all(g_set, DP, 0, 0)


def from_ring(block, axis, away):
    count = lax.axis_size(axis)
    return lax.ppermute(block, axis, [((d + away) % count, d) for d in range(count)])


def passed_round(own_part):
    near = jnp.stack([from_ring(own_part, "zh", away) for away in (1, 2, 3)])
    far = from_ring(near, "zl", 1)
    near_up, near_down = from_ring(near, "x", 1), from_ring(near, "x", -1)
    near_across = from_ring(near_up, "x", 1)
    far_up, far_down = from_ring(far, "x", 1), from_ring(far, "x", -1)
    far_across = from_ring(far_down, "x", -1)
    parts = []
    for one in (near, near_up, near_across, near_down, far, far_up, far_across, far_down):
        parts += [one, from_ring(one, "core", 1)]
    return tuple(parts)


def shards(inputs_down, inputs_up, w_in, w_out):
    y, zh, dp = lax.axis_index("y"), lax.axis_index("zh"), lax.axis_index(DP)
    low_half = y < 2
    stage_p = (y == 0) | (y == 3)

    def own(layer_slot):
        parts = [
            lax.dynamic_slice(w, (0, layer_slot, dp * (D // 16), 0), (1, 1, D // 16, R))[0, 0]
            for w in (w_in, w_out)
        ]
        return jnp.stack(parts)

    def gathered(own_part):
        return lax.all_gather(own_part, ("zh",) + DP).reshape(SET, 16, 2, D // 16, R)

    first_slot = jnp.where(low_half, 0, 1)
    w_b = (gathered(own(1 - first_slot)),)
    w_a = tuple(w[0].reshape(2, 16, D // 16, R) for w in (w_in, w_out)) + passed_round(
        own(first_slot)
    )
    place_flags = jnp.stack([first_slot, zh] + [lax.axis_index(name) for name in DP])

    def flag(active, reverse):
        both = jnp.stack([active.astype(jnp.int32), reverse.astype(jnp.int32)])
        return jnp.concatenate([both, place_flags.astype(jnp.int32)])

    p_a, p_b = flag(stage_p, ~low_half), flag(stage_p, low_half)
    q_a, q_b = flag(~stage_p, ~low_half), flag(~stage_p, low_half)

    mine = jnp.where(low_half, inputs_down, inputs_up).reshape(-1, D)
    mine = lax.dynamic_slice(mine, (zh * REAL, 0), (REAL, D))
    rows = jnp.pad(mine, ((0, ROWS - REAL), (0, 0)))

    rows, h_a, pre_a, act_a = run_forward(p_a, rows, w_a)
    rows = hop(rows)
    rows, h_a, pre_a, act_a = run_forward(q_a, rows, w_a, (h_a, pre_a, act_a))
    rows, h_b, pre_b, act_b = run_forward(q_b, rows, w_b)
    rows = hop(rows)
    rows, h_b, pre_b, act_b = run_forward(p_b, rows, w_b, (h_b, pre_b, act_b))
    act_all = lax.all_gather(jnp.concatenate([act_a, act_b], axis=0), DP)
    rows, g_b = run_backward(p_b, rows, w_b, h_b, pre_b, from_final=True)
    rows = hop(rows)
    rows, g_b = run_backward(q_b, rows, w_b, h_b, pre_b, held=g_b)
    rows, g_a = run_backward(q_a, rows, w_a, h_a, pre_a)
    rows = hop(rows)
    rows, g_a = run_backward(p_a, rows, w_a, h_a, pre_a, held=g_a, last=True)
    place = zh.astype(jnp.int32)[None]
    far_b = spread(g_b)
    g_a, far_b = lax.optimization_barrier((g_a, far_b))
    far_a = spread(g_a)
    sum_b = summed_over_zh(place, far_b, act_all, SET)
    sum_a = summed_over_zh(place, far_a, act_all, 0)
    kept = jnp.where(low_half, sum_a, sum_b)
    other = jnp.where(low_half, sum_b, sum_a)
    received = lax.ppermute(other, "y", [(0, 3), (3, 0), (1, 2), (2, 1)])
    return (kept.astype(jnp.float32) + received.astype(jnp.float32))[None]


def solution(mesh):
    fine = Mesh(mesh.devices.reshape(4, 4, 2, 4, 2), GRID_AXES)
    section = ("y", "zh")
    placed = (
        P(DP, None, None),
        P(DP, None, None),
        P(section, None, None, None),
        P(section, None, None, None),
    )
    return jax.shard_map(
        shards, mesh=fine, in_specs=placed, out_specs=P(section, DP, None), check_vma=False
    )
```

```python
import jax
import jax.numpy as jnp
from jax import lax
from jax.experimental import pallas as pl
from jax.experimental.pallas import tpu as pltpu
from jax.sharding import Mesh, PartitionSpec as P

EPS = 1e-06
COT = 0.0625
D, R = 5120, 256
REAL, ROWS = 18, 24
SET = 4
CH = 4
CW = D // CH
DP = ("zl", "x", "core")
GRID_AXES = ("y", "zh", "zl", "x", "core")
ANY = pl.BlockSpec(memory_space=pl.ANY)
VM = pl.BlockSpec(memory_space=pltpu.VMEM)
SM = pl.BlockSpec(memory_space=pltpu.SMEM)


class Scattered:
    count = 20

    def __init__(self, refs, flags, wbuf, sem):
        self.own, self.halves, self.parts = refs[:2], refs[2:4], refs[4:]
        self.flags, self.wbuf, self.sem = flags, wbuf, sem

    def fetch(self, layer, slot):
        flags = self.flags
        held = jnp.where(flags[1] == 1, SET - 1 - layer, layer)
        zh = flags[3]
        away = lax.rem(held + SET - zh, SET)
        mirrored = held == SET - 1 - zh

        @pl.when(away == 0)
        def _():
            for which in range(2):
                pltpu.make_async_copy(
                    self.own[which].at[flags[2]], self.wbuf.at[slot, :, which], self.sem.at[slot, 0]
                ).start()

        @pl.when(mirrored)
        def _():
            for n in range(2):
                half = lax.rem(flags[6] + n, 2)
                for which in range(2):
                    pltpu.make_async_copy(
                        self.halves[n].at[which],
                        self.wbuf.at[slot, pl.ds(half * 8, 8), which],
                        self.sem.at[slot, 0],
                    ).start()

        @pl.when((away > 0) & jnp.logical_not(mirrored))
        def _():
            entry = jnp.where(away == 2, 1, 0)
            for n in range(16):
                zl_off, x_off, core_off = n // 8, (n // 2) % 4, n % 2
                zl = lax.rem(flags[4] + zl_off, 2)
                x = lax.rem(flags[5] + x_off, 4)
                core = lax.rem(flags[6] + core_off, 2)
                pltpu.make_async_copy(
                    self.parts[n].at[entry],
                    self.wbuf.at[slot, zl * 8 + x * 2 + core],
                    self.sem.at[slot, 0],
                ).start()

    def first(self, layer, order):
        self.leading = order[0]
        self.fetch(layer, 0)

    def begin(self, layer, slot):
        self.fetch(layer, slot)

    def arrive(self, layer, slot, which):
        if which == self.leading:
            pltpu.make_async_copy(
                self.wbuf.at[1 - slot], self.wbuf.at[slot], self.sem.at[slot, 0]
            ).wait()


def chunk(wbuf, slot, which, c):
    per = 16 // CH
    return wbuf[slot, c * per : (c + 1) * per, which].reshape(CW, R)


def columns(c):
    return slice(c * CW, (c + 1) * CW)


def inverse_rms(hbuf, layer):
    total = jnp.zeros((ROWS, 1), jnp.float32)
    for c in range(CH):
        v = hbuf[layer, :, columns(c)].astype(jnp.float32)
        total = total + jnp.sum(v * v, axis=-1, keepdims=True)
    return lax.rsqrt(total * (1.0 / D) + EPS)


def forward_kernel(*refs, source, aliased):
    flags, x_ref = refs[:2]
    w_refs = refs[2 : 2 + source.count]
    refs = refs[2 + source.count + (3 if aliased else 0) :]
    y_ref, h_out, pre_out, act_out = refs[:4]
    wbuf, hbuf, prebuf, actbuf, sem_w, sem_h, sem_p, sem_a = refs[4:]

    @pl.when(flags[0] == 1)
    def _():
        weights = source(w_refs, flags, wbuf, sem_w)
        weights.first(0, (0, 1))
        hbuf[0] = x_ref[...]

        def step(layer, carry):
            slot = lax.rem(layer, 2)


            @pl.when(layer + 1 < SET)
            def _():
                weights.begin(layer + 1, 1 - slot)

            pltpu.make_async_copy(hbuf.at[layer], h_out.at[layer], sem_h.at[layer]).start()
            inv = inverse_rms(hbuf, layer)
            pre = jnp.zeros((ROWS, R), jnp.float32)
            weights.arrive(layer, slot, 0)
            for c in range(CH):
                normed = (hbuf[layer, :, columns(c)].astype(jnp.float32) * inv).astype(jnp.bfloat16)
                pre = pre + jnp.dot(
                    normed, chunk(wbuf, slot, 0, c), preferred_element_type=jnp.float32
                )
            active = (pre / (1.0 + jnp.exp(-pre))).astype(jnp.bfloat16)
            prebuf[layer] = pre
            actbuf[layer] = active
            weights.arrive(layer, slot, 1)
            for c in range(CH):
                branch = lax.dot_general(
                    active,
                    chunk(wbuf, slot, 1, c),
                    (((1,), (1,)), ((), ())),
                    preferred_element_type=jnp.float32,
                )
                before = hbuf[layer, :, columns(c)].astype(jnp.float32)
                hbuf[layer + 1, :, columns(c)] = (before + branch).astype(jnp.bfloat16)
            return carry

        lax.fori_loop(0, SET, step, 0)
        y_ref[...] = hbuf[SET]
        copies = [
            pltpu.make_async_copy(prebuf, pre_out, sem_p.at[0]),
            pltpu.make_async_copy(actbuf, act_out, sem_a.at[0]),
        ]
        for one in copies:
            one.start()
        for layer in range(SET):
            copies.append(
                pltpu.make_async_copy(hbuf.at[layer], h_out.at[layer], sem_h.at[layer])
            )
        for one in copies:
            one.wait()


def run_forward(flags, rows, weights, held=None):
    source = Scattered
    first = 2 + source.count
    outs = (
        jax.ShapeDtypeStruct((ROWS, D), jnp.bfloat16),
        jax.ShapeDtypeStruct((SET, ROWS, D), jnp.bfloat16),
        jax.ShapeDtypeStruct((SET, ROWS, R), jnp.float32),
        jax.ShapeDtypeStruct((SET, ROWS, R), jnp.bfloat16),
    )
    aliased = held is not None
    return pl.pallas_call(
        lambda *refs: forward_kernel(*refs, source=source, aliased=aliased),
        out_shape=outs,
        in_specs=[SM, VM] + [ANY] * (source.count + (3 if aliased else 0)),
        out_specs=(VM, ANY, ANY, ANY),
        scratch_shapes=[
            pltpu.VMEM((2, 16, 2, D // 16, R), jnp.bfloat16),
            pltpu.VMEM((SET + 1, ROWS, D), jnp.bfloat16),
            pltpu.VMEM((SET, ROWS, R), jnp.float32),
            pltpu.VMEM((SET, ROWS, R), jnp.bfloat16),
            pltpu.SemaphoreType.DMA((2, 2)),
            pltpu.SemaphoreType.DMA((SET,)),
            pltpu.SemaphoreType.DMA((1,)),
            pltpu.SemaphoreType.DMA((1,)),
        ],
        input_output_aliases={first: 1, first + 1: 2, first + 2: 3} if aliased else {},
        compiler_params=pltpu.CompilerParams(vmem_limit_bytes=52 * 2**20),
        cost_estimate=pl.CostEstimate(
            flops=SET * ROWS * D * R, bytes_accessed=SET * D * R, transcendentals=0
        ),
        name="forward_set",
    )(flags, rows, *weights, *(held or ()))


def backward_kernel(*refs, source, aliased, from_final, last):
    flags, g_ref, h_in, pre_in = refs[:4]
    w_refs = refs[4 : 4 + source.count]
    refs = refs[4 + source.count + (1 if aliased else 0) :]
    y_ref, g_out = refs[:2]
    wbuf, hbuf, prebuf, gbuf, dnbuf, gcut, sem_w, sem_h, sem_p, sem_g = refs[2:]

    @pl.when(flags[0] == 1)
    def _():
        weights = source(w_refs, flags, wbuf, sem_w)

        def g_copy(step):
            return pltpu.make_async_copy(
                gcut.at[:, step], g_out.at[:, SET - 1 - step], sem_g.at[step]
            )

        def g_send(step):
            for r in range(16):
                gcut[r, step] = gbuf[step, :, r * (D // 16) : (r + 1) * (D // 16)]
            g_copy(step).start()

        def h_copy(layer):
            return pltpu.make_async_copy(h_in.at[layer], hbuf.at[layer], sem_h.at[layer])

        pre_copy = pltpu.make_async_copy(pre_in, prebuf, sem_p.at[0])
        pre_copy.start()
        h_copy(SET - 1).start()
        weights.first(SET - 1, (1, 0))
        for layer in range(SET - 2, -1, -1):
            h_copy(layer).start()
        if from_final:
            gbuf[0] = (g_ref[...].astype(jnp.float32) * COT).astype(jnp.bfloat16)
        else:
            gbuf[0] = g_ref[...]
        pre_copy.wait()
        steps = SET - 1 if last else SET

        def one_layer(step, carry):
            layer = SET - 1 - step
            slot = lax.rem(step, 2)


            @pl.when(step + 1 < steps)
            def _():
                weights.begin(layer - 1, 1 - slot)

            g_send(step)
            h_copy(layer).wait()
            inv = inverse_rms(hbuf, layer)
            pre = prebuf[layer]
            sigma = 1.0 / (1.0 + jnp.exp(-pre))
            slope = sigma * (1.0 + pre * (1.0 - sigma))
            d_active = jnp.zeros((ROWS, R), jnp.float32)
            weights.arrive(layer, slot, 1)
            for c in range(CH):
                d_active = d_active + jnp.dot(
                    gbuf[step, :, columns(c)],
                    chunk(wbuf, slot, 1, c),
                    preferred_element_type=jnp.float32,
                )
            d_pre = (d_active * slope).astype(jnp.bfloat16)
            total = jnp.zeros((ROWS, 1), jnp.float32)
            weights.arrive(layer, slot, 0)
            for c in range(CH):
                d_normed = lax.dot_general(
                    d_pre,
                    chunk(wbuf, slot, 0, c),
                    (((1,), (1,)), ((), ())),
                    preferred_element_type=jnp.float32,
                )
                unit = hbuf[layer, :, columns(c)].astype(jnp.float32) * inv
                total = total + jnp.sum(d_normed * unit, axis=-1, keepdims=True)
                dnbuf[:, columns(c)] = d_normed
            mean = total * (1.0 / D)
            for c in range(CH):
                unit = hbuf[layer, :, columns(c)].astype(jnp.float32) * inv
                moved = inv * (dnbuf[:, columns(c)] - unit * mean)
                before = gbuf[step, :, columns(c)].astype(jnp.float32)
                gbuf[step + 1, :, columns(c)] = (before + moved).astype(jnp.bfloat16)
            return carry

        lax.fori_loop(0, steps, one_layer, 0)
        if last:
            g_send(SET - 1)
            h_copy(0).wait()
        y_ref[...] = gbuf[steps]
        for step in range(SET):
            g_copy(step).wait()


def run_backward(flags, g_rows, weights, h_held, pre_held, held=None, from_final=False, last=False):
    source = Scattered
    outs = (
        jax.ShapeDtypeStruct((ROWS, D), jnp.bfloat16),
        jax.ShapeDtypeStruct((16, SET, ROWS, D // 16), jnp.bfloat16),
    )
    aliased = held is not None
    return pl.pallas_call(
        lambda *refs: backward_kernel(
            *refs, source=source, aliased=aliased, from_final=from_final, last=last
        ),
        out_shape=outs,
        in_specs=[SM, VM, ANY, ANY] + [ANY] * (source.count + (1 if aliased else 0)),
        out_specs=(VM, ANY),
        scratch_shapes=[
            pltpu.VMEM((2, 16, 2, D // 16, R), jnp.bfloat16),
            pltpu.VMEM((SET, ROWS, D), jnp.bfloat16),
            pltpu.VMEM((SET, ROWS, R), jnp.float32),
            pltpu.VMEM((SET + 1, ROWS, D), jnp.bfloat16),
            pltpu.VMEM((ROWS, D), jnp.float32),
            pltpu.VMEM((16, SET, ROWS, D // 16), jnp.bfloat16),
            pltpu.SemaphoreType.DMA((2, 2)),
            pltpu.SemaphoreType.DMA((SET,)),
            pltpu.SemaphoreType.DMA((1,)),
            pltpu.SemaphoreType.DMA((SET,)),
        ],
        input_output_aliases={4 + source.count: 1} if aliased else {},
        compiler_params=pltpu.CompilerParams(vmem_limit_bytes=52 * 2**20),
        cost_estimate=pl.CostEstimate(
            flops=SET * ROWS * D * R, bytes_accessed=SET * D * R, transcendentals=0
        ),
        name="backward_set",
    )(flags, g_rows, h_held, pre_held, *weights, *((held,) if aliased else ()))


def grad_kernel(place, g_ref, act_ref, *out_refs, first):
    for k in range(SET):
        layer = lax.rem(place[0] + k, SET)
        g = g_ref[:, layer].reshape(16 * ROWS, D // 16)
        act = act_ref[:, first + layer].reshape(16 * ROWS, R)
        out_refs[k][...] = lax.dot_general(
            g, act, (((0,), (0,)), ((), ())), preferred_element_type=jnp.float32
        ).astype(jnp.bfloat16)


def run_grad(place, g_all, act_all, first):
    return pl.pallas_call(
        lambda *refs: grad_kernel(*refs, first=first),
        out_shape=(jax.ShapeDtypeStruct((D // 16, R), jnp.bfloat16),) * SET,
        in_specs=[SM, VM, VM],
        out_specs=(VM,) * SET,
        compiler_params=pltpu.CompilerParams(vmem_limit_bytes=52 * 2**20),
        name="grad_set",
    )(place, g_all, act_all)


def summed_over_zh(place, g_all, act_all, first):
    parts = run_grad(place, g_all, act_all, first)
    total = parts[0].astype(jnp.float32)
    for k in range(1, SET):
        route = [(source, (source + k) % SET) for source in range(SET)]
        total = total + lax.ppermute(parts[k], "zh", route).astype(jnp.float32)
    return total.astype(jnp.bfloat16)


def hop(rows):
    return lax.ppermute(rows, "y", [(0, 1), (1, 0), (2, 3), (3, 2)])


def spread(g_set):
    return lax.all_to_all(g_set, DP, 0, 0)


def from_ring(block, axis, away):
    count = lax.axis_size(axis)
    return lax.ppermute(block, axis, [((d + away) % count, d) for d in range(count)])


def across_y(block):
    return lax.ppermute(block, "y", [(0, 3), (3, 0), (1, 2), (2, 1)])


def over_z(chunk_now):
    beside = lax.ppermute(chunk_now, "zh", [(0, 1), (1, 0), (2, 3), (3, 2)])
    return jnp.stack([beside, from_ring(chunk_now, "zh", 2)])


def over_x_first(near):
    far = from_ring(near, "zl", 1)
    return near, from_ring(near, "x", 1), from_ring(near, "x", -1), far


def over_x_rest(near, near_up, near_down, far):
    near_across = from_ring(near_up, "x", 1)
    far_up, far_down = from_ring(far, "x", 1), from_ring(far, "x", -1)
    far_across = from_ring(far_down, "x", -1)
    parts = []
    for one in (near, near_up, near_across, near_down, far, far_up, far_across, far_down):
        parts += [one, from_ring(one, "core", 1)]
    return tuple(parts)


def shards(inputs_down, inputs_up, w_in, w_out):
    y, zh, dp = lax.axis_index("y"), lax.axis_index("zh"), lax.axis_index(DP)
    low_half = y < 2
    stage_p = (y == 0) | (y == 3)

    def own(layer_slot):
        parts = [
            lax.dynamic_slice(w, (0, layer_slot, dp * (D // 16), 0), (1, 1, D // 16, R))[0, 0]
            for w in (w_in, w_out)
        ]
        return jnp.stack(parts)

    def own_half(layer_slot):
        core = lax.axis_index("core")
        parts = [
            lax.dynamic_slice(w, (0, layer_slot, core * (D // 2), 0), (1, 1, D // 2, R))[0, 0]
            for w in (w_in, w_out)
        ]
        return jnp.stack(parts).reshape(2, 8, D // 16, R)

    first_slot = jnp.where(low_half, 0, 1)
    own_layers = tuple(w[0].reshape(2, 16, D // 16, R) for w in (w_in, w_out))
    half_a = across_y(own_half(first_slot))
    near_a = over_z(own(first_slot))
    chunk_b, near_a = lax.optimization_barrier((own(1 - first_slot), near_a))
    step_a = over_x_first(near_a)
    near_b = over_z(chunk_b)
    near_b, step_a = lax.optimization_barrier((near_b, step_a))
    rest_a = over_x_rest(*step_a)
    half_b, half_a = lax.optimization_barrier((own_half(1 - first_slot), half_a))
    half_b = across_y(half_b)
    w_a = own_layers + (half_a, from_ring(half_a, "core", 1)) + rest_a
    rest_b = over_x_rest(*over_x_first(near_b))
    w_b = own_layers + (half_b, from_ring(half_b, "core", 1)) + rest_b

    def flag(active, slot_now):
        reverse = slot_now == 1
        here = [lax.axis_index(name) for name in ("zh",) + DP]
        return jnp.stack([v.astype(jnp.int32) for v in [active, reverse, slot_now] + here])

    p_a, p_b = flag(stage_p, first_slot), flag(stage_p, 1 - first_slot)
    q_a, q_b = flag(~stage_p, first_slot), flag(~stage_p, 1 - first_slot)

    mine = jnp.where(low_half, inputs_down, inputs_up).reshape(-1, D)
    mine = lax.dynamic_slice(mine, (zh * REAL, 0), (REAL, D))
    rows = jnp.pad(mine, ((0, ROWS - REAL), (0, 0)))

    rows, h_a, pre_a, act_a = run_forward(p_a, rows, w_a)
    rows = hop(rows)
    rows, h_a, pre_a, act_a = run_forward(q_a, rows, w_a, (h_a, pre_a, act_a))
    rows, h_b, pre_b, act_b = run_forward(q_b, rows, w_b)
    rows = hop(rows)
    rows, h_b, pre_b, act_b = run_forward(p_b, rows, w_b, (h_b, pre_b, act_b))
    act_all = lax.all_gather(jnp.concatenate([act_a, act_b], axis=0), DP)
    rows, g_b = run_backward(p_b, rows, w_b, h_b, pre_b, from_final=True)
    rows = hop(rows)
    rows, g_b = run_backward(q_b, rows, w_b, h_b, pre_b, held=g_b)
    rows, g_a = run_backward(q_a, rows, w_a, h_a, pre_a)
    rows = hop(rows)
    rows, g_a = run_backward(p_a, rows, w_a, h_a, pre_a, held=g_a, last=True)
    place = zh.astype(jnp.int32)[None]
    far_b = spread(g_b)
    g_a, far_b = lax.optimization_barrier((g_a, far_b))
    far_a = spread(g_a)
    sum_b = summed_over_zh(place, far_b, act_all, SET)
    sum_a = summed_over_zh(place, far_a, act_all, 0)
    kept = jnp.where(low_half, sum_a, sum_b)
    other = jnp.where(low_half, sum_b, sum_a)
    received = across_y(other)
    return (kept.astype(jnp.float32) + received.astype(jnp.float32))[None]


def solution(mesh):
    fine = Mesh(mesh.devices.reshape(4, 4, 2, 4, 2), GRID_AXES)
    section = ("y", "zh")
    placed = (
        P(DP, None, None),
        P(DP, None, None),
        P(section, None, None, None),
        P(section, None, None, None),
    )
    return jax.shard_map(
        shards, mesh=fine, in_specs=placed, out_specs=P(section, DP, None), check_vma=False
    )
```

```python
import jax
import jax.numpy as jnp
from jax import lax
from jax.experimental import pallas as pl
from jax.experimental.pallas import tpu as pltpu
from jax.sharding import Mesh, PartitionSpec as P

EPS = 1e-06
COT = 0.0625
D, R = 5120, 256
REAL, ROWS = 18, 24
SET = 4
CH = 4
CW = D // CH
DP = ("zl", "x", "core")
GRID_AXES = ("y", "zh", "zl", "x", "core")
ANY = pl.BlockSpec(memory_space=pl.ANY)
VM = pl.BlockSpec(memory_space=pltpu.VMEM)
SM = pl.BlockSpec(memory_space=pltpu.SMEM)


class Gathered:
    count = 1

    def __init__(self, refs, flags, wbuf, sem):
        self.w, self.flags, self.wbuf, self.sem = refs[0], flags, wbuf, sem

    def copy(self, layer, slot, which):
        held = jnp.where(self.flags[1] == 1, SET - 1 - layer, layer)
        return pltpu.make_async_copy(
            self.w.at[held, :, which], self.wbuf.at[slot, :, which], self.sem.at[slot, which]
        )

    def first(self, layer, order):
        self.order = order
        self.begin(layer, 0)

    def begin(self, layer, slot):
        for which in self.order:
            self.copy(layer, slot, which).start()

    def arrive(self, layer, slot, which):
        self.copy(layer, slot, which).wait()


class Scattered:
    count = 20

    def __init__(self, refs, flags, wbuf, sem):
        self.own, self.halves, self.parts = refs[:2], refs[2:4], refs[4:]
        self.flags, self.wbuf, self.sem = flags, wbuf, sem

    def fetch(self, layer, slot):
        flags = self.flags
        held = jnp.where(flags[1] == 1, SET - 1 - layer, layer)
        zh = flags[3]
        away = lax.rem(held + SET - zh, SET)
        mirrored = held == SET - 1 - zh

        @pl.when(away == 0)
        def _():
            for which in range(2):
                pltpu.make_async_copy(
                    self.own[which].at[flags[2]], self.wbuf.at[slot, :, which], self.sem.at[slot, 0]
                ).start()

        @pl.when(mirrored)
        def _():
            for n in range(2):
                half = lax.rem(flags[6] + n, 2)
                for which in range(2):
                    pltpu.make_async_copy(
                        self.halves[n].at[which],
                        self.wbuf.at[slot, pl.ds(half * 8, 8), which],
                        self.sem.at[slot, 0],
                    ).start()

        @pl.when((away > 0) & jnp.logical_not(mirrored))
        def _():
            entry = jnp.where(away == 2, 1, 0)
            for n in range(16):
                zl_off, x_off, core_off = n // 8, (n // 2) % 4, n % 2
                zl = lax.rem(flags[4] + zl_off, 2)
                x = lax.rem(flags[5] + x_off, 4)
                core = lax.rem(flags[6] + core_off, 2)
                pltpu.make_async_copy(
                    self.parts[n].at[entry],
                    self.wbuf.at[slot, zl * 8 + x * 2 + core],
                    self.sem.at[slot, 0],
                ).start()

    def first(self, layer, order):
        self.leading = order[0]
        self.fetch(layer, 0)

    def begin(self, layer, slot):
        self.fetch(layer, slot)

    def arrive(self, layer, slot, which):
        if which == self.leading:
            pltpu.make_async_copy(
                self.wbuf.at[1 - slot], self.wbuf.at[slot], self.sem.at[slot, 0]
            ).wait()


def chunk(wbuf, slot, which, c):
    per = 16 // CH
    return wbuf[slot, c * per : (c + 1) * per, which].reshape(CW, R)


def columns(c):
    return slice(c * CW, (c + 1) * CW)


def inverse_rms(hbuf, layer):
    total = jnp.zeros((ROWS, 1), jnp.float32)
    for c in range(CH):
        v = hbuf[layer, :, columns(c)].astype(jnp.float32)
        total = total + jnp.sum(v * v, axis=-1, keepdims=True)
    return lax.rsqrt(total * (1.0 / D) + EPS)


def forward_kernel(*refs, source, aliased):
    flags, x_ref = refs[:2]
    w_refs = refs[2 : 2 + source.count]
    refs = refs[2 + source.count + (3 if aliased else 0) :]
    y_ref, h_out, pre_out, act_out = refs[:4]
    wbuf, hbuf, prebuf, actbuf, sem_w, sem_h, sem_p, sem_a = refs[4:]

    @pl.when(flags[0] == 1)
    def _():
        weights = source(w_refs, flags, wbuf, sem_w)
        weights.first(0, (0, 1))
        hbuf[0] = x_ref[...]

        def step(layer, carry):
            slot = lax.rem(layer, 2)


            @pl.when(layer + 1 < SET)
            def _():
                weights.begin(layer + 1, 1 - slot)

            pltpu.make_async_copy(hbuf.at[layer], h_out.at[layer], sem_h.at[layer]).start()
            inv = inverse_rms(hbuf, layer)
            pre = jnp.zeros((ROWS, R), jnp.float32)
            weights.arrive(layer, slot, 0)
            for c in range(CH):
                normed = (hbuf[layer, :, columns(c)].astype(jnp.float32) * inv).astype(jnp.bfloat16)
                pre = pre + jnp.dot(
                    normed, chunk(wbuf, slot, 0, c), preferred_element_type=jnp.float32
                )
            active = (pre / (1.0 + jnp.exp(-pre))).astype(jnp.bfloat16)
            prebuf[layer] = pre
            actbuf[layer] = active
            weights.arrive(layer, slot, 1)
            for c in range(CH):
                branch = lax.dot_general(
                    active,
                    chunk(wbuf, slot, 1, c),
                    (((1,), (1,)), ((), ())),
                    preferred_element_type=jnp.float32,
                )
                before = hbuf[layer, :, columns(c)].astype(jnp.float32)
                hbuf[layer + 1, :, columns(c)] = (before + branch).astype(jnp.bfloat16)
            return carry

        lax.fori_loop(0, SET, step, 0)
        y_ref[...] = hbuf[SET]
        copies = [
            pltpu.make_async_copy(prebuf, pre_out, sem_p.at[0]),
            pltpu.make_async_copy(actbuf, act_out, sem_a.at[0]),
        ]
        for one in copies:
            one.start()
        for layer in range(SET):
            copies.append(
                pltpu.make_async_copy(hbuf.at[layer], h_out.at[layer], sem_h.at[layer])
            )
        for one in copies:
            one.wait()


def run_forward(flags, rows, weights, held=None):
    source = Gathered if len(weights) == 1 else Scattered
    first = 2 + source.count
    outs = (
        jax.ShapeDtypeStruct((ROWS, D), jnp.bfloat16),
        jax.ShapeDtypeStruct((SET, ROWS, D), jnp.bfloat16),
        jax.ShapeDtypeStruct((SET, ROWS, R), jnp.float32),
        jax.ShapeDtypeStruct((SET, ROWS, R), jnp.bfloat16),
    )
    aliased = held is not None
    return pl.pallas_call(
        lambda *refs: forward_kernel(*refs, source=source, aliased=aliased),
        out_shape=outs,
        in_specs=[SM, VM] + [ANY] * (source.count + (3 if aliased else 0)),
        out_specs=(VM, ANY, ANY, ANY),
        scratch_shapes=[
            pltpu.VMEM((2, 16, 2, D // 16, R), jnp.bfloat16),
            pltpu.VMEM((SET + 1, ROWS, D), jnp.bfloat16),
            pltpu.VMEM((SET, ROWS, R), jnp.float32),
            pltpu.VMEM((SET, ROWS, R), jnp.bfloat16),
            pltpu.SemaphoreType.DMA((2, 2)),
            pltpu.SemaphoreType.DMA((SET,)),
            pltpu.SemaphoreType.DMA((1,)),
            pltpu.SemaphoreType.DMA((1,)),
        ],
        input_output_aliases={first: 1, first + 1: 2, first + 2: 3} if aliased else {},
        compiler_params=pltpu.CompilerParams(vmem_limit_bytes=52 * 2**20),
        cost_estimate=pl.CostEstimate(
            flops=SET * ROWS * D * R, bytes_accessed=SET * D * R, transcendentals=0
        ),
        name="forward_set",
    )(flags, rows, *weights, *(held or ()))


def backward_kernel(*refs, source, aliased, from_final, last):
    flags, g_ref, h_in, pre_in = refs[:4]
    w_refs = refs[4 : 4 + source.count]
    refs = refs[4 + source.count + (1 if aliased else 0) :]
    y_ref, g_out = refs[:2]
    wbuf, hbuf, prebuf, gbuf, dnbuf, gcut, sem_w, sem_h, sem_p, sem_g = refs[2:]

    @pl.when(flags[0] == 1)
    def _():
        weights = source(w_refs, flags, wbuf, sem_w)

        def g_copy(step):
            return pltpu.make_async_copy(
                gcut.at[:, step], g_out.at[:, SET - 1 - step], sem_g.at[step]
            )

        def g_send(step):
            for r in range(16):
                gcut[r, step] = gbuf[step, :, r * (D // 16) : (r + 1) * (D // 16)]
            g_copy(step).start()

        def h_copy(layer):
            return pltpu.make_async_copy(h_in.at[layer], hbuf.at[layer], sem_h.at[layer])

        pre_copy = pltpu.make_async_copy(pre_in, prebuf, sem_p.at[0])
        pre_copy.start()
        h_copy(SET - 1).start()
        weights.first(SET - 1, (1, 0))
        for layer in range(SET - 2, -1, -1):
            h_copy(layer).start()
        if from_final:
            gbuf[0] = (g_ref[...].astype(jnp.float32) * COT).astype(jnp.bfloat16)
        else:
            gbuf[0] = g_ref[...]
        pre_copy.wait()
        steps = SET - 1 if last else SET

        def one_layer(step, carry):
            layer = SET - 1 - step
            slot = lax.rem(step, 2)


            @pl.when(step + 1 < steps)
            def _():
                weights.begin(layer - 1, 1 - slot)

            g_send(step)
            h_copy(layer).wait()
            inv = inverse_rms(hbuf, layer)
            pre = prebuf[layer]
            sigma = 1.0 / (1.0 + jnp.exp(-pre))
            slope = sigma * (1.0 + pre * (1.0 - sigma))
            d_active = jnp.zeros((ROWS, R), jnp.float32)
            weights.arrive(layer, slot, 1)
            for c in range(CH):
                d_active = d_active + jnp.dot(
                    gbuf[step, :, columns(c)],
                    chunk(wbuf, slot, 1, c),
                    preferred_element_type=jnp.float32,
                )
            d_pre = (d_active * slope).astype(jnp.bfloat16)
            total = jnp.zeros((ROWS, 1), jnp.float32)
            weights.arrive(layer, slot, 0)
            for c in range(CH):
                d_normed = lax.dot_general(
                    d_pre,
                    chunk(wbuf, slot, 0, c),
                    (((1,), (1,)), ((), ())),
                    preferred_element_type=jnp.float32,
                )
                unit = hbuf[layer, :, columns(c)].astype(jnp.float32) * inv
                total = total + jnp.sum(d_normed * unit, axis=-1, keepdims=True)
                dnbuf[:, columns(c)] = d_normed
            mean = total * (1.0 / D)
            for c in range(CH):
                unit = hbuf[layer, :, columns(c)].astype(jnp.float32) * inv
                moved = inv * (dnbuf[:, columns(c)] - unit * mean)
                before = gbuf[step, :, columns(c)].astype(jnp.float32)
                gbuf[step + 1, :, columns(c)] = (before + moved).astype(jnp.bfloat16)
            return carry

        lax.fori_loop(0, steps, one_layer, 0)
        if last:
            g_send(SET - 1)
            h_copy(0).wait()
        y_ref[...] = gbuf[steps]
        for step in range(SET):
            g_copy(step).wait()


def run_backward(flags, g_rows, weights, h_held, pre_held, held=None, from_final=False, last=False):
    source = Gathered if len(weights) == 1 else Scattered
    outs = (
        jax.ShapeDtypeStruct((ROWS, D), jnp.bfloat16),
        jax.ShapeDtypeStruct((16, SET, ROWS, D // 16), jnp.bfloat16),
    )
    aliased = held is not None
    return pl.pallas_call(
        lambda *refs: backward_kernel(
            *refs, source=source, aliased=aliased, from_final=from_final, last=last
        ),
        out_shape=outs,
        in_specs=[SM, VM, ANY, ANY] + [ANY] * (source.count + (1 if aliased else 0)),
        out_specs=(VM, ANY),
        scratch_shapes=[
            pltpu.VMEM((2, 16, 2, D // 16, R), jnp.bfloat16),
            pltpu.VMEM((SET, ROWS, D), jnp.bfloat16),
            pltpu.VMEM((SET, ROWS, R), jnp.float32),
            pltpu.VMEM((SET + 1, ROWS, D), jnp.bfloat16),
            pltpu.VMEM((ROWS, D), jnp.float32),
            pltpu.VMEM((16, SET, ROWS, D // 16), jnp.bfloat16),
            pltpu.SemaphoreType.DMA((2, 2)),
            pltpu.SemaphoreType.DMA((SET,)),
            pltpu.SemaphoreType.DMA((1,)),
            pltpu.SemaphoreType.DMA((SET,)),
        ],
        input_output_aliases={4 + source.count: 1} if aliased else {},
        compiler_params=pltpu.CompilerParams(vmem_limit_bytes=52 * 2**20),
        cost_estimate=pl.CostEstimate(
            flops=SET * ROWS * D * R, bytes_accessed=SET * D * R, transcendentals=0
        ),
        name="backward_set",
    )(flags, g_rows, h_held, pre_held, *weights, *((held,) if aliased else ()))


def grad_kernel(place, g_ref, act_ref, *out_refs, first):
    for k in range(SET):
        layer = lax.rem(place[0] + k, SET)
        g = g_ref[:, layer].reshape(16 * ROWS, D // 16)
        act = act_ref[:, first + layer].reshape(16 * ROWS, R)
        out_refs[k][...] = lax.dot_general(
            g, act, (((0,), (0,)), ((), ())), preferred_element_type=jnp.float32
        ).astype(jnp.bfloat16)


def run_grad(place, g_all, act_all, first):
    return pl.pallas_call(
        lambda *refs: grad_kernel(*refs, first=first),
        out_shape=(jax.ShapeDtypeStruct((D // 16, R), jnp.bfloat16),) * SET,
        in_specs=[SM, VM, VM],
        out_specs=(VM,) * SET,
        compiler_params=pltpu.CompilerParams(vmem_limit_bytes=52 * 2**20),
        name="grad_set",
    )(place, g_all, act_all)


def summed_over_zh(place, g_all, act_all, first):
    parts = run_grad(place, g_all, act_all, first)
    total = parts[0].astype(jnp.float32)
    for k in range(1, SET):
        route = [(source, (source + k) % SET) for source in range(SET)]
        total = total + lax.ppermute(parts[k], "zh", route).astype(jnp.float32)
    return total.astype(jnp.bfloat16)


def hop(rows):
    return lax.ppermute(rows, "y", [(0, 1), (1, 0), (2, 3), (3, 2)])


def spread(g_set):
    return lax.all_to_all(g_set, DP, 0, 0)


def from_ring(block, axis, away):
    count = lax.axis_size(axis)
    return lax.ppermute(block, axis, [((d + away) % count, d) for d in range(count)])


def across_y(block):
    return lax.ppermute(block, "y", [(0, 3), (3, 0), (1, 2), (2, 1)])


def over_z(chunk_now):
    beside = lax.ppermute(chunk_now, "zh", [(0, 1), (1, 0), (2, 3), (3, 2)])
    route = []
    for y in range(4):
        for zh in range(4):
            route.append((y * 4 + zh, (3 - y) * 4 + (zh ^ 1)))
    return jnp.stack([beside, lax.ppermute(chunk_now, ("y", "zh"), route)])


def over_x(near):
    far = from_ring(near, "zl", 1)
    near_up, near_down = from_ring(near, "x", 1), from_ring(near, "x", -1)
    near_across = from_ring(near_up, "x", 1)
    far_up, far_down = from_ring(far, "x", 1), from_ring(far, "x", -1)
    far_across = from_ring(far_down, "x", -1)
    parts = []
    for one in (near, near_up, near_across, near_down, far, far_up, far_across, far_down):
        parts += [one, from_ring(one, "core", 1)]
    return tuple(parts)


def shards(inputs_down, inputs_up, w_in, w_out):
    y, zh, dp = lax.axis_index("y"), lax.axis_index("zh"), lax.axis_index(DP)
    low_half = y < 2
    stage_p = (y == 0) | (y == 3)

    def own(layer_slot):
        parts = [
            lax.dynamic_slice(w, (0, layer_slot, dp * (D // 16), 0), (1, 1, D // 16, R))[0, 0]
            for w in (w_in, w_out)
        ]
        return jnp.stack(parts)

    def gathered(own_part):
        return lax.all_gather(own_part, ("zh",) + DP).reshape(SET, 16, 2, D // 16, R)

    def own_half(layer_slot):
        core = lax.axis_index("core")
        parts = [
            lax.dynamic_slice(w, (0, layer_slot, core * (D // 2), 0), (1, 1, D // 2, R))[0, 0]
            for w in (w_in, w_out)
        ]
        return jnp.stack(parts).reshape(2, 8, D // 16, R)

    first_slot = jnp.where(low_half, 0, 1)
    own_layers = tuple(w[0].reshape(2, 16, D // 16, R) for w in (w_in, w_out))
    w_b = (gathered(own(1 - first_slot)),)
    half_a = across_y(own_half(first_slot))
    w_a = own_layers + (half_a, from_ring(half_a, "core", 1)) + over_x(over_z(own(first_slot)))

    def flag(active, slot_now):
        reverse = slot_now == 1
        here = [lax.axis_index(name) for name in ("zh",) + DP]
        return jnp.stack([v.astype(jnp.int32) for v in [active, reverse, slot_now] + here])

    p_a, p_b = flag(stage_p, first_slot), flag(stage_p, 1 - first_slot)
    q_a, q_b = flag(~stage_p, first_slot), flag(~stage_p, 1 - first_slot)

    mine = jnp.where(low_half, inputs_down, inputs_up).reshape(-1, D)
    mine = lax.dynamic_slice(mine, (zh * REAL, 0), (REAL, D))
    rows = jnp.pad(mine, ((0, ROWS - REAL), (0, 0)))

    rows, h_a, pre_a, act_a = run_forward(p_a, rows, w_a)
    rows = hop(rows)
    rows, h_a, pre_a, act_a = run_forward(q_a, rows, w_a, (h_a, pre_a, act_a))
    rows, h_b, pre_b, act_b = run_forward(q_b, rows, w_b)
    rows = hop(rows)
    rows, h_b, pre_b, act_b = run_forward(p_b, rows, w_b, (h_b, pre_b, act_b))
    act_all = lax.all_gather(jnp.concatenate([act_a, act_b], axis=0), DP)
    rows, g_b = run_backward(p_b, rows, w_b, h_b, pre_b, from_final=True)
    rows = hop(rows)
    rows, g_b = run_backward(q_b, rows, w_b, h_b, pre_b, held=g_b)
    rows, g_a = run_backward(q_a, rows, w_a, h_a, pre_a)
    rows, act_all = lax.optimization_barrier((rows, act_all))
    rows = hop(rows)
    rows, g_a = run_backward(p_a, rows, w_a, h_a, pre_a, held=g_a, last=True)
    place = zh.astype(jnp.int32)[None]
    far_b = spread(g_b)
    g_a, far_b = lax.optimization_barrier((g_a, far_b))
    far_a = spread(g_a)
    sum_b = summed_over_zh(place, far_b, act_all, SET)
    sum_a = summed_over_zh(place, far_a, act_all, 0)
    kept = jnp.where(low_half, sum_a, sum_b)
    other = jnp.where(low_half, sum_b, sum_a)
    received = across_y(other)
    return (kept.astype(jnp.float32) + received.astype(jnp.float32))[None]


def solution(mesh):
    fine = Mesh(mesh.devices.reshape(4, 4, 2, 4, 2), GRID_AXES)
    section = ("y", "zh")
    placed = (
        P(DP, None, None),
        P(DP, None, None),
        P(section, None, None, None),
        P(section, None, None, None),
    )
    return jax.shard_map(
        shards, mesh=fine, in_specs=placed, out_specs=P(section, DP, None), check_vma=False
    )
```

```python
import jax
import jax.numpy as jnp
from jax import lax
from jax.experimental import pallas as pl
from jax.experimental.pallas import tpu as pltpu
from jax.sharding import Mesh, PartitionSpec as P

EPS = 1e-06
COT = 0.0625
D, R = 5120, 256
REAL, ROWS = 18, 24
SET = 4
CH = 4
CW = D // CH
DP = ("zl", "x", "core")
GRID_AXES = ("y", "zh", "zl", "x", "core")
ANY = pl.BlockSpec(memory_space=pl.ANY)
VM = pl.BlockSpec(memory_space=pltpu.VMEM)
SM = pl.BlockSpec(memory_space=pltpu.SMEM)


class Scattered:
    count = 20

    def __init__(self, refs, flags, wbuf, sem):
        self.own, self.halves, self.parts = refs[:2], refs[2:4], refs[4:]
        self.flags, self.wbuf, self.sem = flags, wbuf, sem

    def fetch(self, layer, slot):
        flags = self.flags
        held = jnp.where(flags[1] == 1, SET - 1 - layer, layer)
        zh = flags[3]
        away = lax.rem(held + SET - zh, SET)
        mirrored = held == SET - 1 - zh

        @pl.when(away == 0)
        def _():
            for which in range(2):
                pltpu.make_async_copy(
                    self.own[which].at[flags[2]], self.wbuf.at[slot, :, which], self.sem.at[slot, 0]
                ).start()

        @pl.when(mirrored)
        def _():
            for n in range(2):
                half = lax.rem(flags[6] + n, 2)
                for which in range(2):
                    pltpu.make_async_copy(
                        self.halves[n].at[which],
                        self.wbuf.at[slot, pl.ds(half * 8, 8), which],
                        self.sem.at[slot, 0],
                    ).start()

        @pl.when((away > 0) & jnp.logical_not(mirrored))
        def _():
            entry = jnp.where(away == 2, 1, 0)
            for n in range(16):
                zl_off, x_off, core_off = n // 8, (n // 2) % 4, n % 2
                zl = lax.rem(flags[4] + zl_off, 2)
                x = lax.rem(flags[5] + x_off, 4)
                core = lax.rem(flags[6] + core_off, 2)
                pltpu.make_async_copy(
                    self.parts[n].at[entry],
                    self.wbuf.at[slot, zl * 8 + x * 2 + core],
                    self.sem.at[slot, 0],
                ).start()

    def first(self, layer, order):
        self.leading = order[0]
        self.fetch(layer, 0)

    def begin(self, layer, slot):
        self.fetch(layer, slot)

    def arrive(self, layer, slot, which):
        if which == self.leading:
            pltpu.make_async_copy(
                self.wbuf.at[1 - slot], self.wbuf.at[slot], self.sem.at[slot, 0]
            ).wait()


def chunk(wbuf, slot, which, c):
    per = 16 // CH
    return wbuf[slot, c * per : (c + 1) * per, which].reshape(CW, R)


def columns(c):
    return slice(c * CW, (c + 1) * CW)


def inverse_rms(hbuf, layer):
    total = jnp.zeros((ROWS, 1), jnp.float32)
    for c in range(CH):
        v = hbuf[layer, :, columns(c)].astype(jnp.float32)
        total = total + jnp.sum(v * v, axis=-1, keepdims=True)
    return lax.rsqrt(total * (1.0 / D) + EPS)


def forward_kernel(*refs, source, aliased):
    flags, x_ref = refs[:2]
    w_refs = refs[2 : 2 + source.count]
    refs = refs[2 + source.count + (3 if aliased else 0) :]
    y_ref, h_out, pre_out, act_out = refs[:4]
    wbuf, hbuf, prebuf, actbuf, sem_w, sem_h, sem_p, sem_a = refs[4:]

    @pl.when(flags[0] == 1)
    def _():
        weights = source(w_refs, flags, wbuf, sem_w)
        weights.first(0, (0, 1))
        hbuf[0] = x_ref[...]

        def step(layer, carry):
            slot = lax.rem(layer, 2)


            @pl.when(layer + 1 < SET)
            def _():
                weights.begin(layer + 1, 1 - slot)

            pltpu.make_async_copy(hbuf.at[layer], h_out.at[layer], sem_h.at[layer]).start()
            inv = inverse_rms(hbuf, layer)
            pre = jnp.zeros((ROWS, R), jnp.float32)
            weights.arrive(layer, slot, 0)
            for c in range(CH):
                normed = (hbuf[layer, :, columns(c)].astype(jnp.float32) * inv).astype(jnp.bfloat16)
                pre = pre + jnp.dot(
                    normed, chunk(wbuf, slot, 0, c), preferred_element_type=jnp.float32
                )
            active = (pre / (1.0 + jnp.exp(-pre))).astype(jnp.bfloat16)
            prebuf[layer] = pre
            actbuf[layer] = active
            weights.arrive(layer, slot, 1)
            for c in range(CH):
                branch = lax.dot_general(
                    active,
                    chunk(wbuf, slot, 1, c),
                    (((1,), (1,)), ((), ())),
                    preferred_element_type=jnp.float32,
                )
                before = hbuf[layer, :, columns(c)].astype(jnp.float32)
                hbuf[layer + 1, :, columns(c)] = (before + branch).astype(jnp.bfloat16)
            return carry

        lax.fori_loop(0, SET, step, 0)
        y_ref[...] = hbuf[SET]
        copies = [
            pltpu.make_async_copy(prebuf, pre_out, sem_p.at[0]),
            pltpu.make_async_copy(actbuf, act_out, sem_a.at[0]),
        ]
        for one in copies:
            one.start()
        for layer in range(SET):
            copies.append(
                pltpu.make_async_copy(hbuf.at[layer], h_out.at[layer], sem_h.at[layer])
            )
        for one in copies:
            one.wait()


def run_forward(flags, rows, weights, held=None):
    source = Scattered
    first = 2 + source.count
    outs = (
        jax.ShapeDtypeStruct((ROWS, D), jnp.bfloat16),
        jax.ShapeDtypeStruct((SET, ROWS, D), jnp.bfloat16),
        jax.ShapeDtypeStruct((SET, ROWS, R), jnp.float32),
        jax.ShapeDtypeStruct((SET, ROWS, R), jnp.bfloat16),
    )
    aliased = held is not None
    return pl.pallas_call(
        lambda *refs: forward_kernel(*refs, source=source, aliased=aliased),
        out_shape=outs,
        in_specs=[SM, VM] + [ANY] * (source.count + (3 if aliased else 0)),
        out_specs=(VM, ANY, ANY, ANY),
        scratch_shapes=[
            pltpu.VMEM((2, 16, 2, D // 16, R), jnp.bfloat16),
            pltpu.VMEM((SET + 1, ROWS, D), jnp.bfloat16),
            pltpu.VMEM((SET, ROWS, R), jnp.float32),
            pltpu.VMEM((SET, ROWS, R), jnp.bfloat16),
            pltpu.SemaphoreType.DMA((2, 2)),
            pltpu.SemaphoreType.DMA((SET,)),
            pltpu.SemaphoreType.DMA((1,)),
            pltpu.SemaphoreType.DMA((1,)),
        ],
        input_output_aliases={first: 1, first + 1: 2, first + 2: 3} if aliased else {},
        compiler_params=pltpu.CompilerParams(vmem_limit_bytes=52 * 2**20),
        cost_estimate=pl.CostEstimate(
            flops=SET * ROWS * D * R, bytes_accessed=SET * D * R, transcendentals=0
        ),
        name="forward_set",
    )(flags, rows, *weights, *(held or ()))


def backward_kernel(*refs, source, aliased, from_final, last):
    flags, g_ref, h_in, pre_in = refs[:4]
    w_refs = refs[4 : 4 + source.count]
    refs = refs[4 + source.count + (1 if aliased else 0) :]
    y_ref, g_out = refs[:2]
    wbuf, hbuf, prebuf, gbuf, dnbuf, gcut, sem_w, sem_h, sem_p, sem_g = refs[2:]

    @pl.when(flags[0] == 1)
    def _():
        weights = source(w_refs, flags, wbuf, sem_w)

        def g_copy(step):
            return pltpu.make_async_copy(
                gcut.at[:, step], g_out.at[:, SET - 1 - step], sem_g.at[step]
            )

        def g_send(step):
            for r in range(16):
                gcut[r, step] = gbuf[step, :, r * (D // 16) : (r + 1) * (D // 16)]
            g_copy(step).start()

        def h_copy(layer):
            return pltpu.make_async_copy(h_in.at[layer], hbuf.at[layer], sem_h.at[layer])

        pre_copy = pltpu.make_async_copy(pre_in, prebuf, sem_p.at[0])
        pre_copy.start()
        h_copy(SET - 1).start()
        weights.first(SET - 1, (1, 0))
        for layer in range(SET - 2, -1, -1):
            h_copy(layer).start()
        if from_final:
            gbuf[0] = (g_ref[...].astype(jnp.float32) * COT).astype(jnp.bfloat16)
        else:
            gbuf[0] = g_ref[...]
        pre_copy.wait()
        steps = SET - 1 if last else SET

        def one_layer(step, carry):
            layer = SET - 1 - step
            slot = lax.rem(step, 2)


            @pl.when(step + 1 < steps)
            def _():
                weights.begin(layer - 1, 1 - slot)

            g_send(step)
            h_copy(layer).wait()
            inv = inverse_rms(hbuf, layer)
            pre = prebuf[layer]
            sigma = 1.0 / (1.0 + jnp.exp(-pre))
            slope = sigma * (1.0 + pre * (1.0 - sigma))
            d_active = jnp.zeros((ROWS, R), jnp.float32)
            weights.arrive(layer, slot, 1)
            for c in range(CH):
                d_active = d_active + jnp.dot(
                    gbuf[step, :, columns(c)],
                    chunk(wbuf, slot, 1, c),
                    preferred_element_type=jnp.float32,
                )
            d_pre = (d_active * slope).astype(jnp.bfloat16)
            total = jnp.zeros((ROWS, 1), jnp.float32)
            weights.arrive(layer, slot, 0)
            for c in range(CH):
                d_normed = lax.dot_general(
                    d_pre,
                    chunk(wbuf, slot, 0, c),
                    (((1,), (1,)), ((), ())),
                    preferred_element_type=jnp.float32,
                )
                unit = hbuf[layer, :, columns(c)].astype(jnp.float32) * inv
                total = total + jnp.sum(d_normed * unit, axis=-1, keepdims=True)
                dnbuf[:, columns(c)] = d_normed
            mean = total * (1.0 / D)
            for c in range(CH):
                unit = hbuf[layer, :, columns(c)].astype(jnp.float32) * inv
                moved = inv * (dnbuf[:, columns(c)] - unit * mean)
                before = gbuf[step, :, columns(c)].astype(jnp.float32)
                gbuf[step + 1, :, columns(c)] = (before + moved).astype(jnp.bfloat16)
            return carry

        lax.fori_loop(0, steps, one_layer, 0)
        if last:
            g_send(SET - 1)
            h_copy(0).wait()
        y_ref[...] = gbuf[steps]
        for step in range(SET):
            g_copy(step).wait()


def run_backward(flags, g_rows, weights, h_held, pre_held, held=None, from_final=False, last=False):
    source = Scattered
    outs = (
        jax.ShapeDtypeStruct((ROWS, D), jnp.bfloat16),
        jax.ShapeDtypeStruct((16, SET, ROWS, D // 16), jnp.bfloat16),
    )
    aliased = held is not None
    return pl.pallas_call(
        lambda *refs: backward_kernel(
            *refs, source=source, aliased=aliased, from_final=from_final, last=last
        ),
        out_shape=outs,
        in_specs=[SM, VM, ANY, ANY] + [ANY] * (source.count + (1 if aliased else 0)),
        out_specs=(VM, ANY),
        scratch_shapes=[
            pltpu.VMEM((2, 16, 2, D // 16, R), jnp.bfloat16),
            pltpu.VMEM((SET, ROWS, D), jnp.bfloat16),
            pltpu.VMEM((SET, ROWS, R), jnp.float32),
            pltpu.VMEM((SET + 1, ROWS, D), jnp.bfloat16),
            pltpu.VMEM((ROWS, D), jnp.float32),
            pltpu.VMEM((16, SET, ROWS, D // 16), jnp.bfloat16),
            pltpu.SemaphoreType.DMA((2, 2)),
            pltpu.SemaphoreType.DMA((SET,)),
            pltpu.SemaphoreType.DMA((1,)),
            pltpu.SemaphoreType.DMA((SET,)),
        ],
        input_output_aliases={4 + source.count: 1} if aliased else {},
        compiler_params=pltpu.CompilerParams(vmem_limit_bytes=52 * 2**20),
        cost_estimate=pl.CostEstimate(
            flops=SET * ROWS * D * R, bytes_accessed=SET * D * R, transcendentals=0
        ),
        name="backward_set",
    )(flags, g_rows, h_held, pre_held, *weights, *((held,) if aliased else ()))


def grad_kernel(place, g_ref, act_ref, *out_refs, first):
    for k in range(SET):
        layer = lax.rem(place[0] + k, SET)
        g = g_ref[:, layer].reshape(16 * ROWS, D // 16)
        act = act_ref[:, first + layer].reshape(16 * ROWS, R)
        out_refs[k][...] = lax.dot_general(
            g, act, (((0,), (0,)), ((), ())), preferred_element_type=jnp.float32
        ).astype(jnp.bfloat16)


def run_grad(place, g_all, act_all, first):
    return pl.pallas_call(
        lambda *refs: grad_kernel(*refs, first=first),
        out_shape=(jax.ShapeDtypeStruct((D // 16, R), jnp.bfloat16),) * SET,
        in_specs=[SM, VM, VM],
        out_specs=(VM,) * SET,
        compiler_params=pltpu.CompilerParams(vmem_limit_bytes=52 * 2**20),
        name="grad_set",
    )(place, g_all, act_all)


def summed_over_zh(place, g_all, act_all, first):
    parts = run_grad(place, g_all, act_all, first)
    total = parts[0].astype(jnp.float32)
    for k in range(1, SET):
        route = [(source, (source + k) % SET) for source in range(SET)]
        total = total + lax.ppermute(parts[k], "zh", route).astype(jnp.float32)
    return total.astype(jnp.bfloat16)


def hop(rows):
    return lax.ppermute(rows, "y", [(0, 1), (1, 0), (2, 3), (3, 2)])


def spread(g_set):
    return lax.all_to_all(g_set, DP, 0, 0)


def from_ring(block, axis, away):
    count = lax.axis_size(axis)
    return lax.ppermute(block, axis, [((d + away) % count, d) for d in range(count)])


def across_y(block):
    return lax.ppermute(block, "y", [(0, 3), (3, 0), (1, 2), (2, 1)])


def over_z(chunk_now):
    beside = lax.ppermute(chunk_now, "zh", [(0, 1), (1, 0), (2, 3), (3, 2)])
    route = []
    for y in range(4):
        for zh in range(4):
            route.append((y * 4 + zh, (3 - y) * 4 + (zh ^ 1)))
    return jnp.stack([beside, lax.ppermute(chunk_now, ("y", "zh"), route)])


def over_x_sides(block):
    return block, from_ring(block, "x", 1), from_ring(block, "x", -1)


def over_x_across(near_side, far_side):
    near, near_up, near_down = near_side
    far, far_up, far_down = far_side
    near_across, far_across = from_ring(near_up, "x", 1), from_ring(far_down, "x", -1)
    return near, near_up, near_across, near_down, far, far_up, far_across, far_down


def both_cores(blocks):
    parts = []
    for one in blocks:
        parts += [one, from_ring(one, "core", 1)]
    return tuple(parts)


def shards(inputs_down, inputs_up, w_in, w_out):
    y, zh, dp = lax.axis_index("y"), lax.axis_index("zh"), lax.axis_index(DP)
    low_half = y < 2
    stage_p = (y == 0) | (y == 3)

    def own(layer_slot):
        parts = [
            lax.dynamic_slice(w, (0, layer_slot, dp * (D // 16), 0), (1, 1, D // 16, R))[0, 0]
            for w in (w_in, w_out)
        ]
        return jnp.stack(parts)

    def own_half(layer_slot):
        core = lax.axis_index("core")
        parts = [
            lax.dynamic_slice(w, (0, layer_slot, core * (D // 2), 0), (1, 1, D // 2, R))[0, 0]
            for w in (w_in, w_out)
        ]
        return jnp.stack(parts).reshape(2, 8, D // 16, R)

    first_slot = jnp.where(low_half, 0, 1)
    own_layers = tuple(w[0].reshape(2, 16, D // 16, R) for w in (w_in, w_out))
    half_a = across_y(own_half(first_slot))
    near_a = over_z(own(first_slot))
    chunk_b, near_a = lax.optimization_barrier((own(1 - first_slot), near_a))
    near_b = over_z(chunk_b)
    blocks_a = over_x_across(over_x_sides(near_a), over_x_sides(from_ring(near_a, "zl", 1)))
    far_b = from_ring(near_b, "zl", 1)
    near_b, far_b, blocks_a = lax.optimization_barrier((near_b, far_b, blocks_a))
    half_b, half_a = lax.optimization_barrier((own_half(1 - first_slot), half_a))
    half_b = across_y(half_b)
    w_a = own_layers + both_cores((half_a,)) + both_cores(blocks_a)
    near_side, far_side = over_x_sides(near_b), over_x_sides(far_b)

    def flag(active, slot_now):
        reverse = slot_now == 1
        here = [lax.axis_index(name) for name in ("zh",) + DP]
        return jnp.stack([v.astype(jnp.int32) for v in [active, reverse, slot_now] + here])

    p_a, p_b = flag(stage_p, first_slot), flag(stage_p, 1 - first_slot)
    q_a, q_b = flag(~stage_p, first_slot), flag(~stage_p, 1 - first_slot)

    mine = jnp.where(low_half, inputs_down, inputs_up).reshape(-1, D)
    mine = lax.dynamic_slice(mine, (zh * REAL, 0), (REAL, D))
    rows = jnp.pad(mine, ((0, ROWS - REAL), (0, 0)))

    rows, h_a, pre_a, act_a = run_forward(p_a, rows, w_a)
    rows, near_side = lax.optimization_barrier((rows, near_side))
    rows = hop(rows)
    rows, far_side = lax.optimization_barrier((rows, far_side))
    parts_b = both_cores(over_x_across(near_side, far_side))
    rows, h_a, pre_a, act_a = run_forward(q_a, rows, w_a, (h_a, pre_a, act_a))
    rows, half_b = lax.optimization_barrier((rows, half_b))
    w_b = own_layers + both_cores((half_b,)) + parts_b
    rows, h_b, pre_b, act_b = run_forward(q_b, rows, w_b)
    rows = hop(rows)
    rows, h_b, pre_b, act_b = run_forward(p_b, rows, w_b, (h_b, pre_b, act_b))
    act_all = lax.all_gather(jnp.concatenate([act_a, act_b], axis=0), DP)
    rows, g_b = run_backward(p_b, rows, w_b, h_b, pre_b, from_final=True)
    rows = hop(rows)
    rows, g_b = run_backward(q_b, rows, w_b, h_b, pre_b, held=g_b)
    rows, g_a = run_backward(q_a, rows, w_a, h_a, pre_a)
    rows, act_all = lax.optimization_barrier((rows, act_all))
    rows = hop(rows)
    rows, g_a = run_backward(p_a, rows, w_a, h_a, pre_a, held=g_a, last=True)
    place = zh.astype(jnp.int32)[None]
    far_b = spread(g_b)
    g_a, far_b = lax.optimization_barrier((g_a, far_b))
    far_a = spread(g_a)
    sum_b = summed_over_zh(place, far_b, act_all, SET)
    sum_a = summed_over_zh(place, far_a, act_all, 0)
    kept = jnp.where(low_half, sum_a, sum_b)
    other = jnp.where(low_half, sum_b, sum_a)
    received = across_y(other)
    return (kept.astype(jnp.float32) + received.astype(jnp.float32))[None]


def solution(mesh):
    fine = Mesh(mesh.devices.reshape(4, 4, 2, 4, 2), GRID_AXES)
    section = ("y", "zh")
    placed = (
        P(DP, None, None),
        P(DP, None, None),
        P(section, None, None, None),
        P(section, None, None, None),
    )
    return jax.shard_map(
        shards, mesh=fine, in_specs=placed, out_specs=P(section, DP, None), check_vma=False
    )
```

```python
import jax
import jax.numpy as jnp
from jax import lax
from jax.experimental import pallas as pl
from jax.experimental.pallas import tpu as pltpu
from jax.sharding import Mesh, PartitionSpec as P

EPS = 1e-06
COT = 0.0625
D, R = 5120, 256
REAL, ROWS = 18, 24
SET = 4
CH = 4
CW = D // CH
DP = ("zl", "x", "core")
GRID_AXES = ("y", "zh", "zl", "x", "core")
ANY = pl.BlockSpec(memory_space=pl.ANY)
VM = pl.BlockSpec(memory_space=pltpu.VMEM)
SM = pl.BlockSpec(memory_space=pltpu.SMEM)


class Gathered:
    count = 1

    def __init__(self, refs, flags, wbuf, sem):
        self.w, self.flags, self.wbuf, self.sem = refs[0], flags, wbuf, sem

    def copy(self, layer, slot, which):
        held = jnp.where(self.flags[1] == 1, SET - 1 - layer, layer)
        return pltpu.make_async_copy(
            self.w.at[held, :, which], self.wbuf.at[slot, :, which], self.sem.at[slot, which]
        )

    def first(self, layer, order):
        self.order = order
        self.begin(layer, 0)

    def begin(self, layer, slot):
        for which in self.order:
            self.copy(layer, slot, which).start()

    def arrive(self, layer, slot, which):
        self.copy(layer, slot, which).wait()


class Scattered:
    count = 20

    def __init__(self, refs, flags, wbuf, sem):
        self.own, self.halves, self.parts = refs[:2], refs[2:4], refs[4:]
        self.flags, self.wbuf, self.sem = flags, wbuf, sem

    def fetch(self, layer, slot):
        flags = self.flags
        held = jnp.where(flags[1] == 1, SET - 1 - layer, layer)
        zh = flags[3]
        away = lax.rem(held + SET - zh, SET)
        mirrored = held == SET - 1 - zh

        @pl.when(away == 0)
        def _():
            for which in range(2):
                pltpu.make_async_copy(
                    self.own[which].at[flags[2]], self.wbuf.at[slot, :, which], self.sem.at[slot, 0]
                ).start()

        @pl.when(mirrored)
        def _():
            for n in range(2):
                half = lax.rem(flags[6] + n, 2)
                for which in range(2):
                    pltpu.make_async_copy(
                        self.halves[n].at[which],
                        self.wbuf.at[slot, pl.ds(half * 8, 8), which],
                        self.sem.at[slot, 0],
                    ).start()

        @pl.when((away > 0) & jnp.logical_not(mirrored))
        def _():
            entry = jnp.where(away == 2, 1, 0)
            for n in range(16):
                zl_off, x_off, core_off = n // 8, (n // 2) % 4, n % 2
                zl = lax.rem(flags[4] + zl_off, 2)
                x = lax.rem(flags[5] + x_off, 4)
                core = lax.rem(flags[6] + core_off, 2)
                pltpu.make_async_copy(
                    self.parts[n].at[entry],
                    self.wbuf.at[slot, zl * 8 + x * 2 + core],
                    self.sem.at[slot, 0],
                ).start()

    def first(self, layer, order):
        self.leading = order[0]
        self.fetch(layer, 0)

    def begin(self, layer, slot):
        self.fetch(layer, slot)

    def arrive(self, layer, slot, which):
        if which == self.leading:
            pltpu.make_async_copy(
                self.wbuf.at[1 - slot], self.wbuf.at[slot], self.sem.at[slot, 0]
            ).wait()


def chunk(wbuf, slot, which, c):
    per = 16 // CH
    return wbuf[slot, c * per : (c + 1) * per, which].reshape(CW, R)


def columns(c):
    return slice(c * CW, (c + 1) * CW)


def inverse_rms(hbuf, layer):
    total = jnp.zeros((ROWS, 1), jnp.float32)
    for c in range(CH):
        v = hbuf[layer, :, columns(c)].astype(jnp.float32)
        total = total + jnp.sum(v * v, axis=-1, keepdims=True)
    return lax.rsqrt(total * (1.0 / D) + EPS)


def forward_kernel(*refs, source, aliased):
    flags, x_ref = refs[:2]
    w_refs = refs[2 : 2 + source.count]
    refs = refs[2 + source.count + (3 if aliased else 0) :]
    y_ref, h_out, pre_out, act_out = refs[:4]
    wbuf, hbuf, prebuf, actbuf, sem_w, sem_h, sem_p, sem_a = refs[4:]

    @pl.when(flags[0] == 1)
    def _():
        weights = source(w_refs, flags, wbuf, sem_w)
        weights.first(0, (0, 1))
        hbuf[0] = x_ref[...]

        def step(layer, carry):
            slot = lax.rem(layer, 2)


            @pl.when(layer + 1 < SET)
            def _():
                weights.begin(layer + 1, 1 - slot)

            pltpu.make_async_copy(hbuf.at[layer], h_out.at[layer], sem_h.at[layer]).start()
            inv = inverse_rms(hbuf, layer)
            pre = jnp.zeros((ROWS, R), jnp.float32)
            weights.arrive(layer, slot, 0)
            for c in range(CH):
                normed = (hbuf[layer, :, columns(c)].astype(jnp.float32) * inv).astype(jnp.bfloat16)
                pre = pre + jnp.dot(
                    normed, chunk(wbuf, slot, 0, c), preferred_element_type=jnp.float32
                )
            active = (pre / (1.0 + jnp.exp(-pre))).astype(jnp.bfloat16)
            prebuf[layer] = pre
            actbuf[layer] = active
            weights.arrive(layer, slot, 1)
            for c in range(CH):
                branch = lax.dot_general(
                    active,
                    chunk(wbuf, slot, 1, c),
                    (((1,), (1,)), ((), ())),
                    preferred_element_type=jnp.float32,
                )
                before = hbuf[layer, :, columns(c)].astype(jnp.float32)
                hbuf[layer + 1, :, columns(c)] = (before + branch).astype(jnp.bfloat16)
            return carry

        lax.fori_loop(0, SET, step, 0)
        y_ref[...] = hbuf[SET]
        copies = [
            pltpu.make_async_copy(prebuf, pre_out, sem_p.at[0]),
            pltpu.make_async_copy(actbuf, act_out, sem_a.at[0]),
        ]
        for one in copies:
            one.start()
        for layer in range(SET):
            copies.append(
                pltpu.make_async_copy(hbuf.at[layer], h_out.at[layer], sem_h.at[layer])
            )
        for one in copies:
            one.wait()


def run_forward(flags, rows, weights, held=None):
    source = Gathered if len(weights) == 1 else Scattered
    first = 2 + source.count
    outs = (
        jax.ShapeDtypeStruct((ROWS, D), jnp.bfloat16),
        jax.ShapeDtypeStruct((SET, ROWS, D), jnp.bfloat16),
        jax.ShapeDtypeStruct((SET, ROWS, R), jnp.float32),
        jax.ShapeDtypeStruct((SET, ROWS, R), jnp.bfloat16),
    )
    aliased = held is not None
    return pl.pallas_call(
        lambda *refs: forward_kernel(*refs, source=source, aliased=aliased),
        out_shape=outs,
        in_specs=[SM, VM] + [ANY] * (source.count + (3 if aliased else 0)),
        out_specs=(VM, ANY, ANY, ANY),
        scratch_shapes=[
            pltpu.VMEM((2, 16, 2, D // 16, R), jnp.bfloat16),
            pltpu.VMEM((SET + 1, ROWS, D), jnp.bfloat16),
            pltpu.VMEM((SET, ROWS, R), jnp.float32),
            pltpu.VMEM((SET, ROWS, R), jnp.bfloat16),
            pltpu.SemaphoreType.DMA((2, 2)),
            pltpu.SemaphoreType.DMA((SET,)),
            pltpu.SemaphoreType.DMA((1,)),
            pltpu.SemaphoreType.DMA((1,)),
        ],
        input_output_aliases={first: 1, first + 1: 2, first + 2: 3} if aliased else {},
        compiler_params=pltpu.CompilerParams(vmem_limit_bytes=52 * 2**20),
        cost_estimate=pl.CostEstimate(
            flops=SET * ROWS * D * R, bytes_accessed=SET * D * R, transcendentals=0
        ),
        name="forward_set",
    )(flags, rows, *weights, *(held or ()))


def backward_kernel(*refs, source, aliased, from_final, last):
    flags, g_ref, h_in, pre_in = refs[:4]
    w_refs = refs[4 : 4 + source.count]
    refs = refs[4 + source.count + (1 if aliased else 0) :]
    y_ref, g_out = refs[:2]
    wbuf, hbuf, prebuf, gbuf, dnbuf, gcut, sem_w, sem_h, sem_p, sem_g = refs[2:]

    @pl.when(flags[0] == 1)
    def _():
        weights = source(w_refs, flags, wbuf, sem_w)

        def g_copy(step):
            return pltpu.make_async_copy(
                gcut.at[:, step], g_out.at[:, SET - 1 - step], sem_g.at[step]
            )

        def g_send(step):
            for r in range(16):
                gcut[r, step] = gbuf[step, :, r * (D // 16) : (r + 1) * (D // 16)]
            g_copy(step).start()

        def h_copy(layer):
            return pltpu.make_async_copy(h_in.at[layer], hbuf.at[layer], sem_h.at[layer])

        pre_copy = pltpu.make_async_copy(pre_in, prebuf, sem_p.at[0])
        pre_copy.start()
        h_copy(SET - 1).start()
        weights.first(SET - 1, (1, 0))
        for layer in range(SET - 2, -1, -1):
            h_copy(layer).start()
        if from_final:
            gbuf[0] = (g_ref[...].astype(jnp.float32) * COT).astype(jnp.bfloat16)
        else:
            gbuf[0] = g_ref[...]
        pre_copy.wait()
        steps = SET - 1 if last else SET

        def one_layer(step, carry):
            layer = SET - 1 - step
            slot = lax.rem(step, 2)


            @pl.when(step + 1 < steps)
            def _():
                weights.begin(layer - 1, 1 - slot)

            g_send(step)
            h_copy(layer).wait()
            inv = inverse_rms(hbuf, layer)
            pre = prebuf[layer]
            sigma = 1.0 / (1.0 + jnp.exp(-pre))
            slope = sigma * (1.0 + pre * (1.0 - sigma))
            d_active = jnp.zeros((ROWS, R), jnp.float32)
            weights.arrive(layer, slot, 1)
            for c in range(CH):
                d_active = d_active + jnp.dot(
                    gbuf[step, :, columns(c)],
                    chunk(wbuf, slot, 1, c),
                    preferred_element_type=jnp.float32,
                )
            d_pre = (d_active * slope).astype(jnp.bfloat16)
            total = jnp.zeros((ROWS, 1), jnp.float32)
            weights.arrive(layer, slot, 0)
            for c in range(CH):
                d_normed = lax.dot_general(
                    d_pre,
                    chunk(wbuf, slot, 0, c),
                    (((1,), (1,)), ((), ())),
                    preferred_element_type=jnp.float32,
                )
                unit = hbuf[layer, :, columns(c)].astype(jnp.float32) * inv
                total = total + jnp.sum(d_normed * unit, axis=-1, keepdims=True)
                dnbuf[:, columns(c)] = d_normed
            mean = total * (1.0 / D)
            for c in range(CH):
                unit = hbuf[layer, :, columns(c)].astype(jnp.float32) * inv
                moved = inv * (dnbuf[:, columns(c)] - unit * mean)
                before = gbuf[step, :, columns(c)].astype(jnp.float32)
                gbuf[step + 1, :, columns(c)] = (before + moved).astype(jnp.bfloat16)
            return carry

        lax.fori_loop(0, steps, one_layer, 0)
        if last:
            g_send(SET - 1)
            h_copy(0).wait()
        y_ref[...] = gbuf[steps]
        for step in range(SET):
            g_copy(step).wait()


def run_backward(flags, g_rows, weights, h_held, pre_held, held=None, from_final=False, last=False):
    source = Gathered if len(weights) == 1 else Scattered
    outs = (
        jax.ShapeDtypeStruct((ROWS, D), jnp.bfloat16),
        jax.ShapeDtypeStruct((16, SET, ROWS, D // 16), jnp.bfloat16),
    )
    aliased = held is not None
    return pl.pallas_call(
        lambda *refs: backward_kernel(
            *refs, source=source, aliased=aliased, from_final=from_final, last=last
        ),
        out_shape=outs,
        in_specs=[SM, VM, ANY, ANY] + [ANY] * (source.count + (1 if aliased else 0)),
        out_specs=(VM, ANY),
        scratch_shapes=[
            pltpu.VMEM((2, 16, 2, D // 16, R), jnp.bfloat16),
            pltpu.VMEM((SET, ROWS, D), jnp.bfloat16),
            pltpu.VMEM((SET, ROWS, R), jnp.float32),
            pltpu.VMEM((SET + 1, ROWS, D), jnp.bfloat16),
            pltpu.VMEM((ROWS, D), jnp.float32),
            pltpu.VMEM((16, SET, ROWS, D // 16), jnp.bfloat16),
            pltpu.SemaphoreType.DMA((2, 2)),
            pltpu.SemaphoreType.DMA((SET,)),
            pltpu.SemaphoreType.DMA((1,)),
            pltpu.SemaphoreType.DMA((SET,)),
        ],
        input_output_aliases={4 + source.count: 1} if aliased else {},
        compiler_params=pltpu.CompilerParams(vmem_limit_bytes=52 * 2**20),
        cost_estimate=pl.CostEstimate(
            flops=SET * ROWS * D * R, bytes_accessed=SET * D * R, transcendentals=0
        ),
        name="backward_set",
    )(flags, g_rows, h_held, pre_held, *weights, *((held,) if aliased else ()))


def grad_kernel(place, g_ref, act_ref, *out_refs, first):
    for k in range(SET):
        layer = lax.rem(place[0] + k, SET)
        g = g_ref[:, layer].reshape(16 * ROWS, D // 16)
        act = act_ref[:, first + layer].reshape(16 * ROWS, R)
        out_refs[k][...] = lax.dot_general(
            g, act, (((0,), (0,)), ((), ())), preferred_element_type=jnp.float32
        ).astype(jnp.bfloat16)


def run_grad(place, g_all, act_all, first):
    return pl.pallas_call(
        lambda *refs: grad_kernel(*refs, first=first),
        out_shape=(jax.ShapeDtypeStruct((D // 16, R), jnp.bfloat16),) * SET,
        in_specs=[SM, VM, VM],
        out_specs=(VM,) * SET,
        compiler_params=pltpu.CompilerParams(vmem_limit_bytes=52 * 2**20),
        name="grad_set",
    )(place, g_all, act_all)


def summed_over_zh(parts):
    total = parts[0].astype(jnp.float32)
    for k in range(1, SET):
        route = [(source, (source + k) % SET) for source in range(SET)]
        total = total + lax.ppermute(parts[k], "zh", route).astype(jnp.float32)
    return total.astype(jnp.bfloat16)


def hop(rows):
    return lax.ppermute(rows, "y", [(0, 1), (1, 0), (2, 3), (3, 2)])


def spread(g_set):
    return lax.all_to_all(g_set, DP, 0, 0)


def from_ring(block, axis, away):
    count = lax.axis_size(axis)
    return lax.ppermute(block, axis, [((d + away) % count, d) for d in range(count)])


def across_y(block):
    return lax.ppermute(block, "y", [(0, 3), (3, 0), (1, 2), (2, 1)])


def over_z(chunk_now):
    beside = lax.ppermute(chunk_now, "zh", [(0, 1), (1, 0), (2, 3), (3, 2)])
    route = []
    for y in range(4):
        for zh in range(4):
            route.append((y * 4 + zh, (3 - y) * 4 + (zh ^ 1)))
    return jnp.stack([beside, lax.ppermute(chunk_now, ("y", "zh"), route)])


def over_x(near):
    far = from_ring(near, "zl", 1)
    near_up, near_down = from_ring(near, "x", 1), from_ring(near, "x", -1)
    near_across = from_ring(near_up, "x", 1)
    far_up, far_down = from_ring(far, "x", 1), from_ring(far, "x", -1)
    far_across = from_ring(far_down, "x", -1)
    parts = []
    for one in (near, near_up, near_across, near_down, far, far_up, far_across, far_down):
        parts += [one, from_ring(one, "core", 1)]
    return tuple(parts)


def shards(inputs_down, inputs_up, w_in, w_out):
    y, zh, dp = lax.axis_index("y"), lax.axis_index("zh"), lax.axis_index(DP)
    low_half = y < 2
    stage_p = (y == 0) | (y == 3)

    def own(layer_slot):
        parts = [
            lax.dynamic_slice(w, (0, layer_slot, dp * (D // 16), 0), (1, 1, D // 16, R))[0, 0]
            for w in (w_in, w_out)
        ]
        return jnp.stack(parts)

    def gathered(own_part):
        return lax.all_gather(own_part, ("zh",) + DP).reshape(SET, 16, 2, D // 16, R)

    def own_half(layer_slot):
        core = lax.axis_index("core")
        parts = [
            lax.dynamic_slice(w, (0, layer_slot, core * (D // 2), 0), (1, 1, D // 2, R))[0, 0]
            for w in (w_in, w_out)
        ]
        return jnp.stack(parts).reshape(2, 8, D // 16, R)

    first_slot = jnp.where(low_half, 0, 1)
    own_layers = tuple(w[0].reshape(2, 16, D // 16, R) for w in (w_in, w_out))
    w_b = (gathered(own(1 - first_slot)),)
    own_part, near_a = lax.optimization_barrier((own_half(first_slot), over_z(own(first_slot))))
    half_a = across_y(own_part)
    w_a = own_layers + (half_a, from_ring(half_a, "core", 1)) + over_x(near_a)

    def flag(active, slot_now):
        reverse = slot_now == 1
        here = [lax.axis_index(name) for name in ("zh",) + DP]
        return jnp.stack([v.astype(jnp.int32) for v in [active, reverse, slot_now] + here])

    p_a, p_b = flag(stage_p, first_slot), flag(stage_p, 1 - first_slot)
    q_a, q_b = flag(~stage_p, first_slot), flag(~stage_p, 1 - first_slot)

    mine = jnp.where(low_half, inputs_down, inputs_up).reshape(-1, D)
    mine = lax.dynamic_slice(mine, (zh * REAL, 0), (REAL, D))
    rows = jnp.pad(mine, ((0, ROWS - REAL), (0, 0)))

    rows, h_a, pre_a, act_a = run_forward(p_a, rows, w_a)
    rows = hop(rows)
    rows, h_a, pre_a, act_a = run_forward(q_a, rows, w_a, (h_a, pre_a, act_a))
    rows, h_b, pre_b, act_b = run_forward(q_b, rows, w_b)
    rows = hop(rows)
    rows, h_b, pre_b, act_b = run_forward(p_b, rows, w_b, (h_b, pre_b, act_b))
    act_all = lax.all_gather(jnp.concatenate([act_a, act_b], axis=0), DP)
    rows, g_b = run_backward(p_b, rows, w_b, h_b, pre_b, from_final=True)
    rows = hop(rows)
    rows, g_b = run_backward(q_b, rows, w_b, h_b, pre_b, held=g_b)
    rows, g_a = run_backward(q_a, rows, w_a, h_a, pre_a)
    rows, act_all = lax.optimization_barrier((rows, act_all))
    rows = hop(rows)
    place = zh.astype(jnp.int32)[None]
    parts_b = run_grad(place, spread(g_b), act_all, SET)
    rows, parts_b = lax.optimization_barrier((rows, parts_b))
    rows, g_a = run_backward(p_a, rows, w_a, h_a, pre_a, held=g_a, last=True)
    g_a, sum_b = lax.optimization_barrier((g_a, summed_over_zh(parts_b)))
    sum_a = summed_over_zh(run_grad(place, spread(g_a), act_all, 0))
    kept = jnp.where(low_half, sum_a, sum_b)
    other = jnp.where(low_half, sum_b, sum_a)
    received = across_y(other)
    return (kept.astype(jnp.float32) + received.astype(jnp.float32))[None]


def solution(mesh):
    fine = Mesh(mesh.devices.reshape(4, 4, 2, 4, 2), GRID_AXES)
    section = ("y", "zh")
    placed = (
        P(DP, None, None),
        P(DP, None, None),
        P(section, None, None, None),
        P(section, None, None, None),
    )
    return jax.shard_map(
        shards, mesh=fine, in_specs=placed, out_specs=P(section, DP, None), check_vma=False
    )
```

```python
import jax
import jax.numpy as jnp
from jax import lax
from jax.experimental import pallas as pl
from jax.experimental.pallas import tpu as pltpu
from jax.sharding import Mesh, PartitionSpec as P

EPS = 1e-06
COT = 0.0625
D, R = 5120, 256
REAL, ROWS = 18, 24
SET = 4
CH = 4
CW = D // CH
DP = ("zl", "x", "core")
GRID_AXES = ("y", "zh", "zl", "x", "core")
ANY = pl.BlockSpec(memory_space=pl.ANY)
VM = pl.BlockSpec(memory_space=pltpu.VMEM)
SM = pl.BlockSpec(memory_space=pltpu.SMEM)


class Gathered:
    count = 1

    def __init__(self, refs, flags, wbuf, sem):
        self.w, self.flags, self.wbuf, self.sem = refs[0], flags, wbuf, sem

    def copy(self, layer, slot, which):
        held = jnp.where(self.flags[1] == 1, SET - 1 - layer, layer)
        return pltpu.make_async_copy(
            self.w.at[held, :, which], self.wbuf.at[slot, :, which], self.sem.at[slot, which]
        )

    def first(self, layer, order):
        self.order = order
        self.begin(layer, 0)

    def begin(self, layer, slot):
        for which in self.order:
            self.copy(layer, slot, which).start()

    def arrive(self, layer, slot, which):
        self.copy(layer, slot, which).wait()


class Scattered:
    count = 20

    def __init__(self, refs, flags, wbuf, sem):
        self.own, self.halves, self.parts = refs[:2], refs[2:4], refs[4:]
        self.flags, self.wbuf, self.sem = flags, wbuf, sem

    def fetch(self, layer, slot):
        flags = self.flags
        held = jnp.where(flags[1] == 1, SET - 1 - layer, layer)
        zh = flags[3]
        away = lax.rem(held + SET - zh, SET)
        mirrored = held == SET - 1 - zh

        @pl.when(away == 0)
        def _():
            for which in range(2):
                pltpu.make_async_copy(
                    self.own[which].at[flags[2]], self.wbuf.at[slot, :, which], self.sem.at[slot, 0]
                ).start()

        @pl.when(mirrored)
        def _():
            for n in range(2):
                half = lax.rem(flags[6] + n, 2)
                for which in range(2):
                    pltpu.make_async_copy(
                        self.halves[n].at[which],
                        self.wbuf.at[slot, pl.ds(half * 8, 8), which],
                        self.sem.at[slot, 0],
                    ).start()

        @pl.when((away > 0) & jnp.logical_not(mirrored))
        def _():
            entry = jnp.where(away == 2, 1, 0)
            for n in range(16):
                zl_off, x_off, core_off = n // 8, (n // 2) % 4, n % 2
                zl = lax.rem(flags[4] + zl_off, 2)
                x = lax.rem(flags[5] + x_off, 4)
                core = lax.rem(flags[6] + core_off, 2)
                pltpu.make_async_copy(
                    self.parts[n].at[entry],
                    self.wbuf.at[slot, zl * 8 + x * 2 + core],
                    self.sem.at[slot, 0],
                ).start()

    def first(self, layer, order):
        self.leading = order[0]
        self.fetch(layer, 0)

    def begin(self, layer, slot):
        self.fetch(layer, slot)

    def arrive(self, layer, slot, which):
        if which == self.leading:
            pltpu.make_async_copy(
                self.wbuf.at[1 - slot], self.wbuf.at[slot], self.sem.at[slot, 0]
            ).wait()


def chunk(wbuf, slot, which, c):
    per = 16 // CH
    return wbuf[slot, c * per : (c + 1) * per, which].reshape(CW, R)


def columns(c):
    return slice(c * CW, (c + 1) * CW)


def inverse_rms(hbuf, layer):
    total = jnp.zeros((ROWS, 1), jnp.float32)
    for c in range(CH):
        v = hbuf[layer, :, columns(c)].astype(jnp.float32)
        total = total + jnp.sum(v * v, axis=-1, keepdims=True)
    return lax.rsqrt(total * (1.0 / D) + EPS)


def forward_kernel(*refs, source, aliased):
    flags, x_ref = refs[:2]
    w_refs = refs[2 : 2 + source.count]
    refs = refs[2 + source.count + (3 if aliased else 0) :]
    y_ref, h_out, pre_out, act_out = refs[:4]
    wbuf, hbuf, prebuf, actbuf, sem_w, sem_h, sem_p, sem_a = refs[4:]

    @pl.when(flags[0] == 1)
    def _():
        weights = source(w_refs, flags, wbuf, sem_w)
        weights.first(0, (0, 1))
        hbuf[0] = x_ref[...]

        def step(layer, carry):
            slot = lax.rem(layer, 2)


            @pl.when(layer + 1 < SET)
            def _():
                weights.begin(layer + 1, 1 - slot)

            pltpu.make_async_copy(hbuf.at[layer], h_out.at[layer], sem_h.at[layer]).start()
            inv = inverse_rms(hbuf, layer)
            pre = jnp.zeros((ROWS, R), jnp.float32)
            weights.arrive(layer, slot, 0)
            for c in range(CH):
                normed = (hbuf[layer, :, columns(c)].astype(jnp.float32) * inv).astype(jnp.bfloat16)
                pre = pre + jnp.dot(
                    normed, chunk(wbuf, slot, 0, c), preferred_element_type=jnp.float32
                )
            active = (pre / (1.0 + jnp.exp(-pre))).astype(jnp.bfloat16)
            prebuf[layer] = pre
            actbuf[layer] = active
            weights.arrive(layer, slot, 1)
            for c in range(CH):
                branch = lax.dot_general(
                    active,
                    chunk(wbuf, slot, 1, c),
                    (((1,), (1,)), ((), ())),
                    preferred_element_type=jnp.float32,
                )
                before = hbuf[layer, :, columns(c)].astype(jnp.float32)
                hbuf[layer + 1, :, columns(c)] = (before + branch).astype(jnp.bfloat16)
            return carry

        lax.fori_loop(0, SET, step, 0)
        y_ref[...] = hbuf[SET]
        copies = [
            pltpu.make_async_copy(prebuf, pre_out, sem_p.at[0]),
            pltpu.make_async_copy(actbuf, act_out, sem_a.at[0]),
        ]
        for one in copies:
            one.start()
        for layer in range(SET):
            copies.append(
                pltpu.make_async_copy(hbuf.at[layer], h_out.at[layer], sem_h.at[layer])
            )
        for one in copies:
            one.wait()


def run_forward(flags, rows, weights, held=None):
    source = Gathered if len(weights) == 1 else Scattered
    first = 2 + source.count
    outs = (
        jax.ShapeDtypeStruct((ROWS, D), jnp.bfloat16),
        jax.ShapeDtypeStruct((SET, ROWS, D), jnp.bfloat16),
        jax.ShapeDtypeStruct((SET, ROWS, R), jnp.float32),
        jax.ShapeDtypeStruct((SET, ROWS, R), jnp.bfloat16),
    )
    aliased = held is not None
    return pl.pallas_call(
        lambda *refs: forward_kernel(*refs, source=source, aliased=aliased),
        out_shape=outs,
        in_specs=[SM, VM] + [ANY] * (source.count + (3 if aliased else 0)),
        out_specs=(VM, ANY, ANY, ANY),
        scratch_shapes=[
            pltpu.VMEM((2, 16, 2, D // 16, R), jnp.bfloat16),
            pltpu.VMEM((SET + 1, ROWS, D), jnp.bfloat16),
            pltpu.VMEM((SET, ROWS, R), jnp.float32),
            pltpu.VMEM((SET, ROWS, R), jnp.bfloat16),
            pltpu.SemaphoreType.DMA((2, 2)),
            pltpu.SemaphoreType.DMA((SET,)),
            pltpu.SemaphoreType.DMA((1,)),
            pltpu.SemaphoreType.DMA((1,)),
        ],
        input_output_aliases={first: 1, first + 1: 2, first + 2: 3} if aliased else {},
        compiler_params=pltpu.CompilerParams(vmem_limit_bytes=52 * 2**20),
        cost_estimate=pl.CostEstimate(
            flops=SET * ROWS * D * R, bytes_accessed=SET * D * R, transcendentals=0
        ),
        name="forward_set",
    )(flags, rows, *weights, *(held or ()))


def backward_kernel(*refs, source, aliased, from_final, last):
    flags, g_ref, h_in, pre_in = refs[:4]
    w_refs = refs[4 : 4 + source.count]
    refs = refs[4 + source.count + (1 if aliased else 0) :]
    y_ref, g_out = refs[:2]
    wbuf, hbuf, prebuf, gbuf, dnbuf, gcut, sem_w, sem_h, sem_p, sem_g = refs[2:]

    @pl.when(flags[0] == 1)
    def _():
        weights = source(w_refs, flags, wbuf, sem_w)

        def g_copy(step):
            return pltpu.make_async_copy(
                gcut.at[:, step], g_out.at[:, SET - 1 - step], sem_g.at[step]
            )

        def g_send(step):
            for r in range(16):
                gcut[r, step] = gbuf[step, :, r * (D // 16) : (r + 1) * (D // 16)]
            g_copy(step).start()

        def h_copy(layer):
            return pltpu.make_async_copy(h_in.at[layer], hbuf.at[layer], sem_h.at[layer])

        pre_copy = pltpu.make_async_copy(pre_in, prebuf, sem_p.at[0])
        pre_copy.start()
        h_copy(SET - 1).start()
        weights.first(SET - 1, (1, 0))
        for layer in range(SET - 2, -1, -1):
            h_copy(layer).start()
        if from_final:
            gbuf[0] = (g_ref[...].astype(jnp.float32) * COT).astype(jnp.bfloat16)
        else:
            gbuf[0] = g_ref[...]
        pre_copy.wait()
        steps = SET - 1 if last else SET

        def one_layer(step, carry):
            layer = SET - 1 - step
            slot = lax.rem(step, 2)


            @pl.when(step + 1 < steps)
            def _():
                weights.begin(layer - 1, 1 - slot)

            g_send(step)
            h_copy(layer).wait()
            inv = inverse_rms(hbuf, layer)
            pre = prebuf[layer]
            sigma = 1.0 / (1.0 + jnp.exp(-pre))
            slope = sigma * (1.0 + pre * (1.0 - sigma))
            d_active = jnp.zeros((ROWS, R), jnp.float32)
            weights.arrive(layer, slot, 1)
            for c in range(CH):
                d_active = d_active + jnp.dot(
                    gbuf[step, :, columns(c)],
                    chunk(wbuf, slot, 1, c),
                    preferred_element_type=jnp.float32,
                )
            d_pre = (d_active * slope).astype(jnp.bfloat16)
            total = jnp.zeros((ROWS, 1), jnp.float32)
            weights.arrive(layer, slot, 0)
            for c in range(CH):
                d_normed = lax.dot_general(
                    d_pre,
                    chunk(wbuf, slot, 0, c),
                    (((1,), (1,)), ((), ())),
                    preferred_element_type=jnp.float32,
                )
                unit = hbuf[layer, :, columns(c)].astype(jnp.float32) * inv
                total = total + jnp.sum(d_normed * unit, axis=-1, keepdims=True)
                dnbuf[:, columns(c)] = d_normed
            mean = total * (1.0 / D)
            for c in range(CH):
                unit = hbuf[layer, :, columns(c)].astype(jnp.float32) * inv
                moved = inv * (dnbuf[:, columns(c)] - unit * mean)
                before = gbuf[step, :, columns(c)].astype(jnp.float32)
                gbuf[step + 1, :, columns(c)] = (before + moved).astype(jnp.bfloat16)
            return carry

        lax.fori_loop(0, steps, one_layer, 0)
        if last:
            g_send(SET - 1)
            h_copy(0).wait()
        y_ref[...] = gbuf[steps]
        for step in range(SET):
            g_copy(step).wait()


def run_backward(flags, g_rows, weights, h_held, pre_held, held=None, from_final=False, last=False):
    source = Gathered if len(weights) == 1 else Scattered
    outs = (
        jax.ShapeDtypeStruct((ROWS, D), jnp.bfloat16),
        jax.ShapeDtypeStruct((16, SET, ROWS, D // 16), jnp.bfloat16),
    )
    aliased = held is not None
    return pl.pallas_call(
        lambda *refs: backward_kernel(
            *refs, source=source, aliased=aliased, from_final=from_final, last=last
        ),
        out_shape=outs,
        in_specs=[SM, VM, ANY, ANY] + [ANY] * (source.count + (1 if aliased else 0)),
        out_specs=(VM, ANY),
        scratch_shapes=[
            pltpu.VMEM((2, 16, 2, D // 16, R), jnp.bfloat16),
            pltpu.VMEM((SET, ROWS, D), jnp.bfloat16),
            pltpu.VMEM((SET, ROWS, R), jnp.float32),
            pltpu.VMEM((SET + 1, ROWS, D), jnp.bfloat16),
            pltpu.VMEM((ROWS, D), jnp.float32),
            pltpu.VMEM((16, SET, ROWS, D // 16), jnp.bfloat16),
            pltpu.SemaphoreType.DMA((2, 2)),
            pltpu.SemaphoreType.DMA((SET,)),
            pltpu.SemaphoreType.DMA((1,)),
            pltpu.SemaphoreType.DMA((SET,)),
        ],
        input_output_aliases={4 + source.count: 1} if aliased else {},
        compiler_params=pltpu.CompilerParams(vmem_limit_bytes=52 * 2**20),
        cost_estimate=pl.CostEstimate(
            flops=SET * ROWS * D * R, bytes_accessed=SET * D * R, transcendentals=0
        ),
        name="backward_set",
    )(flags, g_rows, h_held, pre_held, *weights, *((held,) if aliased else ()))


def grad_kernel(place, g_ref, act_ref, *out_refs, first):
    for k in range(SET):
        layer = lax.rem(place[0] + k, SET)
        g = g_ref[:, layer].reshape(16 * ROWS, D // 16)
        act = act_ref[:, first + layer].reshape(16 * ROWS, R)
        out_refs[k][...] = lax.dot_general(
            g, act, (((0,), (0,)), ((), ())), preferred_element_type=jnp.float32
        ).astype(jnp.bfloat16)


def run_grad(place, g_all, act_all, first):
    return pl.pallas_call(
        lambda *refs: grad_kernel(*refs, first=first),
        out_shape=(jax.ShapeDtypeStruct((D // 16, R), jnp.bfloat16),) * SET,
        in_specs=[SM, VM, VM],
        out_specs=(VM,) * SET,
        compiler_params=pltpu.CompilerParams(vmem_limit_bytes=52 * 2**20),
        name="grad_set",
    )(place, g_all, act_all)


def summed_over_zh(parts):
    total = parts[0].astype(jnp.float32)
    for k in range(1, SET):
        route = [(source, (source + k) % SET) for source in range(SET)]
        total = total + lax.ppermute(parts[k], "zh", route).astype(jnp.float32)
    return total.astype(jnp.bfloat16)


def hop(rows):
    return lax.ppermute(rows, "y", [(0, 1), (1, 0), (2, 3), (3, 2)])


def spread(g_set):
    return lax.all_to_all(g_set, DP, 0, 0)


def from_ring(block, axis, away):
    count = lax.axis_size(axis)
    return lax.ppermute(block, axis, [((d + away) % count, d) for d in range(count)])


def across_y(block):
    return lax.ppermute(block, "y", [(0, 3), (3, 0), (1, 2), (2, 1)])


def over_z(chunk_now):
    beside = lax.ppermute(chunk_now, "zh", [(0, 1), (1, 0), (2, 3), (3, 2)])
    route = []
    for y in range(4):
        for zh in range(4):
            route.append((y * 4 + zh, (3 - y) * 4 + (zh ^ 1)))
    return jnp.stack([beside, lax.ppermute(chunk_now, ("y", "zh"), route)])


def over_x(near):
    far = from_ring(near, "zl", 1)
    near_up, near_down = from_ring(near, "x", 1), from_ring(near, "x", -1)
    far, near_up, near_down = lax.optimization_barrier((far, near_up, near_down))
    near_across = from_ring(near_up, "x", 1)
    far_up, far_down = from_ring(far, "x", 1), from_ring(far, "x", -1)
    far_across = from_ring(far_down, "x", -1)
    return near, near_up, near_across, near_down, far, far_up, far_across, far_down


def both_cores(blocks):
    parts = []
    for one in blocks:
        parts += [one, from_ring(one, "core", 1)]
    return tuple(parts)


def shards(inputs_down, inputs_up, w_in, w_out):
    y, zh, dp = lax.axis_index("y"), lax.axis_index("zh"), lax.axis_index(DP)
    low_half = y < 2
    stage_p = (y == 0) | (y == 3)

    def own(layer_slot):
        parts = [
            lax.dynamic_slice(w, (0, layer_slot, dp * (D // 16), 0), (1, 1, D // 16, R))[0, 0]
            for w in (w_in, w_out)
        ]
        return jnp.stack(parts)

    def gathered(own_part):
        return lax.all_gather(own_part, ("zh",) + DP).reshape(SET, 16, 2, D // 16, R)

    def own_half(layer_slot):
        core = lax.axis_index("core")
        parts = [
            lax.dynamic_slice(w, (0, layer_slot, core * (D // 2), 0), (1, 1, D // 2, R))[0, 0]
            for w in (w_in, w_out)
        ]
        return jnp.stack(parts).reshape(2, 8, D // 16, R)

    first_slot = jnp.where(low_half, 0, 1)
    own_layers = tuple(w[0].reshape(2, 16, D // 16, R) for w in (w_in, w_out))
    half_own, chunk_a = lax.optimization_barrier((own_half(first_slot), own(first_slot)))
    half_a = across_y(half_own)
    chunk_b, near_a = lax.optimization_barrier((own(1 - first_slot), over_z(chunk_a)))
    w_b = (gathered(chunk_b),)
    blocks = list(over_x(near_a))
    half_a, blocks[2], *blocks[5:7] = lax.optimization_barrier((half_a, blocks[2], *blocks[5:7]))
    w_a = own_layers + both_cores([half_a] + blocks)

    def flag(active, slot_now):
        reverse = slot_now == 1
        here = [lax.axis_index(name) for name in ("zh",) + DP]
        return jnp.stack([v.astype(jnp.int32) for v in [active, reverse, slot_now] + here])

    p_a, p_b = flag(stage_p, first_slot), flag(stage_p, 1 - first_slot)
    q_a, q_b = flag(~stage_p, first_slot), flag(~stage_p, 1 - first_slot)

    mine = jnp.where(low_half, inputs_down, inputs_up).reshape(-1, D)
    mine = lax.dynamic_slice(mine, (zh * REAL, 0), (REAL, D))
    rows = jnp.pad(mine, ((0, ROWS - REAL), (0, 0)))

    rows, h_a, pre_a, act_a = run_forward(p_a, rows, w_a)
    rows = hop(rows)
    rows, h_a, pre_a, act_a = run_forward(q_a, rows, w_a, (h_a, pre_a, act_a))
    rows, h_b, pre_b, act_b = run_forward(q_b, rows, w_b)
    rows = hop(rows)
    rows, h_b, pre_b, act_b = run_forward(p_b, rows, w_b, (h_b, pre_b, act_b))
    act_all = lax.all_gather(jnp.concatenate([act_a, act_b], axis=0), DP)
    rows, g_b = run_backward(p_b, rows, w_b, h_b, pre_b, from_final=True)
    rows = hop(rows)
    rows, g_b = run_backward(q_b, rows, w_b, h_b, pre_b, held=g_b)
    rows, g_a = run_backward(q_a, rows, w_a, h_a, pre_a)
    rows, act_all = lax.optimization_barrier((rows, act_all))
    rows = hop(rows)
    place = zh.astype(jnp.int32)[None]
    parts_b = run_grad(place, spread(g_b), act_all, SET)
    rows, parts_b = lax.optimization_barrier((rows, parts_b))
    rows, g_a = run_backward(p_a, rows, w_a, h_a, pre_a, held=g_a, last=True)
    g_a, sum_b = lax.optimization_barrier((g_a, summed_over_zh(parts_b)))
    sum_a = summed_over_zh(run_grad(place, spread(g_a), act_all, 0))
    kept = jnp.where(low_half, sum_a, sum_b)
    other = jnp.where(low_half, sum_b, sum_a)
    received = across_y(other)
    return (kept.astype(jnp.float32) + received.astype(jnp.float32))[None]


def solution(mesh):
    fine = Mesh(mesh.devices.reshape(4, 4, 2, 4, 2), GRID_AXES)
    section = ("y", "zh")
    placed = (
        P(DP, None, None),
        P(DP, None, None),
        P(section, None, None, None),
        P(section, None, None, None),
    )
    return jax.shard_map(
        shards, mesh=fine, in_specs=placed, out_specs=P(section, DP, None), check_vma=False
    )
```

```python
import jax
import jax.numpy as jnp
from jax import lax
from jax.experimental import pallas as pl
from jax.experimental.pallas import tpu as pltpu
from jax.sharding import Mesh, PartitionSpec as P

EPS = 1e-06
COT = 0.0625
D, R = 5120, 256
REAL, ROWS = 18, 24
SET = 4
CH = 4
CW = D // CH
DP = ("zl", "x", "core")
GRID_AXES = ("y", "zh", "zl", "x", "core")
ANY = pl.BlockSpec(memory_space=pl.ANY)
VM = pl.BlockSpec(memory_space=pltpu.VMEM)
SM = pl.BlockSpec(memory_space=pltpu.SMEM)


class Gathered:
    count = 1

    def __init__(self, refs, flags, wbuf, sem):
        self.w, self.flags, self.wbuf, self.sem = refs[0], flags, wbuf, sem

    def copy(self, layer, slot, which):
        held = jnp.where(self.flags[1] == 1, SET - 1 - layer, layer)
        return pltpu.make_async_copy(
            self.w.at[held, :, which], self.wbuf.at[slot, :, which], self.sem.at[slot, which]
        )

    def first(self, layer, order):
        self.order = order
        self.begin(layer, 0)

    def begin(self, layer, slot):
        for which in self.order:
            self.copy(layer, slot, which).start()

    def arrive(self, layer, slot, which):
        self.copy(layer, slot, which).wait()


class Scattered:
    count = 20

    def __init__(self, refs, flags, wbuf, sem):
        self.own, self.halves, self.parts = refs[:2], refs[2:4], refs[4:]
        self.flags, self.wbuf, self.sem = flags, wbuf, sem

    def fetch(self, layer, slot):
        flags = self.flags
        held = jnp.where(flags[1] == 1, SET - 1 - layer, layer)
        zh = flags[3]
        away = lax.rem(held + SET - zh, SET)
        mirrored = held == SET - 1 - zh

        @pl.when(away == 0)
        def _():
            for which in range(2):
                pltpu.make_async_copy(
                    self.own[which].at[flags[2]], self.wbuf.at[slot, :, which], self.sem.at[slot, 0]
                ).start()

        @pl.when(mirrored)
        def _():
            for n in range(2):
                half = lax.rem(flags[6] + n, 2)
                for which in range(2):
                    pltpu.make_async_copy(
                        self.halves[n].at[which],
                        self.wbuf.at[slot, pl.ds(half * 8, 8), which],
                        self.sem.at[slot, 0],
                    ).start()

        @pl.when((away > 0) & jnp.logical_not(mirrored))
        def _():
            entry = jnp.where(away == 2, 1, 0)
            for n in range(16):
                zl_off, x_off, core_off = n // 8, (n // 2) % 4, n % 2
                zl = lax.rem(flags[4] + zl_off, 2)
                x = lax.rem(flags[5] + x_off, 4)
                core = lax.rem(flags[6] + core_off, 2)
                pltpu.make_async_copy(
                    self.parts[n].at[entry],
                    self.wbuf.at[slot, zl * 8 + x * 2 + core],
                    self.sem.at[slot, 0],
                ).start()

    def first(self, layer, order):
        self.leading = order[0]
        self.fetch(layer, 0)

    def begin(self, layer, slot):
        self.fetch(layer, slot)

    def arrive(self, layer, slot, which):
        if which == self.leading:
            pltpu.make_async_copy(
                self.wbuf.at[1 - slot], self.wbuf.at[slot], self.sem.at[slot, 0]
            ).wait()


def chunk(wbuf, slot, which, c):
    per = 16 // CH
    return wbuf[slot, c * per : (c + 1) * per, which].reshape(CW, R)


def columns(c):
    return slice(c * CW, (c + 1) * CW)


def inverse_rms(hbuf, layer):
    total = jnp.zeros((ROWS, 1), jnp.float32)
    for c in range(CH):
        v = hbuf[layer, :, columns(c)].astype(jnp.float32)
        total = total + jnp.sum(v * v, axis=-1, keepdims=True)
    return lax.rsqrt(total * (1.0 / D) + EPS)


def forward_kernel(*refs, source, aliased):
    flags, x_ref = refs[:2]
    w_refs = refs[2 : 2 + source.count]
    refs = refs[2 + source.count + (3 if aliased else 0) :]
    y_ref, h_out, pre_out, act_out = refs[:4]
    wbuf, hbuf, prebuf, actbuf, sem_w, sem_h, sem_p, sem_a = refs[4:]

    @pl.when(flags[0] == 1)
    def _():
        weights = source(w_refs, flags, wbuf, sem_w)
        weights.first(0, (0, 1))
        hbuf[0] = x_ref[...]

        def step(layer, carry):
            slot = lax.rem(layer, 2)


            @pl.when(layer + 1 < SET)
            def _():
                weights.begin(layer + 1, 1 - slot)

            pltpu.make_async_copy(hbuf.at[layer], h_out.at[layer], sem_h.at[layer]).start()
            inv = inverse_rms(hbuf, layer)
            pre = jnp.zeros((ROWS, R), jnp.float32)
            weights.arrive(layer, slot, 0)
            for c in range(CH):
                normed = (hbuf[layer, :, columns(c)].astype(jnp.float32) * inv).astype(jnp.bfloat16)
                pre = pre + jnp.dot(
                    normed, chunk(wbuf, slot, 0, c), preferred_element_type=jnp.float32
                )
            active = (pre / (1.0 + jnp.exp(-pre))).astype(jnp.bfloat16)
            prebuf[layer] = pre
            actbuf[layer] = active
            weights.arrive(layer, slot, 1)
            for c in range(CH):
                branch = lax.dot_general(
                    active,
                    chunk(wbuf, slot, 1, c),
                    (((1,), (1,)), ((), ())),
                    preferred_element_type=jnp.float32,
                )
                before = hbuf[layer, :, columns(c)].astype(jnp.float32)
                hbuf[layer + 1, :, columns(c)] = (before + branch).astype(jnp.bfloat16)
            return carry

        lax.fori_loop(0, SET, step, 0)
        y_ref[...] = hbuf[SET]
        copies = [
            pltpu.make_async_copy(prebuf, pre_out, sem_p.at[0]),
            pltpu.make_async_copy(actbuf, act_out, sem_a.at[0]),
        ]
        for one in copies:
            one.start()
        for layer in range(SET):
            copies.append(
                pltpu.make_async_copy(hbuf.at[layer], h_out.at[layer], sem_h.at[layer])
            )
        for one in copies:
            one.wait()


def run_forward(flags, rows, weights, held=None):
    source = Gathered if len(weights) == 1 else Scattered
    first = 2 + source.count
    outs = (
        jax.ShapeDtypeStruct((ROWS, D), jnp.bfloat16),
        jax.ShapeDtypeStruct((SET, ROWS, D), jnp.bfloat16),
        jax.ShapeDtypeStruct((SET, ROWS, R), jnp.float32),
        jax.ShapeDtypeStruct((SET, ROWS, R), jnp.bfloat16),
    )
    aliased = held is not None
    return pl.pallas_call(
        lambda *refs: forward_kernel(*refs, source=source, aliased=aliased),
        out_shape=outs,
        in_specs=[SM, VM] + [ANY] * (source.count + (3 if aliased else 0)),
        out_specs=(VM, ANY, ANY, ANY),
        scratch_shapes=[
            pltpu.VMEM((2, 16, 2, D // 16, R), jnp.bfloat16),
            pltpu.VMEM((SET + 1, ROWS, D), jnp.bfloat16),
            pltpu.VMEM((SET, ROWS, R), jnp.float32),
            pltpu.VMEM((SET, ROWS, R), jnp.bfloat16),
            pltpu.SemaphoreType.DMA((2, 2)),
            pltpu.SemaphoreType.DMA((SET,)),
            pltpu.SemaphoreType.DMA((1,)),
            pltpu.SemaphoreType.DMA((1,)),
        ],
        input_output_aliases={first: 1, first + 1: 2, first + 2: 3} if aliased else {},
        compiler_params=pltpu.CompilerParams(vmem_limit_bytes=52 * 2**20),
        cost_estimate=pl.CostEstimate(
            flops=SET * ROWS * D * R, bytes_accessed=SET * D * R, transcendentals=0
        ),
        name="forward_set",
    )(flags, rows, *weights, *(held or ()))


def backward_kernel(*refs, source, aliased, from_final, last):
    flags, g_ref, h_in, pre_in = refs[:4]
    w_refs = refs[4 : 4 + source.count]
    refs = refs[4 + source.count + (1 if aliased else 0) :]
    y_ref, g_out = refs[:2]
    wbuf, hbuf, prebuf, gbuf, dnbuf, gcut, sem_w, sem_h, sem_p, sem_g = refs[2:]

    @pl.when(flags[0] == 1)
    def _():
        weights = source(w_refs, flags, wbuf, sem_w)

        def g_copy(step):
            return pltpu.make_async_copy(
                gcut.at[:, step], g_out.at[:, SET - 1 - step], sem_g.at[step]
            )

        def g_send(step):
            for r in range(16):
                gcut[r, step] = gbuf[step, :, r * (D // 16) : (r + 1) * (D // 16)]
            g_copy(step).start()

        def h_copy(layer):
            return pltpu.make_async_copy(h_in.at[layer], hbuf.at[layer], sem_h.at[layer])

        pre_copy = pltpu.make_async_copy(pre_in, prebuf, sem_p.at[0])
        pre_copy.start()
        h_copy(SET - 1).start()
        weights.first(SET - 1, (1, 0))
        for layer in range(SET - 2, -1, -1):
            h_copy(layer).start()
        if from_final:
            gbuf[0] = (g_ref[...].astype(jnp.float32) * COT).astype(jnp.bfloat16)
        else:
            gbuf[0] = g_ref[...]
        pre_copy.wait()
        steps = SET - 1 if last else SET

        def one_layer(step, carry):
            layer = SET - 1 - step
            slot = lax.rem(step, 2)


            @pl.when(step + 1 < steps)
            def _():
                weights.begin(layer - 1, 1 - slot)

            g_send(step)
            h_copy(layer).wait()
            inv = inverse_rms(hbuf, layer)
            pre = prebuf[layer]
            sigma = 1.0 / (1.0 + jnp.exp(-pre))
            slope = sigma * (1.0 + pre * (1.0 - sigma))
            d_active = jnp.zeros((ROWS, R), jnp.float32)
            weights.arrive(layer, slot, 1)
            for c in range(CH):
                d_active = d_active + jnp.dot(
                    gbuf[step, :, columns(c)],
                    chunk(wbuf, slot, 1, c),
                    preferred_element_type=jnp.float32,
                )
            d_pre = (d_active * slope).astype(jnp.bfloat16)
            total = jnp.zeros((ROWS, 1), jnp.float32)
            weights.arrive(layer, slot, 0)
            for c in range(CH):
                d_normed = lax.dot_general(
                    d_pre,
                    chunk(wbuf, slot, 0, c),
                    (((1,), (1,)), ((), ())),
                    preferred_element_type=jnp.float32,
                )
                unit = hbuf[layer, :, columns(c)].astype(jnp.float32) * inv
                total = total + jnp.sum(d_normed * unit, axis=-1, keepdims=True)
                dnbuf[:, columns(c)] = d_normed
            mean = total * (1.0 / D)
            for c in range(CH):
                unit = hbuf[layer, :, columns(c)].astype(jnp.float32) * inv
                moved = inv * (dnbuf[:, columns(c)] - unit * mean)
                before = gbuf[step, :, columns(c)].astype(jnp.float32)
                gbuf[step + 1, :, columns(c)] = (before + moved).astype(jnp.bfloat16)
            return carry

        lax.fori_loop(0, steps, one_layer, 0)
        if last:
            g_send(SET - 1)
            h_copy(0).wait()
        y_ref[...] = gbuf[steps]
        for step in range(SET):
            g_copy(step).wait()


def run_backward(flags, g_rows, weights, h_held, pre_held, held=None, from_final=False, last=False):
    source = Gathered if len(weights) == 1 else Scattered
    outs = (
        jax.ShapeDtypeStruct((ROWS, D), jnp.bfloat16),
        jax.ShapeDtypeStruct((16, SET, ROWS, D // 16), jnp.bfloat16),
    )
    aliased = held is not None
    return pl.pallas_call(
        lambda *refs: backward_kernel(
            *refs, source=source, aliased=aliased, from_final=from_final, last=last
        ),
        out_shape=outs,
        in_specs=[SM, VM, ANY, ANY] + [ANY] * (source.count + (1 if aliased else 0)),
        out_specs=(VM, ANY),
        scratch_shapes=[
            pltpu.VMEM((2, 16, 2, D // 16, R), jnp.bfloat16),
            pltpu.VMEM((SET, ROWS, D), jnp.bfloat16),
            pltpu.VMEM((SET, ROWS, R), jnp.float32),
            pltpu.VMEM((SET + 1, ROWS, D), jnp.bfloat16),
            pltpu.VMEM((ROWS, D), jnp.float32),
            pltpu.VMEM((16, SET, ROWS, D // 16), jnp.bfloat16),
            pltpu.SemaphoreType.DMA((2, 2)),
            pltpu.SemaphoreType.DMA((SET,)),
            pltpu.SemaphoreType.DMA((1,)),
            pltpu.SemaphoreType.DMA((SET,)),
        ],
        input_output_aliases={4 + source.count: 1} if aliased else {},
        compiler_params=pltpu.CompilerParams(vmem_limit_bytes=52 * 2**20),
        cost_estimate=pl.CostEstimate(
            flops=SET * ROWS * D * R, bytes_accessed=SET * D * R, transcendentals=0
        ),
        name="backward_set",
    )(flags, g_rows, h_held, pre_held, *weights, *((held,) if aliased else ()))


def grad_kernel(place, g_ref, act_ref, *out_refs, first):
    for k in range(SET):
        layer = lax.rem(place[0] + k, SET)
        g = g_ref[:, layer].reshape(16 * ROWS, D // 16)
        act = act_ref[:, first + layer].reshape(16 * ROWS, R)
        out_refs[k][...] = lax.dot_general(
            g, act, (((0,), (0,)), ((), ())), preferred_element_type=jnp.float32
        ).astype(jnp.bfloat16)


def run_grad(place, g_all, act_all, first):
    return pl.pallas_call(
        lambda *refs: grad_kernel(*refs, first=first),
        out_shape=(jax.ShapeDtypeStruct((D // 16, R), jnp.bfloat16),) * SET,
        in_specs=[SM, VM, VM],
        out_specs=(VM,) * SET,
        compiler_params=pltpu.CompilerParams(vmem_limit_bytes=52 * 2**20),
        name="grad_set",
    )(place, g_all, act_all)


def summed_over_zh(parts):
    total = parts[0].astype(jnp.float32)
    for k in range(1, SET):
        route = [(source, (source + k) % SET) for source in range(SET)]
        total = total + lax.ppermute(parts[k], "zh", route).astype(jnp.float32)
    return total.astype(jnp.bfloat16)


def hop(rows):
    return lax.ppermute(rows, "y", [(0, 1), (1, 0), (2, 3), (3, 2)])


def spread(g_set):
    return lax.all_to_all(g_set, DP, 0, 0)


def from_ring(block, axis, away):
    count = lax.axis_size(axis)
    return lax.ppermute(block, axis, [((d + away) % count, d) for d in range(count)])


def across_y(block):
    return lax.ppermute(block, "y", [(0, 3), (3, 0), (1, 2), (2, 1)])


def over_z(chunk_now):
    beside = lax.ppermute(chunk_now, "zh", [(0, 1), (1, 0), (2, 3), (3, 2)])
    route = []
    for y in range(4):
        for zh in range(4):
            route.append((y * 4 + zh, (3 - y) * 4 + (zh ^ 1)))
    return jnp.stack([beside, lax.ppermute(chunk_now, ("y", "zh"), route)])


def over_x(near):
    far = from_ring(near, "zl", 1)
    near_up, near_down = from_ring(near, "x", 1), from_ring(near, "x", -1)
    far, near_up, near_down = lax.optimization_barrier((far, near_up, near_down))
    near_across = from_ring(near_up, "x", 1)
    far_up, far_down = from_ring(far, "x", 1), from_ring(far, "x", -1)
    far_across = from_ring(far_down, "x", -1)
    return near, near_up, near_across, near_down, far, far_up, far_across, far_down


def both_cores(blocks):
    parts = []
    for one in blocks:
        parts += [one, from_ring(one, "core", 1)]
    return tuple(parts)


def shards(inputs_down, inputs_up, w_in, w_out):
    y, zh, dp = lax.axis_index("y"), lax.axis_index("zh"), lax.axis_index(DP)
    low_half = y < 2
    stage_p = (y == 0) | (y == 3)

    def own(layer_slot):
        parts = [
            lax.dynamic_slice(w, (0, layer_slot, dp * (D // 16), 0), (1, 1, D // 16, R))[0, 0]
            for w in (w_in, w_out)
        ]
        return jnp.stack(parts)

    def gathered(own_part):
        return lax.all_gather(own_part, ("zh",) + DP).reshape(SET, 16, 2, D // 16, R)

    def own_half(layer_slot):
        core = lax.axis_index("core")
        parts = [
            lax.dynamic_slice(w, (0, layer_slot, core * (D // 2), 0), (1, 1, D // 2, R))[0, 0]
            for w in (w_in, w_out)
        ]
        return jnp.stack(parts).reshape(2, 8, D // 16, R)

    first_slot = jnp.where(low_half, 0, 1)
    own_layers = tuple(w[0].reshape(2, 16, D // 16, R) for w in (w_in, w_out))
    half_own, chunk_a = lax.optimization_barrier((own_half(first_slot), own(first_slot)))
    half_a = across_y(half_own)
    chunk_b, near_a = lax.optimization_barrier((own(1 - first_slot), over_z(chunk_a)))
    w_b = (gathered(chunk_b),)
    blocks = list(over_x(near_a))
    early = both_cores([blocks[0], blocks[1], blocks[3], blocks[4]])
    half_a, early, blocks[2], *blocks[5:7] = lax.optimization_barrier(
        (half_a, early, blocks[2], *blocks[5:7])
    )
    late = both_cores([half_a, blocks[2]] + blocks[5:])
    w_a = own_layers + late[:2] + early[:4] + late[2:4] + early[4:] + late[4:]

    def flag(active, slot_now):
        reverse = slot_now == 1
        here = [lax.axis_index(name) for name in ("zh",) + DP]
        return jnp.stack([v.astype(jnp.int32) for v in [active, reverse, slot_now] + here])

    p_a, p_b = flag(stage_p, first_slot), flag(stage_p, 1 - first_slot)
    q_a, q_b = flag(~stage_p, first_slot), flag(~stage_p, 1 - first_slot)

    mine = jnp.where(low_half, inputs_down, inputs_up).reshape(-1, D)
    mine = lax.dynamic_slice(mine, (zh * REAL, 0), (REAL, D))
    rows = jnp.pad(mine, ((0, ROWS - REAL), (0, 0)))

    rows, h_a, pre_a, act_a = run_forward(p_a, rows, w_a)
    rows = hop(rows)
    rows, h_a, pre_a, act_a = run_forward(q_a, rows, w_a, (h_a, pre_a, act_a))
    rows, h_b, pre_b, act_b = run_forward(q_b, rows, w_b)
    rows = hop(rows)
    rows, h_b, pre_b, act_b = run_forward(p_b, rows, w_b, (h_b, pre_b, act_b))
    act_all = lax.all_gather(jnp.concatenate([act_a, act_b], axis=0), DP)
    rows, g_b = run_backward(p_b, rows, w_b, h_b, pre_b, from_final=True)
    rows = hop(rows)
    rows, g_b = run_backward(q_b, rows, w_b, h_b, pre_b, held=g_b)
    rows, g_a = run_backward(q_a, rows, w_a, h_a, pre_a)
    rows, act_all = lax.optimization_barrier((rows, act_all))
    rows = hop(rows)
    place = zh.astype(jnp.int32)[None]
    parts_b = run_grad(place, spread(g_b), act_all, SET)
    rows, parts_b = lax.optimization_barrier((rows, parts_b))
    rows, g_a = run_backward(p_a, rows, w_a, h_a, pre_a, held=g_a, last=True)
    g_a, sum_b = lax.optimization_barrier((g_a, summed_over_zh(parts_b)))
    sum_a = summed_over_zh(run_grad(place, spread(g_a), act_all, 0))
    kept = jnp.where(low_half, sum_a, sum_b)
    other = jnp.where(low_half, sum_b, sum_a)
    received = across_y(other)
    return (kept.astype(jnp.float32) + received.astype(jnp.float32))[None]


def solution(mesh):
    fine = Mesh(mesh.devices.reshape(4, 4, 2, 4, 2), GRID_AXES)
    section = ("y", "zh")
    placed = (
        P(DP, None, None),
        P(DP, None, None),
        P(section, None, None, None),
        P(section, None, None, None),
    )
    return jax.shard_map(
        shards, mesh=fine, in_specs=placed, out_specs=P(section, DP, None), check_vma=False
    )
```

```python
import jax
import jax.numpy as jnp
from jax import lax
from jax.experimental import pallas as pl
from jax.experimental.pallas import tpu as pltpu
from jax.sharding import Mesh, PartitionSpec as P

EPS = 1e-06
COT = 0.0625
D, R = 5120, 256
REAL, ROWS = 18, 24
SET = 4
CH = 4
CW = D // CH
DP = ("zl", "x", "core")
GRID_AXES = ("y", "zh", "zl", "x", "core")
ANY = pl.BlockSpec(memory_space=pl.ANY)
VM = pl.BlockSpec(memory_space=pltpu.VMEM)
SM = pl.BlockSpec(memory_space=pltpu.SMEM)


class Gathered:
    count = 1

    def __init__(self, refs, flags, wbuf, sem):
        self.w, self.flags, self.wbuf, self.sem = refs[0], flags, wbuf, sem

    def copy(self, layer, slot, which):
        held = jnp.where(self.flags[1] == 1, SET - 1 - layer, layer)
        return pltpu.make_async_copy(
            self.w.at[held, :, which], self.wbuf.at[slot, :, which], self.sem.at[slot, which]
        )

    def first(self, layer, order):
        self.order = order
        self.begin(layer, 0)

    def begin(self, layer, slot):
        for which in self.order:
            self.copy(layer, slot, which).start()

    def arrive(self, layer, slot, which):
        self.copy(layer, slot, which).wait()


class Scattered:
    count = 20

    def __init__(self, refs, flags, wbuf, sem):
        self.own, self.halves, self.parts = refs[:2], refs[2:4], refs[4:]
        self.flags, self.wbuf, self.sem = flags, wbuf, sem

    def fetch(self, layer, slot):
        flags = self.flags
        held = jnp.where(flags[1] == 1, SET - 1 - layer, layer)
        zh = flags[3]
        away = lax.rem(held + SET - zh, SET)
        mirrored = held == SET - 1 - zh

        @pl.when(away == 0)
        def _():
            for which in range(2):
                pltpu.make_async_copy(
                    self.own[which].at[flags[2]], self.wbuf.at[slot, :, which], self.sem.at[slot, 0]
                ).start()

        @pl.when(mirrored)
        def _():
            for n in range(2):
                half = lax.rem(flags[6] + n, 2)
                for which in range(2):
                    pltpu.make_async_copy(
                        self.halves[n].at[which],
                        self.wbuf.at[slot, pl.ds(half * 8, 8), which],
                        self.sem.at[slot, 0],
                    ).start()

        @pl.when((away > 0) & jnp.logical_not(mirrored))
        def _():
            entry = jnp.where(away == 2, 1, 0)
            for n in range(16):
                zl_off, x_off, core_off = n // 8, (n // 2) % 4, n % 2
                zl = lax.rem(flags[4] + zl_off, 2)
                x = lax.rem(flags[5] + x_off, 4)
                core = lax.rem(flags[6] + core_off, 2)
                pltpu.make_async_copy(
                    self.parts[n].at[entry],
                    self.wbuf.at[slot, zl * 8 + x * 2 + core],
                    self.sem.at[slot, 0],
                ).start()

    def first(self, layer, order):
        self.leading = order[0]
        self.fetch(layer, 0)

    def begin(self, layer, slot):
        self.fetch(layer, slot)

    def arrive(self, layer, slot, which):
        if which == self.leading:
            pltpu.make_async_copy(
                self.wbuf.at[1 - slot], self.wbuf.at[slot], self.sem.at[slot, 0]
            ).wait()


def chunk(wbuf, slot, which, c):
    per = 16 // CH
    return wbuf[slot, c * per : (c + 1) * per, which].reshape(CW, R)


def columns(c):
    return slice(c * CW, (c + 1) * CW)


def inverse_rms(hbuf, layer):
    total = jnp.zeros((ROWS, 1), jnp.float32)
    for c in range(CH):
        v = hbuf[layer, :, columns(c)].astype(jnp.float32)
        total = total + jnp.sum(v * v, axis=-1, keepdims=True)
    return lax.rsqrt(total * (1.0 / D) + EPS)


def forward_kernel(*refs, source, aliased):
    flags, x_ref = refs[:2]
    w_refs = refs[2 : 2 + source.count]
    refs = refs[2 + source.count + (3 if aliased else 0) :]
    y_ref, h_out, pre_out, act_out = refs[:4]
    wbuf, hbuf, prebuf, actbuf, sem_w, sem_h, sem_p, sem_a = refs[4:]

    @pl.when(flags[0] == 1)
    def _():
        weights = source(w_refs, flags, wbuf, sem_w)
        weights.first(0, (0, 1))
        hbuf[0] = x_ref[...]

        def step(layer, carry):
            slot = lax.rem(layer, 2)


            @pl.when(layer + 1 < SET)
            def _():
                weights.begin(layer + 1, 1 - slot)

            pltpu.make_async_copy(hbuf.at[layer], h_out.at[layer], sem_h.at[layer]).start()
            inv = inverse_rms(hbuf, layer)
            pre = jnp.zeros((ROWS, R), jnp.float32)
            weights.arrive(layer, slot, 0)
            for c in range(CH):
                normed = (hbuf[layer, :, columns(c)].astype(jnp.float32) * inv).astype(jnp.bfloat16)
                pre = pre + jnp.dot(
                    normed, chunk(wbuf, slot, 0, c), preferred_element_type=jnp.float32
                )
            active = (pre / (1.0 + jnp.exp(-pre))).astype(jnp.bfloat16)
            prebuf[layer] = pre
            actbuf[layer] = active
            weights.arrive(layer, slot, 1)
            for c in range(CH):
                branch = lax.dot_general(
                    active,
                    chunk(wbuf, slot, 1, c),
                    (((1,), (1,)), ((), ())),
                    preferred_element_type=jnp.float32,
                )
                before = hbuf[layer, :, columns(c)].astype(jnp.float32)
                hbuf[layer + 1, :, columns(c)] = (before + branch).astype(jnp.bfloat16)
            return carry

        lax.fori_loop(0, SET, step, 0)
        y_ref[...] = hbuf[SET]
        copies = [
            pltpu.make_async_copy(prebuf, pre_out, sem_p.at[0]),
            pltpu.make_async_copy(actbuf, act_out, sem_a.at[0]),
        ]
        for one in copies:
            one.start()
        for layer in range(SET):
            copies.append(
                pltpu.make_async_copy(hbuf.at[layer], h_out.at[layer], sem_h.at[layer])
            )
        for one in copies:
            one.wait()


def run_forward(flags, rows, weights, held=None):
    source = Gathered if len(weights) == 1 else Scattered
    first = 2 + source.count
    outs = (
        jax.ShapeDtypeStruct((ROWS, D), jnp.bfloat16),
        jax.ShapeDtypeStruct((SET, ROWS, D), jnp.bfloat16),
        jax.ShapeDtypeStruct((SET, ROWS, R), jnp.float32),
        jax.ShapeDtypeStruct((SET, ROWS, R), jnp.bfloat16),
    )
    aliased = held is not None
    return pl.pallas_call(
        lambda *refs: forward_kernel(*refs, source=source, aliased=aliased),
        out_shape=outs,
        in_specs=[SM, VM] + [ANY] * (source.count + (3 if aliased else 0)),
        out_specs=(VM, ANY, ANY, ANY),
        scratch_shapes=[
            pltpu.VMEM((2, 16, 2, D // 16, R), jnp.bfloat16),
            pltpu.VMEM((SET + 1, ROWS, D), jnp.bfloat16),
            pltpu.VMEM((SET, ROWS, R), jnp.float32),
            pltpu.VMEM((SET, ROWS, R), jnp.bfloat16),
            pltpu.SemaphoreType.DMA((2, 2)),
            pltpu.SemaphoreType.DMA((SET,)),
            pltpu.SemaphoreType.DMA((1,)),
            pltpu.SemaphoreType.DMA((1,)),
        ],
        input_output_aliases={first: 1, first + 1: 2, first + 2: 3} if aliased else {},
        compiler_params=pltpu.CompilerParams(vmem_limit_bytes=52 * 2**20),
        cost_estimate=pl.CostEstimate(
            flops=SET * ROWS * D * R, bytes_accessed=SET * D * R, transcendentals=0
        ),
        name="forward_set",
    )(flags, rows, *weights, *(held or ()))


def backward_kernel(*refs, source, aliased, from_final, last):
    flags, g_ref, h_in, pre_in = refs[:4]
    w_refs = refs[4 : 4 + source.count]
    refs = refs[4 + source.count + (1 if aliased else 0) :]
    y_ref, g_out = refs[:2]
    wbuf, hbuf, prebuf, gbuf, dnbuf, gcut, sem_w, sem_h, sem_p, sem_g = refs[2:]

    @pl.when(flags[0] == 1)
    def _():
        weights = source(w_refs, flags, wbuf, sem_w)

        def g_copy(step):
            return pltpu.make_async_copy(
                gcut.at[:, step], g_out.at[:, SET - 1 - step], sem_g.at[step]
            )

        def g_send(step):
            for r in range(16):
                gcut[r, step] = gbuf[step, :, r * (D // 16) : (r + 1) * (D // 16)]
            g_copy(step).start()

        def h_copy(layer):
            return pltpu.make_async_copy(h_in.at[layer], hbuf.at[layer], sem_h.at[layer])

        pre_copy = pltpu.make_async_copy(pre_in, prebuf, sem_p.at[0])
        pre_copy.start()
        h_copy(SET - 1).start()
        weights.first(SET - 1, (1, 0))
        for layer in range(SET - 2, -1, -1):
            h_copy(layer).start()
        if from_final:
            gbuf[0] = (g_ref[...].astype(jnp.float32) * COT).astype(jnp.bfloat16)
        else:
            gbuf[0] = g_ref[...]
        pre_copy.wait()
        steps = SET - 1 if last else SET

        def one_layer(step, carry):
            layer = SET - 1 - step
            slot = lax.rem(step, 2)


            @pl.when(step + 1 < steps)
            def _():
                weights.begin(layer - 1, 1 - slot)

            g_send(step)
            h_copy(layer).wait()
            inv = inverse_rms(hbuf, layer)
            pre = prebuf[layer]
            sigma = 1.0 / (1.0 + jnp.exp(-pre))
            slope = sigma * (1.0 + pre * (1.0 - sigma))
            d_active = jnp.zeros((ROWS, R), jnp.float32)
            weights.arrive(layer, slot, 1)
            for c in range(CH):
                d_active = d_active + jnp.dot(
                    gbuf[step, :, columns(c)],
                    chunk(wbuf, slot, 1, c),
                    preferred_element_type=jnp.float32,
                )
            d_pre = (d_active * slope).astype(jnp.bfloat16)
            total = jnp.zeros((ROWS, 1), jnp.float32)
            weights.arrive(layer, slot, 0)
            for c in range(CH):
                d_normed = lax.dot_general(
                    d_pre,
                    chunk(wbuf, slot, 0, c),
                    (((1,), (1,)), ((), ())),
                    preferred_element_type=jnp.float32,
                )
                unit = hbuf[layer, :, columns(c)].astype(jnp.float32) * inv
                total = total + jnp.sum(d_normed * unit, axis=-1, keepdims=True)
                dnbuf[:, columns(c)] = d_normed
            mean = total * (1.0 / D)
            for c in range(CH):
                unit = hbuf[layer, :, columns(c)].astype(jnp.float32) * inv
                moved = inv * (dnbuf[:, columns(c)] - unit * mean)
                before = gbuf[step, :, columns(c)].astype(jnp.float32)
                gbuf[step + 1, :, columns(c)] = (before + moved).astype(jnp.bfloat16)
            return carry

        lax.fori_loop(0, steps, one_layer, 0)
        if last:
            g_send(SET - 1)
            h_copy(0).wait()
        y_ref[...] = gbuf[steps]
        for step in range(SET):
            g_copy(step).wait()


def run_backward(flags, g_rows, weights, h_held, pre_held, held=None, from_final=False, last=False):
    source = Gathered if len(weights) == 1 else Scattered
    outs = (
        jax.ShapeDtypeStruct((ROWS, D), jnp.bfloat16),
        jax.ShapeDtypeStruct((16, SET, ROWS, D // 16), jnp.bfloat16),
    )
    aliased = held is not None
    return pl.pallas_call(
        lambda *refs: backward_kernel(
            *refs, source=source, aliased=aliased, from_final=from_final, last=last
        ),
        out_shape=outs,
        in_specs=[SM, VM, ANY, ANY] + [ANY] * (source.count + (1 if aliased else 0)),
        out_specs=(VM, ANY),
        scratch_shapes=[
            pltpu.VMEM((2, 16, 2, D // 16, R), jnp.bfloat16),
            pltpu.VMEM((SET, ROWS, D), jnp.bfloat16),
            pltpu.VMEM((SET, ROWS, R), jnp.float32),
            pltpu.VMEM((SET + 1, ROWS, D), jnp.bfloat16),
            pltpu.VMEM((ROWS, D), jnp.float32),
            pltpu.VMEM((16, SET, ROWS, D // 16), jnp.bfloat16),
            pltpu.SemaphoreType.DMA((2, 2)),
            pltpu.SemaphoreType.DMA((SET,)),
            pltpu.SemaphoreType.DMA((1,)),
            pltpu.SemaphoreType.DMA((SET,)),
        ],
        input_output_aliases={4 + source.count: 1} if aliased else {},
        compiler_params=pltpu.CompilerParams(vmem_limit_bytes=52 * 2**20),
        cost_estimate=pl.CostEstimate(
            flops=SET * ROWS * D * R, bytes_accessed=SET * D * R, transcendentals=0
        ),
        name="backward_set",
    )(flags, g_rows, h_held, pre_held, *weights, *((held,) if aliased else ()))


def grad_kernel(place, g_ref, act_ref, *out_refs, first):
    for k in range(SET):
        layer = lax.rem(place[0] + k, SET)
        g = g_ref[:, layer].reshape(16 * ROWS, D // 16)
        act = act_ref[:, first + layer].reshape(16 * ROWS, R)
        out_refs[k][...] = lax.dot_general(
            g, act, (((0,), (0,)), ((), ())), preferred_element_type=jnp.float32
        ).astype(jnp.bfloat16)


def run_grad(place, g_all, act_all, first):
    return pl.pallas_call(
        lambda *refs: grad_kernel(*refs, first=first),
        out_shape=(jax.ShapeDtypeStruct((D // 16, R), jnp.bfloat16),) * SET,
        in_specs=[SM, VM, VM],
        out_specs=(VM,) * SET,
        compiler_params=pltpu.CompilerParams(vmem_limit_bytes=52 * 2**20),
        name="grad_set",
    )(place, g_all, act_all)


def summed_over_zh(parts):
    total = parts[0].astype(jnp.float32)
    for k in range(1, SET):
        route = [(source, (source + k) % SET) for source in range(SET)]
        total = total + lax.ppermute(parts[k], "zh", route).astype(jnp.float32)
    return total.astype(jnp.bfloat16)


def hop(rows):
    return lax.ppermute(rows, "y", [(0, 1), (1, 0), (2, 3), (3, 2)])


def spread(g_set):
    return lax.all_to_all(g_set, DP, 0, 0)


def from_ring(block, axis, away):
    count = lax.axis_size(axis)
    return lax.ppermute(block, axis, [((d + away) % count, d) for d in range(count)])


def across_y(block):
    return lax.ppermute(block, "y", [(0, 3), (3, 0), (1, 2), (2, 1)])


def over_z(chunk_now):
    beside = lax.ppermute(chunk_now, "zh", [(0, 1), (1, 0), (2, 3), (3, 2)])
    route = []
    for y in range(4):
        for zh in range(4):
            route.append((y * 4 + zh, (3 - y) * 4 + (zh ^ 1)))
    return jnp.stack([beside, lax.ppermute(chunk_now, ("y", "zh"), route)])


def over_x(near):
    far = from_ring(near, "zl", 1)
    near_up, near_down = from_ring(near, "x", 1), from_ring(near, "x", -1)
    far, near_up, near_down = lax.optimization_barrier((far, near_up, near_down))
    near_across = from_ring(near_up, "x", 1)
    far_up, far_down = from_ring(far, "x", 1), from_ring(far, "x", -1)
    far_across = from_ring(far_down, "x", -1)
    return near, near_up, near_across, near_down, far, far_up, far_across, far_down


def both_cores(blocks):
    parts = []
    for one in blocks:
        parts += [one, from_ring(one, "core", 1)]
    return tuple(parts)


def shards(inputs_down, inputs_up, w_in, w_out):
    y, zh, dp = lax.axis_index("y"), lax.axis_index("zh"), lax.axis_index(DP)
    low_half = y < 2
    stage_p = (y == 0) | (y == 3)

    def own(layer_slot):
        parts = [
            lax.dynamic_slice(w, (0, layer_slot, dp * (D // 16), 0), (1, 1, D // 16, R))[0, 0]
            for w in (w_in, w_out)
        ]
        return jnp.stack(parts)

    def gathered(own_part):
        return lax.all_gather(own_part, ("zh",) + DP).reshape(SET, 16, 2, D // 16, R)

    def own_half(layer_slot):
        core = lax.axis_index("core")
        parts = [
            lax.dynamic_slice(w, (0, layer_slot, core * (D // 2), 0), (1, 1, D // 2, R))[0, 0]
            for w in (w_in, w_out)
        ]
        return jnp.stack(parts).reshape(2, 8, D // 16, R)

    first_slot = jnp.where(low_half, 0, 1)
    own_layers = tuple(w[0].reshape(2, 16, D // 16, R) for w in (w_in, w_out))
    half_own, chunk_a = lax.optimization_barrier((own_half(first_slot), own(first_slot)))
    half_a = across_y(half_own)
    chunk_b, near_a = lax.optimization_barrier((own(1 - first_slot), over_z(chunk_a)))
    w_b = (gathered(chunk_b),)
    blocks = list(over_x(near_a))
    half_a, blocks[2], *blocks[5:7] = lax.optimization_barrier((half_a, blocks[2], *blocks[5:7]))
    w_a = own_layers + both_cores([half_a] + blocks)

    def flag(active, slot_now):
        reverse = slot_now == 1
        here = [lax.axis_index(name) for name in ("zh",) + DP]
        return jnp.stack([v.astype(jnp.int32) for v in [active, reverse, slot_now] + here])

    p_a, p_b = flag(stage_p, first_slot), flag(stage_p, 1 - first_slot)
    q_a, q_b = flag(~stage_p, first_slot), flag(~stage_p, 1 - first_slot)

    mine = jnp.where(low_half, inputs_down, inputs_up).reshape(-1, D)
    mine = lax.dynamic_slice(mine, (zh * REAL, 0), (REAL, D))
    rows = jnp.pad(mine, ((0, ROWS - REAL), (0, 0)))

    rows, h_a, pre_a, act_a = run_forward(p_a, rows, w_a)
    rows = hop(rows)
    rows, h_a, pre_a, act_a = run_forward(q_a, rows, w_a, (h_a, pre_a, act_a))
    rows, h_b, pre_b, act_b = run_forward(q_b, rows, w_b)
    rows = hop(rows)
    rows, h_b, pre_b, act_b = run_forward(p_b, rows, w_b, (h_b, pre_b, act_b))
    act_all = lax.all_gather(jnp.concatenate([act_a, act_b], axis=0), DP)
    rows, g_b = run_backward(p_b, rows, w_b, h_b, pre_b, from_final=True)
    rows = hop(rows)
    rows, g_b = run_backward(q_b, rows, w_b, h_b, pre_b, held=g_b)
    rows, g_a = run_backward(q_a, rows, w_a, h_a, pre_a)
    rows, act_all = lax.optimization_barrier((rows, act_all))
    rows = hop(rows)
    place = zh.astype(jnp.int32)[None]
    parts_b = run_grad(place, spread(g_b), act_all, SET)
    rows, parts_b = lax.optimization_barrier((rows, parts_b))
    rows, g_a = run_backward(p_a, rows, w_a, h_a, pre_a, held=g_a, last=True)
    g_a, parts_b = lax.optimization_barrier((g_a, parts_b))
    sum_b = summed_over_zh(parts_b)
    sum_a = summed_over_zh(run_grad(place, spread(g_a), act_all, 0))
    kept = jnp.where(low_half, sum_a, sum_b)
    other = jnp.where(low_half, sum_b, sum_a)
    received = across_y(other)
    return (kept.astype(jnp.float32) + received.astype(jnp.float32))[None]


def solution(mesh):
    fine = Mesh(mesh.devices.reshape(4, 4, 2, 4, 2), GRID_AXES)
    section = ("y", "zh")
    placed = (
        P(DP, None, None),
        P(DP, None, None),
        P(section, None, None, None),
        P(section, None, None, None),
    )
    return jax.shard_map(
        shards, mesh=fine, in_specs=placed, out_specs=P(section, DP, None), check_vma=False
    )
```
